128 devices in a mesh: seq: 16 (over x, z), shard: 8 (over y, core).
Axes of the slice: x: 4, y: 4, z: 4, core: 2. Of those that a mesh axis runs over, the one named last changes fastest.
Arguments:
- stream: bfloat16 [8, 4096, 1152], P('shard', 'seq'), may hold values from -9 to 9
- doc_starts: int32 [8, 8], P('shard'), may hold values from 0 to 4095, as said below
- cotangent: bfloat16 [8, 4096, 1152], P('shard', 'seq'), may hold values from -6 to 6
- attention_norm: bfloat16 [1152], P(('seq', 'shard')), may hold values from 0.25 to 1.75
- query_weight: bfloat16 [1152, 1024], P(('seq', 'shard')), may hold values from -0.1875 to 0.1875
- key_weight: bfloat16 [1152, 256], P(('seq', 'shard')), may hold values from -0.1875 to 0.1875
- value_weight: bfloat16 [1152, 256], P(('seq', 'shard')), may hold values from -0.1875 to 0.1875
- query_norm: bfloat16 [256], P(('seq', 'shard')), may hold values from 0.25 to 1.75
- key_norm: bfloat16 [256], P(('seq', 'shard')), may hold values from 0.25 to 1.75
- output_weight: bfloat16 [1024, 1152], P(('seq', 'shard')), may hold values from -0.1875 to 0.1875
- attention_post_norm: bfloat16 [1152], P(('seq', 'shard')), may hold values from 0.25 to 1.75
- mlp_norm: bfloat16 [1152], P(('seq', 'shard')), may hold values from 0.25 to 1.75
- gate_weight: bfloat16 [1152, 6912], P(('seq', 'shard')), may hold values from -0.1875 to 0.1875
- up_weight: bfloat16 [1152, 6912], P(('seq', 'shard')), may hold values from -0.1875 to 0.1875
- down_weight: bfloat16 [6912, 1152], P(('seq', 'shard')), may hold values from -0.078125 to 0.078125
- mlp_post_norm: bfloat16 [1152], P(('seq', 'shard')), may hold values from 0.25 to 1.75
Outputs:
- block_output: bfloat16 [8, 4096, 1152], P('shard', 'seq')
- stream_grad: bfloat16 [8, 4096, 1152], P('shard', 'seq')
- attention_norm_grad: float32 [1152], P(('seq', 'shard'))
- query_weight_grad: float32 [1152, 1024], P(('seq', 'shard'))
- key_weight_grad: float32 [1152, 256], P(('seq', 'shard'))
- value_weight_grad: float32 [1152, 256], P(('seq', 'shard'))
- query_norm_grad: float32 [256], P(('seq', 'shard'))
- key_norm_grad: float32 [256], P(('seq', 'shard'))
- output_weight_grad: float32 [1024, 1152], P(('seq', 'shard'))
- attention_post_norm_grad: float32 [1152], P(('seq', 'shard'))
- mlp_norm_grad: float32 [1152], P(('seq', 'shard'))
- gate_weight_grad: float32 [1152, 6912], P(('seq', 'shard'))
- up_weight_grad: float32 [1152, 6912], P(('seq', 'shard'))
- down_weight_grad: float32 [6912, 1152], P(('seq', 'shard'))
- mlp_post_norm_grad: float32 [1152], P(('seq', 'shard'))
- stream_rms: float32 [3], replicated
The draws below stay inside these ranges and needn't reach their ends.
Inputs may be any that keep to these rules, and one draw needn't show every extreme that they name: `doc_starts`: each row is non-decreasing and begins with 0. In every draw one sequence, drawn from the seed, has all entries 0: it is one document.
All inputs are finite; a program needn't handle non-finite values.
Results may differ from the reference program's by a relative error of at most 0.025.
Values may be sent and summed in bfloat16 or wider, within the bound.
A program may use at most 192 MiB of HBM per device.

```python
import math
import jax
import jax.numpy as jnp
from jax import lax

D = 1152
HEADS = 4
HEAD_DIM = 256
FF = 6912
WINDOW = 512
DOCS = 8
LENGTH = 4096
SEQS = 8


def draw_stream(key, part):
    key = jax.random.fold_in(key, 11)
    place = jnp.arange(LENGTH, dtype=jnp.float32) / LENGTH
    rising = (0.5 + place)[None, :, None]
    base = jnp.clip(jax.random.normal(key, (SEQS, LENGTH, D), jnp.float32), -6.0, 6.0)
    return (base * rising).astype(jnp.bfloat16)


def draw_doc_starts(key, part):
    key = jax.random.fold_in(key, 23)
    first_key, second_key = jax.random.split(key)
    inner = jnp.sort(jax.random.randint(first_key, (SEQS, DOCS - 1), 1, LENGTH, dtype=jnp.int32), axis=1)
    starts = jnp.concatenate([jnp.zeros((SEQS, 1), jnp.int32), inner], axis=1)
    chosen = jax.random.randint(second_key, (), 0, SEQS, dtype=jnp.int32)
    rows = jnp.arange(SEQS, dtype=jnp.int32)
    columns = jnp.arange(DOCS, dtype=jnp.int32)
    last_row = (rows == (chosen + 1) % SEQS)[:, None] & (columns == DOCS - 1)[None, :]
    starts = jnp.where(last_row, jnp.full_like(starts, LENGTH - 1), starts)
    picked = (rows == chosen)[:, None]
    return jnp.where(picked, jnp.zeros_like(starts), starts)


def block_levels(own_key, dims, shards, least, high):
    factor_of, own = 1.0, jax.random.fold_in(own_key, 6)
    for axis_at, parts in shards:
        heights = jnp.exp(jax.random.uniform(jax.random.fold_in(own, axis_at), (parts,), jnp.float32, least / len(shards), high / len(shards)))
        factor_of = factor_of * jnp.repeat(heights, dims[axis_at] // parts).reshape([-1 if axis == axis_at else 1 for axis in range(len(dims))])
    return factor_of


def gaussian(key, dims, spread, reach, pieces=(), held_as=jnp.bfloat16):
    values = jax.random.normal(key, dims, jnp.float32) * spread
    if len(pieces) > 0:
        values = block_levels(key, dims, pieces, -0.22, 0.18) * values
    return jnp.clip(values, min=-reach, max=reach).astype(held_as)


def setup_inputs(seed: int = 0) -> dict:
    key_of = jax.random.split(jax.random.key(seed), 17)
    return {
        "stream": draw_stream(jax.random.fold_in(key_of[16], 71), 0),
        "doc_starts": draw_doc_starts(jax.random.fold_in(key_of[16], 71), 0),
        "cotangent": gaussian(key_of[2], (SEQS, LENGTH, D), 1.0, 6.0, ((0, 8), (1, 16))),
        "attention_norm": jnp.clip(1.0 + 0.15 * jax.random.normal(key_of[3], (D,), jnp.float32), 0.25, 1.75).astype(jnp.bfloat16),
        "query_weight": gaussian(key_of[4], (D, HEADS * HEAD_DIM), D ** -0.5, 0.1875, ((0, 128),)),
        "key_weight": gaussian(key_of[5], (D, HEAD_DIM), D ** -0.5, 0.1875, ((0, 128),)),
        "value_weight": gaussian(key_of[6], (D, HEAD_DIM), D ** -0.5, 0.1875, ((0, 128),)),
        "query_norm": jnp.clip(1.0 + 0.15 * jax.random.normal(key_of[7], (HEAD_DIM,), jnp.float32), 0.25, 1.75).astype(jnp.bfloat16),
        "key_norm": jnp.clip(1.0 + 0.15 * jax.random.normal(key_of[8], (HEAD_DIM,), jnp.float32), 0.25, 1.75).astype(jnp.bfloat16),
        "output_weight": gaussian(key_of[9], (HEADS * HEAD_DIM, D), (HEADS * HEAD_DIM) ** -0.5, 0.1875, ((0, 128),)),
        "attention_post_norm": jnp.clip(1.0 + 0.15 * jax.random.normal(key_of[10], (D,), jnp.float32), 0.25, 1.75).astype(jnp.bfloat16),
        "mlp_norm": jnp.clip(1.0 + 0.15 * jax.random.normal(key_of[11], (D,), jnp.float32), 0.25, 1.75).astype(jnp.bfloat16),
        "gate_weight": gaussian(key_of[12], (D, FF), D ** -0.5, 0.1875, ((0, 128),)),
        "up_weight": gaussian(key_of[13], (D, FF), D ** -0.5, 0.1875, ((0, 128),)),
        "down_weight": gaussian(key_of[14], (FF, D), FF ** -0.5, 0.078125, ((0, 128),)),
        "mlp_post_norm": jnp.clip(1.0 + 0.15 * jax.random.normal(key_of[15], (D,), jnp.float32), 0.25, 1.75).astype(jnp.bfloat16),
    }


@jax.custom_vjp
def low(v):
    return lax.optimization_barrier(v.astype(jnp.bfloat16)).astype(jnp.float32)

@jax.custom_vjp
def low_back(v):
    return v

def low_keep(v):
    return (low(v), None)

def low_pass(kept, grad):
    return (grad,)

def back_keep(v):
    return (v, None)

def back_low(kept, grad):
    return (low(grad),)
low.defvjp(low_keep, low_pass)
low_back.defvjp(back_keep, back_low)
EPSILON = 1e-06
NEGATIVE = -1e+30
HIGHEST = lax.Precision.HIGHEST

def norm_rows(values, weight):
    return values * lax.rsqrt(lax.optimization_barrier(jnp.mean(values * values, axis=-1, keepdims=True)) + EPSILON) * weight

def rotate(values, angles):
    middle = values.shape[-1] // 2
    leading = values[..., :middle]
    trailing = values[..., middle:]
    cosine = jnp.cos(angles)
    sine_part = jnp.sin(angles)
    return jnp.concatenate([leading * cosine - trailing * sine_part, trailing * cosine + leading * sine_part], axis=-1)

def head_prep(values, weight, angles):
    return rotate(norm_rows(values, weight), angles)

def geglu(gate_part, up_part):
    return jax.nn.gelu(gate_part, approximate=True) * up_part

def frequencies(width):
    return jnp.exp(jnp.arange(width // 2, dtype=jnp.float32) * (-2.0 * math.log(10000.0) / width))

def attend(query_rot, key_rot, values_low, beginning):
    length = query_rot.shape[0]
    query_rows = min(length, 512)
    scale = HEAD_DIM ** (-0.5)
    padded_keys = jnp.concatenate([jnp.zeros((WINDOW, HEAD_DIM), jnp.float32), key_rot], axis=0)
    padded_values = jnp.concatenate([jnp.zeros((WINDOW, HEAD_DIM), jnp.float32), values_low], axis=0)

    def one_block(number):
        query_low = number * query_rows
        query_part = lax.dynamic_slice_in_dim(query_rot, query_low, query_rows, 0)
        key_part = lax.dynamic_slice_in_dim(padded_keys, query_low, query_rows + WINDOW, 0)
        value_part = lax.dynamic_slice_in_dim(padded_values, query_low, query_rows + WINDOW, 0)
        query_place = query_low + jnp.arange(query_rows, dtype=jnp.int32)
        key_place = query_low - WINDOW + jnp.arange(query_rows + WINDOW, dtype=jnp.int32)
        query_begin = lax.dynamic_slice_in_dim(beginning, query_low, query_rows, 0)
        allowed = (key_place[None, :] <= query_place[:, None]) & (key_place[None, :] > query_place[:, None] - WINDOW) & (key_place[None, :] >= query_begin[:, None])
        raw = jnp.einsum('qhd,kd->hqk', query_part, key_part, precision=HIGHEST)
        scores = jnp.where(allowed[None], low_back(raw) * scale, NEGATIVE)
        highest = lax.optimization_barrier(jnp.max(scores, axis=-1, keepdims=True))
        exponent = jnp.exp(scores - highest)
        probability = low(exponent / lax.optimization_barrier(jnp.sum(exponent, axis=-1, keepdims=True)))
        return jnp.einsum('hqk,kd->qhd', probability, value_part, precision=HIGHEST)
    outputs = lax.map(jax.checkpoint(one_block), jnp.arange(length // query_rows, dtype=jnp.int32))
    return outputs.reshape(length, HEADS * HEAD_DIM)

def sequence_forward(inputs, weights, starts):
    attention_norm, query_weight, key_weight, value_weight, query_norm, key_norm, output_weight, attention_post_norm, mlp_norm, gate_weight, up_weight, down_weight, mlp_post_norm = weights
    length = inputs.shape[0]
    positions = jnp.arange(length, dtype=jnp.int32)
    beginning = lax.optimization_barrier(jnp.max(jnp.where(starts[None, :] <= positions[:, None], starts[None, :], 0), axis=1))
    angles = (positions - beginning).astype(jnp.float32)[:, None] * frequencies(HEAD_DIM)[None, :]
    normed = low(norm_rows(inputs, attention_norm))
    query_proj = low_back(jnp.dot(normed, query_weight, precision=HIGHEST)).reshape(length, HEADS, HEAD_DIM)
    key_proj = low_back(jnp.dot(normed, key_weight, precision=HIGHEST))
    values_low = low(low_back(jnp.dot(normed, value_weight, precision=HIGHEST)))
    query_rot = low(head_prep(query_proj, query_norm, angles[:, None, :]))
    key_rot = low(head_prep(key_proj, key_norm, angles))
    mixed = low(low_back(attend(query_rot, key_rot, values_low, beginning)))
    branch = low_back(jnp.dot(mixed, output_weight, precision=HIGHEST))
    hidden = inputs + norm_rows(branch, attention_post_norm)
    feed = low(norm_rows(hidden, mlp_norm))
    gate_out = low_back(jnp.dot(feed, gate_weight, precision=HIGHEST))
    up_out = low_back(jnp.dot(feed, up_weight, precision=HIGHEST))
    active = low(geglu(gate_out, up_out))
    down_out = low_back(jnp.dot(active, down_weight, precision=HIGHEST))
    result = hidden + norm_rows(down_out, mlp_post_norm)
    return (result, hidden)

def reference(stream, doc_starts, cotangent, attention_norm, query_weight, key_weight, value_weight, query_norm, key_norm, output_weight, attention_post_norm, mlp_norm, gate_weight, up_weight, down_weight, mlp_post_norm):
    params = tuple((weight.astype(jnp.float32) for weight in (attention_norm, query_weight, key_weight, value_weight, query_norm, key_norm, output_weight, attention_post_norm, mlp_norm, gate_weight, up_weight, down_weight, mlp_post_norm)))
    zeroed = tuple((jnp.zeros(weight.shape, jnp.float32) for weight in params))

    def one_sequence(carry, item):
        grads, sums = carry
        inputs_low, cotangent_low, starts = item
        inputs = inputs_low.astype(jnp.float32)

        def forward(inputs_in, weights_in):
            return sequence_forward(inputs_in, weights_in, starts)
        result, pullback, hidden = jax.vjp(forward, inputs, params, has_aux=True)
        stream_back, weight_back = pullback(cotangent_low.astype(jnp.float32))
        grads = tuple((total + extra for total, extra in zip(grads, weight_back)))
        sums = sums + jnp.stack([jnp.sum(inputs * inputs), jnp.sum(hidden * hidden), jnp.sum(result * result)])
        return ((grads, sums), (result.astype(jnp.bfloat16), stream_back.astype(jnp.bfloat16)))
    (grads, sums), (outputs, stream_backs) = lax.scan(one_sequence, (zeroed, jnp.zeros((3,), jnp.float32)), (stream, cotangent, doc_starts))
    stream_rms = jnp.sqrt(sums / (SEQS * LENGTH * D))
    return (outputs, stream_backs, grads[0], grads[1], grads[2], grads[3], grads[4], grads[5], grads[6], grads[7], grads[8], grads[9], grads[10], grads[11], grads[12], stream_rms)
```

```python
import functools
import math

import jax
import jax.numpy as jnp
from jax import lax
from jax.experimental import pallas as pl
from jax.experimental.pallas import tpu as pltpu
from jax.sharding import PartitionSpec as P

D = 1152
HEADS = 4
HEAD_DIM = 256
WINDOW = 512
FF = 6912
PIECE = 54
SLOT = 56
WIDE = 16 * SLOT

EPSILON = 1e-06
NEGATIVE = -1e30
MESH = pl.DeviceIdType.MESH
MIB = 2**20


def place():
    q, s = lax.axis_index("seq"), lax.axis_index("shard")
    return q // 4, s // 2, q % 4, s % 2


def device(x, y, z, c):
    return {"seq": x % 4 * 4 + z % 4, "shard": y % 4 * 2 + c}


def greet(targets):
    barrier = pltpu.get_barrier_semaphore()
    for target in targets:
        pl.semaphore_signal(barrier, inc=1, device_id=target, device_id_type=MESH)
    pl.semaphore_wait(barrier, len(targets))


class Sems:
    def __init__(self, send, recv):
        self.send, self.recv, self.used = send, recv, 0

    def take(self):
        self.used += 1
        return self.send.at[self.used - 1], self.recv.at[self.used - 1]


class Push:
    def __init__(self, src, dst, sems, to, lands=None):
        send, recv = sems.take()
        self.out = pltpu.make_async_remote_copy(
            src_ref=src, dst_ref=dst, send_sem=send, recv_sem=recv, device_id=to, device_id_type=MESH
        )
        lands = dst if lands is None else lands
        self.back = pltpu.make_async_remote_copy(
            src_ref=lands, dst_ref=lands, send_sem=send, recv_sem=recv, device_id=to, device_id_type=MESH
        )

    def start(self):
        self.out.start()

    def arrived(self):
        self.back.wait_recv()

    def sent(self):
        self.out.wait_send()


class RingGather:
    def __init__(self, own, slot, half, me, peer, sems):
        up, down, far = (me + 1) % 4, (me + 3) % 4, (me + 2) % 4
        self.right = Push(own, slot(me), sems, peer(up), slot(down))
        self.left = Push(own, slot(me), sems, peer(down), slot(up))
        self.right2 = Push(half(down, 0), half(down, 0), sems, peer(up), half(far, 0))
        split = half(up, 1)
        self.left2 = None if split is None else Push(split, split, sems, peer(down), half(far, 1))

    def first(self):
        self.right.start()
        self.left.start()

    def relay(self):
        self.right.arrived()
        self.right2.start()
        self.left.arrived()
        if self.left2 is not None:
            self.left2.start()

    def last(self):
        self.right2.arrived()
        if self.left2 is not None:
            self.left2.arrived()

    def close(self):
        for push in (self.right, self.left, self.right2, self.left2):
            if push is not None:
                push.sent()


class RingSum:
    def __init__(self, chunk, half, inbox, me, peer, sems, add):
        up, down, far = (me + 1) % 4, (me + 3) % 4, (me + 2) % 4
        self.chunk, self.half, self.inbox, self.add = chunk, half, inbox, add
        self.me, self.up, self.down = me, up, down
        near_a, near_b, right, left = inbox
        self.far_a = Push(half(far, 0), near_a, sems, peer(up))
        split = half(far, 1)
        self.far_b = None if split is None else Push(split, near_b, sems, peer(down))
        self.right = Push(chunk(up), right, sems, peer(up))
        self.left = Push(chunk(down), left, sems, peer(down))

    def first(self):
        self.far_a.start()
        if self.far_b is not None:
            self.far_b.start()

    def second(self):
        self.far_a.arrived()
        self.add(self.half(self.up, 0), self.inbox[0])
        self.right.start()
        if self.far_b is not None:
            self.far_b.arrived()
            self.add(self.half(self.down, 1), self.inbox[1])
        self.left.start()

    def third(self):
        self.right.arrived()
        self.add(self.chunk(self.me), self.inbox[2])
        self.left.arrived()
        self.add(self.chunk(self.me), self.inbox[3])

    def close(self):
        for push in (self.far_a, self.far_b, self.right, self.left):
            if push is not None:
                push.sent()


def add_into(total, extra):
    if len(total.shape) == 2:
        summed = total[...].astype(jnp.float32) + extra[...].astype(jnp.float32)
        total[...] = summed.astype(total.dtype)
        return

    @pl.loop(0, total.shape[0])
    def _(step):
        add_into(total.at[step], extra.at[step])


ANY = pl.BlockSpec(memory_space=pl.ANY)
VMEM = pl.BlockSpec(memory_space=pltpu.VMEM)


def call(kernel, name, number, outs, ins, scratch, copies, in_specs=None, out_specs=None, local=0):
    outs = [jax.ShapeDtypeStruct(shape, dtype) for shape, dtype in outs]
    scratch = list(scratch) + [pltpu.SemaphoreType.DMA((copies,)), pltpu.SemaphoreType.DMA((copies,))]
    if local:
        scratch.append(pltpu.SemaphoreType.DMA((local,)))
    return pl.pallas_call(
        kernel,
        name=name,
        out_shape=outs,
        in_specs=in_specs or [ANY] * len(ins),
        out_specs=out_specs or [ANY] * len(outs),
        scratch_shapes=scratch,
        compiler_params=pltpu.CompilerParams(
            collective_id=number, has_side_effects=True, vmem_limit_bytes=56 * MIB
        ),
    )(*ins)


SHARD_STEPS = [(dy, dc) for dy in range(4) for dc in range(2) if dy or dc]


def exchange_shard(name, number, shared, spread):
    n_shared, n = len(shared), len(shared) + len(spread)

    def kernel(*refs):
        ins, outs, (send, recv, here) = refs[:n], refs[n : 2 * n], refs[2 * n :]
        x, y, z, c = place()
        mine = y * 2 + c
        sems = Sems(send, recv)
        greet([device(x, y + dy, z, (c + dc) % 2) for dy, dc in SHARD_STEPS])
        pushes = []
        for dy, dc in SHARD_STEPS:
            to_y, to_c = (y + dy) % 4, (c + dc) % 2
            from_y, from_c = (y + 4 - dy) % 4, (c + 2 - dc) % 2
            for at in range(n):
                src = ins[at] if at < n_shared else ins[at].at[to_y * 2 + to_c]
                push = Push(
                    src, outs[at].at[mine], sems, device(x, to_y, z, to_c), outs[at].at[from_y * 2 + from_c]
                )
                push.start()
                pushes.append(push)
        own = []
        for at in range(n):
            src = ins[at] if at < n_shared else ins[at].at[mine]
            own.append(pltpu.make_async_copy(src, outs[at].at[mine], here.at[at]))
            own[-1].start()
        for copy in own:
            copy.wait()
        for push in pushes:
            push.arrived()
            push.sent()

    outs = [((8,) + a.shape, a.dtype) for a in shared] + [(a.shape, a.dtype) for a in spread]
    return call(kernel, name, number, outs, list(shared) + list(spread), [], 7 * n, local=n)


def lane_halves(width):
    low = width // 256 * 128 if width % 256 == 0 else (width // 128 + 1) // 2 * 128
    return ((0, low), (low, width - low)) if width > 128 else ((0, width), None)


def gather_seq(name, number, z_first, x_first, shared):
    ins = list(z_first) + list(x_first) + list(shared)
    n = len(ins)
    copies = 8 * n + 4 * len(shared)

    def kernel(*refs):
        sources, outs, (send, recv, here) = refs[:n], refs[n : 2 * n], refs[2 * n :]
        x, y, z, c = place()
        sems = Sems(send, recv)
        greet(
            [device(x, y, z + 1, c), device(x, y, z + 3, c), device(x + 1, y, z, c), device(x + 3, y, z, c)]
            + ([device(x, y, z, 1 - c)] if shared else [])
        )

        def z_peer(k):
            return device(x, y, k, c)

        def x_peer(k):
            return device(k, y, z, c)

        jobs, own = [], []
        for at in range(n):
            source, out = sources[at], outs[at]
            rows, width = source.shape
            is_shared, by_rows = at >= len(z_first) + len(x_first), rows % 32 == 0
            part = lambda ref: ref
            if is_shared and by_rows:
                share = pl.ds(pl.multiple_of(c * (rows // 2), 16), rows // 2)
                part = lambda ref, share=share: ref.at[(slice(None),) * (len(ref.shape) - 2) + (share,)]
            elif is_shared:
                width //= 2
                share = pl.ds(pl.multiple_of(c * width, 128), width)
                part = lambda ref, share=share: ref.at[(slice(None),) * (len(ref.shape) - 1) + (share,)]
            halves = lane_halves(width)

            def lanes(ref, h, halves=halves, part=part):
                return None if halves[h] is None else part(ref).at[:, pl.ds(*halves[h])]

            mine = part(source)
            own.append(pltpu.make_async_copy(mine, part(out.at[x, z]), here.at[at]))
            own[-1].start()
            if at < len(z_first):
                one = RingGather(
                    mine,
                    lambda k, out=out, part=part: part(out.at[x, k]),
                    lambda k, h, out=out, lanes=lanes: lanes(out.at[x, k], h),
                    z, z_peer, sems,
                )
                two = RingGather(
                    part(out.at[x]),
                    lambda k, out=out, part=part: part(out.at[k]),
                    lambda k, h, out=out, part=part: part(out.at[k, pl.ds(2 * h, 2)]),
                    x, x_peer, sems,
                )
                piece = lambda k, out=out, part=part: part(out.at[k])
                me = x
            else:
                one = RingGather(
                    mine,
                    lambda k, out=out, part=part: part(out.at[k, z]),
                    lambda k, h, out=out, lanes=lanes: lanes(out.at[k, z], h),
                    x, x_peer, sems,
                )
                two = RingGather(
                    part(out.at[:, z]),
                    lambda k, out=out, part=part: part(out.at[:, k]),
                    lambda k, h, out=out, part=part: part(out.at[pl.ds(2 * h, 2), k]),
                    z, z_peer, sems,
                )
                piece = lambda k, out=out, part=part: part(out.at[:, k])
                me = z
            crossings = []
            if is_shared:
                half = rows // 2 if by_rows else width
                theirs = pl.ds(pl.multiple_of((1 - c) * half, 16 if by_rows else 128), half)
                for k in (me, (me + 3) % 4, (me + 1) % 4, (me + 2) % 4):
                    lands = out.at[:, k, theirs] if by_rows else out.at[:, k, :, theirs]
                    crossings.append(Push(piece(k), piece(k), sems, device(x, y, z, 1 - c), lands))
            jobs.append((one, two, crossings))
        for one, _, _ in jobs:
            one.first()
        for one, _, _ in jobs:
            one.relay()
        for copy in own:
            copy.wait()
        for one, two, crossings in jobs:
            one.last()
            two.first()
            if crossings:
                crossings[0].start()
        for _, two, crossings in jobs:
            two.relay()
            if crossings:
                crossings[1].start()
                crossings[2].start()
        for one, two, crossings in jobs:
            two.last()
            if crossings:
                crossings[3].start()
        for one, two, crossings in jobs:
            for push in crossings:
                push.arrived()
                push.sent()
            one.close()
            two.close()

    outs = [((4, 4) + a.shape, a.dtype) for a in ins]
    return call(kernel, name, number, outs, ins, [], copies, local=n)


def halo(name, number, steps, value):
    def kernel(src, out, send, recv):
        q, s = lax.axis_index("seq"), lax.axis_index("shard")
        sems = Sems(send, recv)
        there = [{"seq": (q + 16 + d) % 16, "shard": s} for d in steps]
        back = [{"seq": (q + 16 - d) % 16, "shard": s} for d in steps]
        greet(there + back)
        pushes = []
        for at in range(len(steps)):
            piece = src if len(src.shape) == 2 else src.at[at]
            pushes.append(Push(piece, out.at[at], sems, there[at]))
            pushes[-1].start()
        for push in pushes:
            push.arrived()
            push.sent()

    shape = (len(steps),) + value.shape[-2:]
    return call(kernel, name, number, [(shape, value.dtype)], [value], [], len(steps))[0]


def gather_tokens(name, number, value):
    rows, width = value.shape

    def kernel(src, out, send, recv, here):
        x, y, z, c = place()
        sems = Sems(send, recv)
        other = device(x, y, z, 1 - c)
        greet([device(x, y + 1, z, c), device(x, y + 3, z, c), other])
        slot = lambda k: out.at[k * 2 + c]
        ring = RingGather(
            src, slot, lambda k, h: out.at[k * 2 + c, pl.ds(h * (rows // 2), rows // 2)],
            y, lambda k: device(x, k, z, c), sems,
        )
        there = lambda k: out.at[k * 2 + 1 - c]
        cross = [
            Push(src if i == 0 else slot((y + i) % 4), slot((y + i) % 4), sems, other, there((y + i) % 4))
            for i in range(4)
        ]
        ring.first()
        cross[0].start()
        own = pltpu.make_async_copy(src, slot(y), here.at[0])
        own.start()
        ring.relay()
        cross[3].start()
        cross[1].start()
        ring.last()
        cross[2].start()
        own.wait()
        for push in cross:
            push.arrived()
            push.sent()
        ring.close()

    return call(kernel, name, number, [((8, rows, width), value.dtype)], [value], [], 8, local=1)[0]


def sum_tokens(name, number, value):
    _, rows, width = value.shape
    half = rows // 2

    def kernel(src, out, chunks, inbox, near_a, near_b, right, left, send, recv, here):
        x, y, z, c = place()
        sems = Sems(send, recv)
        other = device(x, y, z, 1 - c)
        greet([device(x, y + 1, z, c), device(x, y + 3, z, c), other])
        order = [(y + 2) % 4, (y + 1) % 4, (y + 3) % 4, y]
        cross = [Push(src.at[k * 2 + 1 - c], inbox.at[i], sems, other) for i, k in enumerate(order)]
        for push in cross:
            push.start()
        loads = [pltpu.make_async_copy(src.at[k * 2 + c], chunks.at[i], here.at[i]) for i, k in enumerate(order)]
        for load in loads:
            load.start()
        at = {2: 0, 1: 1, 3: 2, 0: 3}
        to = lambda d: device(x, y + d, z, c)
        far_a = Push(chunks.at[0, pl.ds(0, half)], near_a, sems, to(1))
        far_b = Push(chunks.at[0, pl.ds(half, half)], near_b, sems, to(3))
        go_right = Push(chunks.at[1], right, sems, to(1))
        go_left = Push(chunks.at[2], left, sems, to(3))
        for i in range(4):
            loads[i].wait()
            cross[i].arrived()
            if i < 3:
                add_into(chunks.at[i], inbox.at[i])
            if i == 0:
                far_a.start()
                far_b.start()
        far_a.arrived()
        add_into(chunks.at[1, pl.ds(0, half)], near_a)
        go_right.start()
        far_b.arrived()
        add_into(chunks.at[2, pl.ds(half, half)], near_b)
        go_left.start()
        out[...] = chunks[3].astype(jnp.float32) + inbox[3].astype(jnp.float32)
        go_right.arrived()
        out[...] += right[...].astype(jnp.float32)
        go_left.arrived()
        out[...] += left[...].astype(jnp.float32)
        for push in cross + [far_a, far_b, go_right, go_left]:
            push.sent()

    kind = value.dtype
    scratch = [
        pltpu.VMEM((4, rows, width), kind),
        pltpu.VMEM((4, rows, width), kind),
        pltpu.VMEM((half, width), kind),
        pltpu.VMEM((half, width), kind),
        pltpu.VMEM((rows, width), kind),
        pltpu.VMEM((rows, width), kind),
    ]
    return call(
        kernel, name, number, [((rows, width), jnp.float32)], [value], scratch, 8, out_specs=[VMEM], local=4
    )[0]


def sum_seq(name, number, z_first, x_first, shared):
    ins = list(z_first) + list(x_first) + [a for a, _, _ in shared]
    n, plain = len(ins), len(z_first) + len(x_first)
    shapes = [a.shape for a in z_first + x_first] + [a.shape[:3] + (size,) for a, _, size in shared]
    kinds = [a.dtype for a in ins]
    copies = 8 * n + len(shared)

    def boxes(shape, kind, first_axis):
        rows, width = shape[2:]
        lanes = lane_halves(width)
        out = [pltpu.VMEM((2, rows, width), kind)] * 2 + [pltpu.VMEM((4, rows, width), kind)] * 2
        out += [pltpu.VMEM((rows, lanes[0][1]), kind)]
        out += [pltpu.VMEM((rows, (lanes[1] or lanes[0])[1]), kind)]
        out += [pltpu.VMEM((rows, width), kind)] * 2
        return out

    scratch = []
    for at in range(n):
        scratch.append(pltpu.VMEM(shapes[at], kinds[at]))
        scratch += boxes(shapes[at], kinds[at], 0)
    for at in range(plain, n):
        scratch.append(pltpu.VMEM(shapes[at], kinds[at]))

    def kernel(*refs):
        sources, outs = refs[:n], refs[n : 2 * n]
        room = refs[2 * n : 2 * n + 9 * n]
        extra = refs[11 * n : 11 * n + len(shared)]
        send, recv, here = refs[11 * n + len(shared) :]
        x, y, z, c = place()
        sems = Sems(send, recv)
        greet(
            [device(x, y, z + 1, c), device(x, y, z + 3, c), device(x + 1, y, z, c), device(x + 3, y, z, c)]
            + ([device(x, y, z, 1 - c)] if shared else [])
        )
        z_peer = lambda k: device(x, y, k, c)
        x_peer = lambda k: device(k, y, z, c)
        loads, cross, jobs = [], [], []
        for at in range(n):
            total = room[9 * at]
            source = sources[at]
            if at >= plain:
                _, step, size = shared[at - plain]
                theirs = source.at[:, :, :, pl.ds(pl.multiple_of((1 - c) * step, 128), size)]
                cross.append(Push(theirs, extra[at - plain], sems, device(x, y, z, 1 - c)))
                cross[-1].start()
                source = source.at[:, :, :, pl.ds(pl.multiple_of(c * step, 128), size)]
            loads.append(pltpu.make_async_copy(source, total, here.at[at]))
            loads[-1].start()
            halves = lane_halves(shapes[at][3])

            def lanes(ref, h, halves=halves):
                return None if halves[h] is None else ref.at[:, pl.ds(*halves[h])]

            inbox1, inbox2 = room[9 * at + 1 : 9 * at + 5], room[9 * at + 5 : 9 * at + 9]
            if at < len(z_first):
                one = RingSum(
                    lambda k, t=total: t.at[:, k],
                    lambda k, h, t=total: t.at[pl.ds(2 * h, 2), k],
                    inbox1, z, z_peer, sems, add_into,
                )
                two = RingSum(
                    lambda k, t=total: t.at[k, z],
                    lambda k, h, t=total, lanes=lanes: lanes(t.at[k, z], h),
                    inbox2, x, x_peer, sems, add_into,
                )
            else:
                one = RingSum(
                    lambda k, t=total: t.at[k],
                    lambda k, h, t=total: t.at[k, pl.ds(2 * h, 2)],
                    inbox1, x, x_peer, sems, add_into,
                )
                two = RingSum(
                    lambda k, t=total: t.at[x, k],
                    lambda k, h, t=total, lanes=lanes: lanes(t.at[x, k], h),
                    inbox2, z, z_peer, sems, add_into,
                )
            jobs.append((one, two))
        for at in range(n):
            loads[at].wait()
            if at >= plain:
                cross[at - plain].arrived()
                add_into(room[9 * at], extra[at - plain])
            jobs[at][0].first()
        for one, _ in jobs:
            one.second()
        for one, two in jobs:
            one.third()
            two.first()
        for _, two in jobs:
            two.second()
        for at, (one, two) in enumerate(jobs):
            two.third()
            outs[at][...] = room[9 * at][x, z].astype(outs[at].dtype)
        for one, two in jobs:
            one.close()
            two.close()
        for push in cross:
            push.sent()

    outs = [(shape[2:], kind) for shape, kind in zip(shapes, kinds)]
    return call(kernel, name, number, outs, ins, scratch, copies, out_specs=[VMEM] * n, local=n)


def norm_rows(values, weight):
    return values * lax.rsqrt(jnp.mean(values * values, axis=-1, keepdims=True) + EPSILON) * weight


def rotate(values, angles):
    middle = values.shape[-1] // 2
    leading = values[..., :middle]
    trailing = values[..., middle:]
    cosine = jnp.cos(angles)
    sine_part = jnp.sin(angles)
    return jnp.concatenate(
        [leading * cosine - trailing * sine_part, trailing * cosine + leading * sine_part], axis=-1
    )


def head_prep(values, weight, angles):
    return rotate(norm_rows(values, weight), angles)


def geglu(gate_part, up_part):
    return jax.nn.gelu(gate_part, approximate=True) * up_part


def frequencies(width):
    return jnp.exp(jnp.arange(width // 2, dtype=jnp.float32) * (-2.0 * math.log(10000.0) / width))


def matmul(a, b):
    return jnp.dot(a, b, preferred_element_type=jnp.float32)


def matmul_tn(a, b):
    return lax.dot_general(a, b, (((0,), (0,)), ((), ())), preferred_element_type=jnp.float32)


def matmul_nt(a, b):
    return lax.dot_general(a, b, (((1,), (1,)), ((), ())), preferred_element_type=jnp.float32)


def heads_first(values):
    return jnp.concatenate([values[:, h * HEAD_DIM : (h + 1) * HEAD_DIM] for h in range(HEADS)], axis=0)


def heads_last(values):
    rows = values.shape[0] // HEADS
    return jnp.concatenate([values[h * rows : (h + 1) * rows] for h in range(HEADS)], axis=1)


def pad_rows(values, rows):
    return jnp.pad(values, ((0, rows - values.shape[0]), (0, 128 - values.shape[1])))


def split_hidden(weight):
    parts = weight.reshape(9, 16, 8, PIECE).transpose(2, 0, 1, 3)
    return jnp.pad(parts, ((0, 0), (0, 0), (0, 0), (0, SLOT - PIECE))).reshape(8, 9, WIDE)


def local(
    stream, doc_starts, cotangent, attention_norm, query_weight, key_weight, value_weight, query_norm, key_norm,
    output_weight, attention_post_norm, mlp_norm, gate_weight, up_weight, down_weight, mlp_post_norm,
):
    tokens = stream.shape[1]
    scale = HEAD_DIM ** (-0.5)
    inputs = stream[0].astype(jnp.float32)
    upstream = cotangent[0].astype(jnp.float32)
    offset = lax.axis_index("seq") * tokens
    positions = offset + jnp.arange(tokens, dtype=jnp.int32)
    starts_row = doc_starts[0]
    beginning = jnp.max(
        jnp.where(starts_row[None, :] <= positions[:, None], starts_row[None, :], 0), axis=1
    )
    angles = (positions - beginning).astype(jnp.float32)[:, None] * frequencies(HEAD_DIM)[None, :]
    angles_q = jnp.concatenate([angles] * HEADS, axis=0)

    own_qkv = jnp.concatenate([query_weight, key_weight, value_weight], axis=1)
    own_gains = jnp.stack(
        [jnp.pad(g, (0, 9 - g.shape[0])) for g in (attention_norm, attention_post_norm, mlp_norm, mlp_post_norm, query_norm, key_norm)]
    )
    own_both = jnp.concatenate([split_hidden(gate_weight), split_hidden(up_weight)], axis=2)
    qkv8, out8, gains8, both8 = exchange_shard(
        "exchange_weights", 0, [own_qkv, output_weight, pad_rows(own_gains, 16)], [own_both]
    )
    gains_row = gains8[:, :6, :9].transpose(1, 0, 2).reshape(6, 72)
    both16, gains16, down16, qkv16, out16 = gather_seq(
        "gather_weights", 1, [both8.reshape(72, 2 * WIDE), pad_rows(gains_row, 16)], [down_weight],
        [qkv8.reshape(72, 1536), out8.reshape(64, D)],
    )
    full_both = both16.reshape(D, 2 * WIDE)
    full_gate, full_up = full_both[:, :WIDE], full_both[:, WIDE:]
    full_down = jnp.pad(down16.reshape(16, PIECE, D), ((0, 0), (0, SLOT - PIECE), (0, 0))).reshape(WIDE, D)
    full_qkv = qkv16.reshape(D, 1536)
    full_output = out16.reshape(HEADS * HEAD_DIM, D)
    gains = gains16.reshape(16, 16, 128).astype(jnp.float32)
    gain_input, gain_post, gain_mlp, gain_mlp_post = (gains[:, i, :72].reshape(D) for i in range(4))
    gain_query, gain_key = (gains[:, i, :72].reshape(16, 8, 9)[:, :, :2].reshape(HEAD_DIM) for i in (4, 5))

    normed = norm_rows(inputs, gain_input).astype(jnp.bfloat16)
    projected = matmul(normed, full_qkv)
    query_proj = heads_first(projected[:, :1024])
    key_proj = projected[:, 1024:1280]
    values_low = projected[:, 1280:].astype(jnp.bfloat16)
    query_rot = head_prep(query_proj, gain_query, angles_q).astype(jnp.bfloat16)
    key_rot = head_prep(key_proj, gain_key, angles).astype(jnp.bfloat16)
    own_kv = jnp.concatenate([key_rot, values_low], axis=1)
    far_kv = halo("halo", 2, (2, 1), own_kv)
    kv = jnp.concatenate([far_kv.reshape(2 * tokens, 2 * HEAD_DIM), own_kv], axis=0)
    keys_all, values_all = kv[:, :HEAD_DIM], kv[:, HEAD_DIM:]
    key_place = offset - WINDOW + jnp.arange(tokens + WINDOW, dtype=jnp.int32)
    allowed = (
        (key_place[None, :] <= positions[:, None])
        & (key_place[None, :] > positions[:, None] - WINDOW)
        & (key_place[None, :] >= beginning[:, None])
    )
    allowed = jnp.concatenate([allowed] * HEADS, axis=0)
    scores = jnp.where(allowed, matmul_nt(query_rot, keys_all) * scale, NEGATIVE)
    highest = jnp.max(scores, axis=-1, keepdims=True)
    exponent = jnp.exp(scores - highest)
    totals = jnp.sum(exponent, axis=-1, keepdims=True)
    probability = exponent / totals
    probability_low = probability.astype(jnp.bfloat16)
    mixed = heads_last(matmul(probability_low, values_all).astype(jnp.bfloat16))
    branch = matmul(mixed, full_output)
    hidden = inputs + norm_rows(branch, gain_post)
    feed = norm_rows(hidden, gain_mlp).astype(jnp.bfloat16)

    feed_all = gather_tokens("gather_feed", 3, feed).reshape(8 * tokens, D)
    gate_out = matmul(feed_all, full_gate)
    up_out = matmul(feed_all, full_up)
    active = geglu(gate_out, up_out).astype(jnp.bfloat16)
    down_part = matmul(active, full_down).astype(jnp.bfloat16)
    down_out = sum_tokens("sum_down", 4, down_part.reshape(8, tokens, D))
    result = hidden + norm_rows(down_out, gain_mlp_post)
    down_grad, gain_mlp_post_grad = jax.vjp(norm_rows, down_out, gain_mlp_post)[1](upstream)
    down_all = gather_tokens("gather_down", 5, down_grad.astype(jnp.bfloat16)).reshape(8 * tokens, D)
    active_grad = matmul_nt(down_all, full_down)
    down_term = matmul_tn(active, down_all).astype(jnp.bfloat16)
    gate_grad, up_grad = jax.vjp(geglu, gate_out, up_out)[1](active_grad)
    both_low = jnp.concatenate([gate_grad.astype(jnp.bfloat16), up_grad.astype(jnp.bfloat16)], axis=1)
    both_term = matmul_tn(feed_all, both_low).astype(jnp.bfloat16)
    feed_part = matmul_nt(both_low, full_both).astype(jnp.bfloat16)
    feed_grad = sum_tokens("sum_feed", 6, feed_part.reshape(8, tokens, D))

    hidden_extra, gain_mlp_grad = jax.vjp(norm_rows, hidden, gain_mlp)[1](feed_grad)
    hidden_grad = upstream + hidden_extra
    branch_grad, gain_post_grad = jax.vjp(norm_rows, branch, gain_post)[1](hidden_grad)
    branch_low = branch_grad.astype(jnp.bfloat16)
    output_term = matmul_tn(mixed, branch_low).astype(jnp.bfloat16)
    mixed_grad = heads_first(matmul_nt(branch_low, full_output).astype(jnp.bfloat16))
    prob_grad = matmul_nt(mixed_grad, values_all)
    inner_sum = jnp.sum(probability * prob_grad, axis=-1, keepdims=True)
    score_low = (probability * (prob_grad - inner_sum) * scale).astype(jnp.bfloat16)
    query_grad_rot = matmul(score_low, keys_all)
    key_grads = matmul_tn(score_low, query_rot)
    value_grads = matmul_tn(probability_low, mixed_grad)
    kv_grads = jnp.concatenate([key_grads, value_grads], axis=1)
    returned = halo(
        "halo_back", 7, (-2, -1), kv_grads[:WINDOW].astype(jnp.bfloat16).reshape(2, tokens, 2 * HEAD_DIM)
    )
    kv_own = kv_grads[WINDOW:] + returned[0].astype(jnp.float32) + returned[1].astype(jnp.float32)
    query_grad, gain_query_grad = jax.vjp(lambda v, w: head_prep(v, w, angles_q), query_proj, gain_query)[1](
        query_grad_rot
    )
    key_grad, gain_key_grad = jax.vjp(lambda v, w: head_prep(v, w, angles), key_proj, gain_key)[1](
        kv_own[:, :HEAD_DIM]
    )
    qkv_low = jnp.concatenate([heads_last(query_grad), key_grad, kv_own[:, HEAD_DIM:]], axis=1).astype(jnp.bfloat16)
    qkv_term = matmul_tn(normed, qkv_low).astype(jnp.bfloat16)
    normed_grad = matmul_nt(qkv_low, full_qkv)
    input_extra, gain_input_grad = jax.vjp(norm_rows, inputs, gain_input)[1](normed_grad)
    stream_grad = (hidden_grad + input_extra).astype(jnp.bfloat16)

    squares = jnp.stack([jnp.sum(inputs * inputs), jnp.sum(hidden * hidden), jnp.sum(result * result)])
    small = [g.reshape(16, 72) for g in (gain_input_grad, gain_post_grad, gain_mlp_grad, gain_mlp_post_grad)]
    small += [jnp.pad(g.reshape(16, 16), ((0, 0), (0, 56))) for g in (gain_query_grad, gain_key_grad)]
    small.append(jnp.pad(jnp.broadcast_to(squares[None], (16, 3)), ((0, 0), (0, 69))))
    small = jnp.pad(jnp.stack(small, axis=1), ((0, 0), (0, 1), (0, 56))).reshape(4, 4, 8, 128)
    down_blocks = down_term.reshape(16, SLOT, D)[:, :PIECE].reshape(4, 4, PIECE, D)
    both_sum, small_sum, down_sum, qkv_sum, output_sum = sum_seq(
        "sum_weights", 8, [both_term.reshape(4, 4, 72, 2 * WIDE), small], [down_blocks],
        [(qkv_term.reshape(4, 4, 72, 1536), 768, 768), (output_term.reshape(4, 4, 64, D), 512, 640)],
    )
    small_all, both_rows, qkv_rows, output_rows = exchange_shard(
        "exchange_grads", 9, [small_sum],
        [both_sum.reshape(8, 9, 2 * WIDE), qkv_sum.reshape(8, 9, 768), output_sum.reshape(8, 8, 640)],
    )

    def whole(rows):
        parts = rows.reshape(8, 9, 16, SLOT)[..., :PIECE]
        return parts.transpose(1, 2, 0, 3).reshape(9, FF).astype(jnp.float32)

    qkv_grad = jnp.sum(qkv_rows.reshape(4, 2, 9, 768).astype(jnp.float32), axis=0)
    qkv_grad = jnp.concatenate([qkv_grad[0], qkv_grad[1]], axis=1)
    output_grad = jnp.sum(output_rows.reshape(4, 2, 8, 640).astype(jnp.float32), axis=0)
    output_grad = jnp.concatenate([output_grad[0][:, :512], output_grad[1]], axis=1)
    small_sum = jnp.sum(small_all, axis=0)
    shard = lax.axis_index("shard")
    gain_grads = lax.dynamic_slice_in_dim(small_sum, shard * 9, 9, 1)
    head_grads = lax.dynamic_slice_in_dim(small_sum, shard * 2, 2, 1)
    stream_rms = jnp.sqrt(small_sum[6, :3] / (32768 * D))
    return (
        result.astype(jnp.bfloat16)[None],
        stream_grad[None],
        gain_grads[0],
        qkv_grad[:, :1024],
        qkv_grad[:, 1024:1280],
        qkv_grad[:, 1280:],
        head_grads[4],
        head_grads[5],
        output_grad,
        gain_grads[1],
        gain_grads[2],
        whole(both_rows[:, :, :WIDE]),
        whole(both_rows[:, :, WIDE:]),
        down_sum.astype(jnp.float32),
        gain_grads[3],
        stream_rms,
    )


def solution(mesh):
    rows = P(("seq", "shard"))
    tokens = P("shard", "seq", None)
    table = P(("seq", "shard"), None)
    return jax.shard_map(
        local,
        mesh=mesh,
        in_specs=(
            tokens, P("shard", None), tokens, rows, table, table, table, rows, rows, table, rows, rows, table, table,
            table, rows,
        ),
        out_specs=(
            tokens, tokens, rows, table, table, table, rows, rows, table, rows, rows, table, table, table, rows, P(),
        ),
        check_vma=False,
    )
```

```python
import functools
import math

import jax
import jax.numpy as jnp
from jax import lax
from jax.experimental import pallas as pl
from jax.experimental.pallas import tpu as pltpu
from jax.sharding import PartitionSpec as P

D = 1152
HEADS = 4
HEAD_DIM = 256
WINDOW = 512
FF = 6912
PIECE = 54
SLOT = 56
WIDE = 16 * SLOT

EPSILON = 1e-06
NEGATIVE = -1e30
MESH = pl.DeviceIdType.MESH
MIB = 2**20


def place():
    q, s = lax.axis_index("seq"), lax.axis_index("shard")
    return q // 4, s // 2, q % 4, s % 2


def device(x, y, z, c):
    return {"seq": x % 4 * 4 + z % 4, "shard": y % 4 * 2 + c}


def greet(targets):
    barrier = pltpu.get_barrier_semaphore()
    for target in targets:
        pl.semaphore_signal(barrier, inc=1, device_id=target, device_id_type=MESH)
    pl.semaphore_wait(barrier, len(targets))


class Sems:
    def __init__(self, send, recv):
        self.send, self.recv, self.used = send, recv, 0

    def take(self):
        self.used += 1
        return self.send.at[self.used - 1], self.recv.at[self.used - 1]


class Push:
    def __init__(self, src, dst, sems, to, lands=None):
        send, recv = sems.take()
        self.out = pltpu.make_async_remote_copy(
            src_ref=src, dst_ref=dst, send_sem=send, recv_sem=recv, device_id=to, device_id_type=MESH
        )
        lands = dst if lands is None else lands
        self.back = pltpu.make_async_remote_copy(
            src_ref=lands, dst_ref=lands, send_sem=send, recv_sem=recv, device_id=to, device_id_type=MESH
        )

    def start(self):
        self.out.start()

    def arrived(self):
        self.back.wait_recv()

    def sent(self):
        self.out.wait_send()


class RingGather:
    def __init__(self, own, slot, half, me, peer, sems):
        up, down, far = (me + 1) % 4, (me + 3) % 4, (me + 2) % 4
        self.right = Push(own, slot(me), sems, peer(up), slot(down))
        self.left = Push(own, slot(me), sems, peer(down), slot(up))
        self.right2 = Push(half(down, 0), half(down, 0), sems, peer(up), half(far, 0))
        split = half(up, 1)
        self.left2 = None if split is None else Push(split, split, sems, peer(down), half(far, 1))

    def first(self):
        self.right.start()
        self.left.start()

    def relay(self):
        self.right.arrived()
        self.right2.start()
        self.left.arrived()
        if self.left2 is not None:
            self.left2.start()

    def last(self):
        self.right2.arrived()
        if self.left2 is not None:
            self.left2.arrived()

    def close(self):
        for push in (self.right, self.left, self.right2, self.left2):
            if push is not None:
                push.sent()


class RingSum:
    def __init__(self, chunk, half, inbox, me, peer, sems, add):
        up, down, far = (me + 1) % 4, (me + 3) % 4, (me + 2) % 4
        self.chunk, self.half, self.inbox, self.add = chunk, half, inbox, add
        self.me, self.up, self.down = me, up, down
        near_a, near_b, right, left = inbox
        self.far_a = Push(half(far, 0), near_a, sems, peer(up))
        split = half(far, 1)
        self.far_b = None if split is None else Push(split, near_b, sems, peer(down))
        self.right = Push(chunk(up), right, sems, peer(up))
        self.left = Push(chunk(down), left, sems, peer(down))

    def first(self):
        self.far_a.start()
        if self.far_b is not None:
            self.far_b.start()

    def second(self):
        self.far_a.arrived()
        self.add(self.half(self.up, 0), self.inbox[0])
        self.right.start()
        if self.far_b is not None:
            self.far_b.arrived()
            self.add(self.half(self.down, 1), self.inbox[1])
        self.left.start()

    def third(self):
        self.right.arrived()
        self.add(self.chunk(self.me), self.inbox[2])
        self.left.arrived()
        self.add(self.chunk(self.me), self.inbox[3])

    def close(self):
        for push in (self.far_a, self.far_b, self.right, self.left):
            if push is not None:
                push.sent()


def add_into(total, extra):
    if len(total.shape) == 2:
        summed = total[...].astype(jnp.float32) + extra[...].astype(jnp.float32)
        total[...] = summed.astype(total.dtype)
        return

    @pl.loop(0, total.shape[0])
    def _(step):
        add_into(total.at[step], extra.at[step])


ANY = pl.BlockSpec(memory_space=pl.ANY)
VMEM = pl.BlockSpec(memory_space=pltpu.VMEM)


def call(kernel, name, number, outs, ins, scratch, copies, in_specs=None, out_specs=None, local=0):
    outs = [jax.ShapeDtypeStruct(shape, dtype) for shape, dtype in outs]
    scratch = list(scratch) + [pltpu.SemaphoreType.DMA((copies,)), pltpu.SemaphoreType.DMA((copies,))]
    if local:
        scratch.append(pltpu.SemaphoreType.DMA((local,)))
    return pl.pallas_call(
        kernel,
        name=name,
        out_shape=outs,
        in_specs=in_specs or [ANY] * len(ins),
        out_specs=out_specs or [ANY] * len(outs),
        scratch_shapes=scratch,
        compiler_params=pltpu.CompilerParams(
            collective_id=number, has_side_effects=True, vmem_limit_bytes=56 * MIB
        ),
    )(*ins)


SHARD_STEPS = [(dy, dc) for dy in range(4) for dc in range(2) if dy or dc]


def exchange_shard(name, number, shared, spread):
    n_shared, n = len(shared), len(shared) + len(spread)

    def kernel(*refs):
        ins, outs, (send, recv, here) = refs[:n], refs[n : 2 * n], refs[2 * n :]
        x, y, z, c = place()
        mine = y * 2 + c
        sems = Sems(send, recv)
        greet([device(x, y + dy, z, (c + dc) % 2) for dy, dc in SHARD_STEPS])
        pushes = []
        for dy, dc in SHARD_STEPS:
            to_y, to_c = (y + dy) % 4, (c + dc) % 2
            from_y, from_c = (y + 4 - dy) % 4, (c + 2 - dc) % 2
            for at in range(n):
                src = ins[at] if at < n_shared else ins[at].at[to_y * 2 + to_c]
                push = Push(
                    src, outs[at].at[mine], sems, device(x, to_y, z, to_c), outs[at].at[from_y * 2 + from_c]
                )
                push.start()
                pushes.append(push)
        own = []
        for at in range(n):
            src = ins[at] if at < n_shared else ins[at].at[mine]
            own.append(pltpu.make_async_copy(src, outs[at].at[mine], here.at[at]))
            own[-1].start()
        for copy in own:
            copy.wait()
        for push in pushes:
            push.arrived()
            push.sent()

    outs = [((8,) + a.shape, a.dtype) for a in shared] + [(a.shape, a.dtype) for a in spread]
    return call(kernel, name, number, outs, list(shared) + list(spread), [], 7 * n, local=n)


def lane_halves(width):
    low = width // 256 * 128 if width % 256 == 0 else (width // 128 + 1) // 2 * 128
    return ((0, low), (low, width - low)) if width > 128 else ((0, width), None)


def gather_seq(name, number, z_first, x_first, shared):
    ins = list(z_first) + list(x_first) + list(shared)
    n = len(ins)
    copies = 8 * n + 4 * len(shared)

    def kernel(*refs):
        sources, outs, (send, recv, here) = refs[:n], refs[n : 2 * n], refs[2 * n :]
        x, y, z, c = place()
        sems = Sems(send, recv)
        greet(
            [device(x, y, z + 1, c), device(x, y, z + 3, c), device(x + 1, y, z, c), device(x + 3, y, z, c)]
            + ([device(x, y, z, 1 - c)] if shared else [])
        )

        def z_peer(k):
            return device(x, y, k, c)

        def x_peer(k):
            return device(k, y, z, c)

        jobs, own = [], []
        for at in range(n):
            source, out = sources[at], outs[at]
            rows, width = source.shape
            is_shared, by_rows = at >= len(z_first) + len(x_first), rows % 32 == 0
            part = lambda ref: ref
            if is_shared and by_rows:
                share = pl.ds(pl.multiple_of(c * (rows // 2), 16), rows // 2)
                part = lambda ref, share=share: ref.at[(slice(None),) * (len(ref.shape) - 2) + (share,)]
            elif is_shared:
                width //= 2
                share = pl.ds(pl.multiple_of(c * width, 128), width)
                part = lambda ref, share=share: ref.at[(slice(None),) * (len(ref.shape) - 1) + (share,)]
            halves = lane_halves(width)

            def lanes(ref, h, halves=halves, part=part):
                return None if halves[h] is None else part(ref).at[:, pl.ds(*halves[h])]

            mine = part(source)
            own.append(pltpu.make_async_copy(mine, part(out.at[x, z]), here.at[at]))
            own[-1].start()
            if at < len(z_first):
                one = RingGather(
                    mine,
                    lambda k, out=out, part=part: part(out.at[x, k]),
                    lambda k, h, out=out, lanes=lanes: lanes(out.at[x, k], h),
                    z, z_peer, sems,
                )
                two = RingGather(
                    part(out.at[x]),
                    lambda k, out=out, part=part: part(out.at[k]),
                    lambda k, h, out=out, part=part: part(out.at[k, pl.ds(2 * h, 2)]),
                    x, x_peer, sems,
                )
                piece = lambda k, out=out, part=part: part(out.at[k])
                me = x
            else:
                one = RingGather(
                    mine,
                    lambda k, out=out, part=part: part(out.at[k, z]),
                    lambda k, h, out=out, lanes=lanes: lanes(out.at[k, z], h),
                    x, x_peer, sems,
                )
                two = RingGather(
                    part(out.at[:, z]),
                    lambda k, out=out, part=part: part(out.at[:, k]),
                    lambda k, h, out=out, part=part: part(out.at[pl.ds(2 * h, 2), k]),
                    z, z_peer, sems,
                )
                piece = lambda k, out=out, part=part: part(out.at[:, k])
                me = z
            crossings = []
            if is_shared:
                half = rows // 2 if by_rows else width
                theirs = pl.ds(pl.multiple_of((1 - c) * half, 16 if by_rows else 128), half)
                for k in (me, (me + 3) % 4, (me + 1) % 4, (me + 2) % 4):
                    lands = out.at[:, k, theirs] if by_rows else out.at[:, k, :, theirs]
                    crossings.append(Push(piece(k), piece(k), sems, device(x, y, z, 1 - c), lands))
            jobs.append((one, two, crossings))
        for one, _, _ in jobs:
            one.first()
        for one, _, _ in jobs:
            one.relay()
        for copy in own:
            copy.wait()
        for one, two, crossings in jobs:
            one.last()
            two.first()
            if crossings:
                crossings[0].start()
        for _, two, crossings in jobs:
            two.relay()
            if crossings:
                crossings[1].start()
                crossings[2].start()
        for one, two, crossings in jobs:
            two.last()
            if crossings:
                crossings[3].start()
        for one, two, crossings in jobs:
            for push in crossings:
                push.arrived()
                push.sent()
            one.close()
            two.close()

    outs = [((4, 4) + a.shape, a.dtype) for a in ins]
    return call(kernel, name, number, outs, ins, [], copies, local=n)


def halo(name, number, steps, value):
    def kernel(src, out, send, recv):
        q, s = lax.axis_index("seq"), lax.axis_index("shard")
        sems = Sems(send, recv)
        there = [{"seq": (q + 16 + d) % 16, "shard": s} for d in steps]
        back = [{"seq": (q + 16 - d) % 16, "shard": s} for d in steps]
        greet(there + back)
        pushes = []
        for at in range(len(steps)):
            piece = src if len(src.shape) == 2 else src.at[at]
            pushes.append(Push(piece, out.at[at], sems, there[at]))
            pushes[-1].start()
        for push in pushes:
            push.arrived()
            push.sent()

    shape = (len(steps),) + value.shape[-2:]
    return call(kernel, name, number, [(shape, value.dtype)], [value], [], len(steps))[0]


def gather_tokens(name, number, value):
    rows, width = value.shape

    def kernel(src, out, send, recv, here):
        x, y, z, c = place()
        sems = Sems(send, recv)
        other = device(x, y, z, 1 - c)
        greet([device(x, y + 1, z, c), device(x, y + 3, z, c), other])
        slot = lambda k: out.at[k * 2 + c]
        ring = RingGather(
            src, slot, lambda k, h: out.at[k * 2 + c, pl.ds(h * (rows // 2), rows // 2)],
            y, lambda k: device(x, k, z, c), sems,
        )
        there = lambda k: out.at[k * 2 + 1 - c]
        cross = [
            Push(src if i == 0 else slot((y + i) % 4), slot((y + i) % 4), sems, other, there((y + i) % 4))
            for i in range(4)
        ]
        ring.first()
        cross[0].start()
        own = pltpu.make_async_copy(src, slot(y), here.at[0])
        own.start()
        ring.relay()
        cross[3].start()
        cross[1].start()
        ring.last()
        cross[2].start()
        own.wait()
        for push in cross:
            push.arrived()
            push.sent()
        ring.close()

    return call(kernel, name, number, [((8, rows, width), value.dtype)], [value], [], 8, local=1)[0]


def sum_tokens(name, number, value):
    _, rows, width = value.shape
    half = rows // 2

    def kernel(src, out, chunks, inbox, near_a, near_b, right, left, send, recv, here):
        x, y, z, c = place()
        sems = Sems(send, recv)
        other = device(x, y, z, 1 - c)
        greet([device(x, y + 1, z, c), device(x, y + 3, z, c), other])
        order = [(y + 2) % 4, (y + 1) % 4, (y + 3) % 4, y]
        cross = [Push(src.at[k * 2 + 1 - c], inbox.at[i], sems, other) for i, k in enumerate(order)]
        for push in cross:
            push.start()
        loads = [pltpu.make_async_copy(src.at[k * 2 + c], chunks.at[i], here.at[i]) for i, k in enumerate(order)]
        for load in loads:
            load.start()
        at = {2: 0, 1: 1, 3: 2, 0: 3}
        to = lambda d: device(x, y + d, z, c)
        far_a = Push(chunks.at[0, pl.ds(0, half)], near_a, sems, to(1))
        far_b = Push(chunks.at[0, pl.ds(half, half)], near_b, sems, to(3))
        go_right = Push(chunks.at[1], right, sems, to(1))
        go_left = Push(chunks.at[2], left, sems, to(3))
        for i in range(4):
            loads[i].wait()
            cross[i].arrived()
            if i < 3:
                add_into(chunks.at[i], inbox.at[i])
            if i == 0:
                far_a.start()
                far_b.start()
        far_a.arrived()
        add_into(chunks.at[1, pl.ds(0, half)], near_a)
        go_right.start()
        far_b.arrived()
        add_into(chunks.at[2, pl.ds(half, half)], near_b)
        go_left.start()
        out[...] = chunks[3].astype(jnp.float32) + inbox[3].astype(jnp.float32)
        go_right.arrived()
        out[...] += right[...].astype(jnp.float32)
        go_left.arrived()
        out[...] += left[...].astype(jnp.float32)
        for push in cross + [far_a, far_b, go_right, go_left]:
            push.sent()

    kind = value.dtype
    scratch = [
        pltpu.VMEM((4, rows, width), kind),
        pltpu.VMEM((4, rows, width), kind),
        pltpu.VMEM((half, width), kind),
        pltpu.VMEM((half, width), kind),
        pltpu.VMEM((rows, width), kind),
        pltpu.VMEM((rows, width), kind),
    ]
    return call(
        kernel, name, number, [((rows, width), jnp.float32)], [value], scratch, 8, out_specs=[VMEM], local=4
    )[0]


def sum_seq(name, number, z_first, x_first, shared):
    ins = list(z_first) + list(x_first) + [a for a, _, _ in shared]
    n, plain = len(ins), len(z_first) + len(x_first)
    shapes = [a.shape for a in z_first + x_first] + [a.shape[:3] + (size,) for a, _, size in shared]
    kinds = [a.dtype for a in ins]
    copies = 8 * n + len(shared)

    def boxes(shape, kind, first_axis):
        rows, width = shape[2:]
        lanes = lane_halves(width)
        out = [pltpu.VMEM((2, rows, width), kind)] * 2 + [pltpu.VMEM((4, rows, width), kind)] * 2
        out += [pltpu.VMEM((rows, lanes[0][1]), kind)]
        out += [pltpu.VMEM((rows, (lanes[1] or lanes[0])[1]), kind)]
        out += [pltpu.VMEM((rows, width), kind)] * 2
        return out

    scratch = []
    for at in range(n):
        scratch.append(pltpu.VMEM(shapes[at], kinds[at]))
        scratch += boxes(shapes[at], kinds[at], 0)
    for at in range(plain, n):
        scratch.append(pltpu.VMEM(shapes[at], kinds[at]))

    def kernel(*refs):
        sources, outs = refs[:n], refs[n : 2 * n]
        room = refs[2 * n : 2 * n + 9 * n]
        extra = refs[11 * n : 11 * n + len(shared)]
        send, recv, here = refs[11 * n + len(shared) :]
        x, y, z, c = place()
        sems = Sems(send, recv)
        greet(
            [device(x, y, z + 1, c), device(x, y, z + 3, c), device(x + 1, y, z, c), device(x + 3, y, z, c)]
            + ([device(x, y, z, 1 - c)] if shared else [])
        )
        z_peer = lambda k: device(x, y, k, c)
        x_peer = lambda k: device(k, y, z, c)
        loads, cross, jobs = [], [], []
        for at in range(n):
            total = room[9 * at]
            source = sources[at]
            if at >= plain:
                _, step, size = shared[at - plain]
                theirs = source.at[:, :, :, pl.ds(pl.multiple_of((1 - c) * step, 128), size)]
                cross.append(Push(theirs, extra[at - plain], sems, device(x, y, z, 1 - c)))
                cross[-1].start()
                source = source.at[:, :, :, pl.ds(pl.multiple_of(c * step, 128), size)]
            loads.append(pltpu.make_async_copy(source, total, here.at[at]))
            loads[-1].start()
            halves = lane_halves(shapes[at][3])

            def lanes(ref, h, halves=halves):
                return None if halves[h] is None else ref.at[:, pl.ds(*halves[h])]

            inbox1, inbox2 = room[9 * at + 1 : 9 * at + 5], room[9 * at + 5 : 9 * at + 9]
            if at < len(z_first):
                one = RingSum(
                    lambda k, t=total: t.at[:, k],
                    lambda k, h, t=total: t.at[pl.ds(2 * h, 2), k],
                    inbox1, z, z_peer, sems, add_into,
                )
                two = RingSum(
                    lambda k, t=total: t.at[k, z],
                    lambda k, h, t=total, lanes=lanes: lanes(t.at[k, z], h),
                    inbox2, x, x_peer, sems, add_into,
                )
            else:
                one = RingSum(
                    lambda k, t=total: t.at[k],
                    lambda k, h, t=total: t.at[k, pl.ds(2 * h, 2)],
                    inbox1, x, x_peer, sems, add_into,
                )
                two = RingSum(
                    lambda k, t=total: t.at[x, k],
                    lambda k, h, t=total, lanes=lanes: lanes(t.at[x, k], h),
                    inbox2, z, z_peer, sems, add_into,
                )
            jobs.append((one, two))
        for at in range(n):
            loads[at].wait()
            if at >= plain:
                cross[at - plain].arrived()
                add_into(room[9 * at], extra[at - plain])
            jobs[at][0].first()
        for one, _ in jobs:
            one.second()
        for one, two in jobs:
            one.third()
            two.first()
        for _, two in jobs:
            two.second()
        for at, (one, two) in enumerate(jobs):
            two.third()
            outs[at][...] = room[9 * at][x, z].astype(outs[at].dtype)
        for one, two in jobs:
            one.close()
            two.close()
        for push in cross:
            push.sent()

    outs = [(shape[2:], kind) for shape, kind in zip(shapes, kinds)]
    return call(kernel, name, number, outs, ins, scratch, copies, out_specs=[VMEM] * n, local=n)


def dot(a, b, contract_a, contract_b):
    return lax.dot_general(a, b, (((contract_a,), (contract_b,)), ((), ())), preferred_element_type=jnp.float32)


SUBS = 2
BACK = (0, 1, 3, 2)


def gelu_terms(gate):
    a, b = math.sqrt(2.0 / math.pi), 0.044715
    square = gate * gate
    bend = jnp.tanh(a * gate * (1.0 + b * square))
    half = 0.5 * (1.0 + bend)
    slope = half + 0.5 * gate * (1.0 - bend * bend) * a * (1.0 + 3.0 * b * square)
    return gate * half, slope


def feed_forward(name, number, feed, full_both, full_down, hidden, cotangent, gain):
    tokens, width = feed.shape
    rows = tokens // SUBS
    half = rows // 2

    def kernel(
        feed_in, both_in, down_in, hidden_in, cotangent_in, gain_in,
        block_out, feed_out, gain_out, square_out, both_out, down_out,
        feeds, downs, both, active, part, inbox, near, right, left, w_both, w_down, send, recv, here,
    ):
        x, y, z, c = place()
        sems = Sems(send, recv)
        other = device(x, y, z, 1 - c)
        to = lambda d: device(x, y + d, z, c)
        greet([to(1), to(3), other])
        loads = [
            pltpu.make_async_copy(both_in, w_both, here.at[0]),
            pltpu.make_async_copy(down_in, w_down, here.at[1]),
        ]

        def gather(source, blocks, s):
            slot = lambda k: blocks.at[s, k * 2 + c]
            ring = RingGather(
                source, slot, lambda k, h: blocks.at[s, k * 2 + c, pl.ds(h * half, half)],
                y, lambda k: device(x, k, z, c), sems,
            )
            cross = []
            for d in range(4):
                k = (y + d) % 4
                cross.append(
                    Push(source if d == 0 else slot(k), slot(k), sems, other, blocks.at[s, k * 2 + 1 - c])
                )

            def first():
                ring.first()
                cross[0].start()

            def relay():
                ring.relay()
                cross[1].start()
                cross[3].start()

            def last():
                ring.last()
                cross[2].start()

            def close():
                ring.close()
                for push in cross:
                    push.sent()

            return first, relay, last, [push.arrived for push in cross], close

        class Total:
            def __init__(self, s):
                self.s = s
                self.cross = {}
                for d in range(4):
                    k = (y + d) % 4
                    self.cross[d] = Push(part.at[s, k * 2 + 1 - c], inbox.at[s, d], sems, other)
                self.own = lambda d: part.at[s, (y + d) % 4 * 2 + c]
                self.far_a = Push(self.own(2).at[pl.ds(0, half)], near.at[s, 0], sems, to(1))
                self.far_b = Push(self.own(2).at[pl.ds(half, half)], near.at[s, 1], sems, to(3))
                self.right = Push(self.own(1), right.at[s], sems, to(1))
                self.left = Push(self.own(3), left.at[s], sems, to(3))

            def far(self):
                self.cross[2].arrived()
                add_into(self.own(2), inbox.at[self.s, 2])
                self.far_a.start()
                self.far_b.start()

            def sides(self):
                for d in (1, 3):
                    self.cross[d].arrived()
                    add_into(self.own(d), inbox.at[self.s, d])

            def go(self):
                self.far_a.arrived()
                add_into(self.own(1).at[pl.ds(0, half)], near.at[self.s, 0])
                self.right.start()
                self.far_b.arrived()
                add_into(self.own(3).at[pl.ds(half, half)], near.at[self.s, 1])
                self.left.start()

            def final(self):
                self.cross[0].arrived()
                self.right.arrived()
                self.left.arrived()
                s = self.s
                pieces = (self.own(0), inbox.at[s, 0], right.at[s], left.at[s])
                return functools.reduce(jnp.add, [p[...].astype(jnp.float32) for p in pieces])

            def close(self):
                for push in list(self.cross.values()) + [self.far_a, self.far_b, self.right, self.left]:
                    push.sent()

        def steps(body, before, totals):
            @pl.loop(0, 4 * SUBS)
            def _(t):
                for at, hook in before.items():
                    pl.when(t == at)(hook)
                s, i = t // 4, t % 4
                d = i + i // 2 - i // 3 * 2
                body(s, pl.ds((y + d) % 4 * 2, 2))
                for at in range(4 * SUBS):
                    push = totals[at // 4].cross[BACK[at % 4]]
                    pl.when(t == at)(push.start)

        def flat(value):
            return value.reshape(2 * rows, value.shape[-1])

        def pair(value):
            return value.reshape(2, rows, value.shape[-1])

        def forward(s, chip):
            sums = dot(flat(feeds[s, chip]), w_both[...], 1, 0)
            both[s, chip] = pair(sums.astype(jnp.bfloat16))
            bent, _ = gelu_terms(sums[:, :WIDE])
            low = (bent * sums[:, WIDE:]).astype(jnp.bfloat16)
            active[s, chip] = pair(low)
            part[s, chip] = pair(dot(low, w_down[...], 1, 0).astype(jnp.bfloat16))

        def backward(s, chip):
            grad = dot(flat(downs[s, chip]), w_down[...], 1, 1)
            sums = flat(both[s, chip]).astype(jnp.float32)
            bent, slope = gelu_terms(sums[:, :WIDE])
            gate_grad = (grad * sums[:, WIDE:] * slope).astype(jnp.bfloat16)
            up_grad = (grad * bent).astype(jnp.bfloat16)
            both[s, chip, :, :WIDE] = pair(gate_grad)
            both[s, chip, :, WIDE:] = pair(up_grad)
            part[s, chip] = pair(dot(flat(both[s, chip]), w_both[...], 1, 1).astype(jnp.bfloat16))

        span = lambda s: pl.ds(s * rows, rows)
        gain_out[...] = jnp.zeros_like(gain_out)
        square_out[...] = jnp.zeros_like(square_out)

        def norm_back(total, s):
            down = total.final()
            gain_row = gain_in[...]
            upstream = cotangent_in[span(s), :].astype(jnp.float32)
            scale = lax.rsqrt(jnp.mean(down * down, axis=-1, keepdims=True) + EPSILON)
            unit = down * scale
            result = hidden_in[span(s), :] + unit * gain_row
            block_out[span(s), :] = result.astype(jnp.bfloat16)
            square_out[...] += jnp.sum(result * result, axis=0, keepdims=True)
            gain_out[...] += jnp.sum(upstream * unit, axis=0, keepdims=True)
            scaled = gain_row * upstream
            grad = scale * (scaled - unit * jnp.mean(unit * scaled, axis=-1, keepdims=True))
            downs[s, y * 2 + c] = grad.astype(jnp.bfloat16)

        a, b = 0, 1
        first_a, relay_a, last_a, met_a, close_a = gather(feed_in.at[span(a)], feeds, a)
        first_b, relay_b, last_b, met_b, close_b = gather(feed_in.at[span(b)], feeds, b)
        sum_a, sum_b = Total(a), Total(b)
        first_a()
        for load in loads:
            load.start()
        own = [pltpu.make_async_copy(feed_in.at[span(s)], feeds.at[s, y * 2 + c], here.at[2 + s]) for s in (a, b)]
        for copy in own:
            copy.start()
        for copy in own + loads:
            copy.wait()

        def at_1():
            relay_a()
            first_b()
            met_a[1]()

        def at_2():
            last_a()
            met_a[3]()

        def at_3():
            relay_b()
            met_a[2]()

        def at_4():
            sum_a.far()
            met_b[0]()

        def at_5():
            last_b()
            sum_a.sides()
            met_b[1]()

        def at_6():
            sum_a.go()
            met_b[3]()

        steps(
            forward,
            {0: met_a[0], 1: at_1, 2: at_2, 3: at_3, 4: at_4, 5: at_5, 6: at_6, 7: met_b[2]},
            (sum_a, sum_b),
        )
        sum_b.far()
        norm_back(sum_a, a)
        sum_a.close()
        close_a()
        first_a, relay_a, last_a, met_a, close_a = gather(downs.at[a, y * 2 + c], downs, a)
        first_a()
        sum_b.sides()
        sum_b.go()
        old_a, old_b, old_close_b = sum_a, sum_b, close_b
        first_b, relay_b, last_b, met_b, close_b = gather(downs.at[b, y * 2 + c], downs, b)
        sum_a, sum_b = Total(a), Total(b)

        def back_1():
            relay_a()
            met_a[1]()

        def back_2():
            last_a()
            norm_back(old_b, b)
            old_b.close()
            old_close_b()
            first_b()
            met_a[3]()

        def back_4():
            sum_a.far()
            met_b[0]()

        def back_5():
            relay_b()
            sum_a.sides()
            met_b[1]()

        def back_6():
            last_b()
            sum_a.go()
            met_b[3]()

        steps(
            backward,
            {0: met_a[0], 1: back_1, 2: back_2, 3: met_a[2], 4: back_4, 5: back_5, 6: back_6, 7: met_b[2]},
            (sum_a, sum_b),
        )
        sum_b.far()
        sum_b.sides()
        every = 8 * tokens

        @pl.loop(0, WIDE // 128)
        def _(i):
            units = pl.ds(pl.multiple_of(i * 128, 128), 128)
            lhs = active[:, :, :, units].reshape(every, 128)
            down_out[units, :] = dot(lhs, downs[...].reshape(every, width), 0, 0).astype(jnp.bfloat16)

        sum_b.go()
        feed_out[span(a), :] = sum_a.final()

        @pl.loop(0, width // 128)
        def _(i):
            lanes = pl.ds(pl.multiple_of(i * 128, 128), 128)
            lhs = feeds[:, :, :, lanes].reshape(every, 128)
            both_out[lanes, :] = dot(lhs, both[...].reshape(every, 2 * WIDE), 0, 0).astype(jnp.bfloat16)

        feed_out[span(b), :] = sum_b.final()
        sum_a.close()
        sum_b.close()
        close_a()
        close_b()

    low, wide = jnp.bfloat16, jnp.float32
    blocks = (SUBS, 8, rows)
    scratch = [
        pltpu.VMEM(blocks + (width,), low),
        pltpu.VMEM(blocks + (width,), low),
        pltpu.VMEM(blocks + (2 * WIDE,), low),
        pltpu.VMEM(blocks + (WIDE,), low),
        pltpu.VMEM(blocks + (width,), low),
        pltpu.VMEM((SUBS, 4, rows, width), low),
        pltpu.VMEM((SUBS, 2, half, width), low),
        pltpu.VMEM((SUBS, rows, width), low),
        pltpu.VMEM((SUBS, rows, width), low),
        pltpu.VMEM((width, 2 * WIDE), low),
        pltpu.VMEM((WIDE, width), low),
    ]
    outs = [
        ((tokens, width), low),
        ((tokens, width), wide),
        ((1, width), wide),
        ((1, width), wide),
        ((width, 2 * WIDE), low),
        ((WIDE, width), low),
    ]
    return call(
        kernel, name, number, outs, [feed, full_both, full_down, hidden, cotangent, gain], scratch, 32 * SUBS,
        in_specs=[ANY, ANY, ANY, VMEM, VMEM, VMEM], out_specs=[VMEM] * 6, local=2 + SUBS,
    )


def norm_rows(values, weight):
    return values * lax.rsqrt(jnp.mean(values * values, axis=-1, keepdims=True) + EPSILON) * weight


def rotate(values, angles):
    middle = values.shape[-1] // 2
    leading = values[..., :middle]
    trailing = values[..., middle:]
    cosine = jnp.cos(angles)
    sine_part = jnp.sin(angles)
    return jnp.concatenate(
        [leading * cosine - trailing * sine_part, trailing * cosine + leading * sine_part], axis=-1
    )


def head_prep(values, weight, angles):
    return rotate(norm_rows(values, weight), angles)


def frequencies(width):
    return jnp.exp(jnp.arange(width // 2, dtype=jnp.float32) * (-2.0 * math.log(10000.0) / width))


def matmul(a, b):
    return jnp.dot(a, b, preferred_element_type=jnp.float32)


def matmul_tn(a, b):
    return lax.dot_general(a, b, (((0,), (0,)), ((), ())), preferred_element_type=jnp.float32)


def matmul_nt(a, b):
    return lax.dot_general(a, b, (((1,), (1,)), ((), ())), preferred_element_type=jnp.float32)


def heads_first(values):
    return jnp.concatenate([values[:, h * HEAD_DIM : (h + 1) * HEAD_DIM] for h in range(HEADS)], axis=0)


def heads_last(values):
    rows = values.shape[0] // HEADS
    return jnp.concatenate([values[h * rows : (h + 1) * rows] for h in range(HEADS)], axis=1)


def pad_rows(values, rows):
    return jnp.pad(values, ((0, rows - values.shape[0]), (0, 128 - values.shape[1])))


def split_hidden(weight):
    parts = weight.reshape(9, 16, 8, PIECE).transpose(2, 0, 1, 3)
    return jnp.pad(parts, ((0, 0), (0, 0), (0, 0), (0, SLOT - PIECE))).reshape(8, 9, WIDE)


def local(
    stream, doc_starts, cotangent, attention_norm, query_weight, key_weight, value_weight, query_norm, key_norm,
    output_weight, attention_post_norm, mlp_norm, gate_weight, up_weight, down_weight, mlp_post_norm,
):
    tokens = stream.shape[1]
    scale = HEAD_DIM ** (-0.5)
    inputs = stream[0].astype(jnp.float32)
    upstream = cotangent[0].astype(jnp.float32)
    offset = lax.axis_index("seq") * tokens
    positions = offset + jnp.arange(tokens, dtype=jnp.int32)
    starts_row = doc_starts[0]
    beginning = jnp.max(
        jnp.where(starts_row[None, :] <= positions[:, None], starts_row[None, :], 0), axis=1
    )
    angles = (positions - beginning).astype(jnp.float32)[:, None] * frequencies(HEAD_DIM)[None, :]
    angles_q = jnp.concatenate([angles] * HEADS, axis=0)

    own_qkv = jnp.concatenate([query_weight, key_weight, value_weight], axis=1)
    own_gains = jnp.stack(
        [jnp.pad(g, (0, 9 - g.shape[0])) for g in (attention_norm, attention_post_norm, mlp_norm, mlp_post_norm, query_norm, key_norm)]
    )
    own_both = jnp.concatenate([split_hidden(gate_weight), split_hidden(up_weight)], axis=2)
    qkv8, out8, gains8, both8 = exchange_shard(
        "exchange_weights", 0, [own_qkv, output_weight, pad_rows(own_gains, 16)], [own_both]
    )
    gains_row = gains8[:, :6, :9].transpose(1, 0, 2).reshape(6, 72)
    both16, gains16, down16, qkv16, out16 = gather_seq(
        "gather_weights", 1, [both8.reshape(72, 2 * WIDE), pad_rows(gains_row, 16)], [down_weight],
        [qkv8.reshape(72, 1536), out8.reshape(64, D)],
    )
    full_both = both16.reshape(D, 2 * WIDE)
    full_down = jnp.pad(down16.reshape(16, PIECE, D), ((0, 0), (0, SLOT - PIECE), (0, 0))).reshape(WIDE, D)
    full_qkv = qkv16.reshape(D, 1536)
    full_output = out16.reshape(HEADS * HEAD_DIM, D)
    gains = gains16.reshape(16, 16, 128).astype(jnp.float32)
    gain_input, gain_post, gain_mlp, gain_mlp_post = (gains[:, i, :72].reshape(D) for i in range(4))
    gain_query, gain_key = (gains[:, i, :72].reshape(16, 8, 9)[:, :, :2].reshape(HEAD_DIM) for i in (4, 5))

    normed = norm_rows(inputs, gain_input).astype(jnp.bfloat16)
    projected = matmul(normed, full_qkv)
    query_proj = heads_first(projected[:, :1024])
    key_proj = projected[:, 1024:1280]
    values_low = projected[:, 1280:].astype(jnp.bfloat16)
    query_rot = head_prep(query_proj, gain_query, angles_q).astype(jnp.bfloat16)
    key_rot = head_prep(key_proj, gain_key, angles).astype(jnp.bfloat16)
    own_kv = jnp.concatenate([key_rot, values_low], axis=1)
    far_kv = halo("halo", 2, (2, 1), own_kv)
    kv = jnp.concatenate([far_kv.reshape(2 * tokens, 2 * HEAD_DIM), own_kv], axis=0)
    keys_all, values_all = kv[:, :HEAD_DIM], kv[:, HEAD_DIM:]
    key_place = offset - WINDOW + jnp.arange(tokens + WINDOW, dtype=jnp.int32)
    allowed = (
        (key_place[None, :] <= positions[:, None])
        & (key_place[None, :] > positions[:, None] - WINDOW)
        & (key_place[None, :] >= beginning[:, None])
    )
    allowed = jnp.concatenate([allowed] * HEADS, axis=0)
    scores = jnp.where(allowed, matmul_nt(query_rot, keys_all) * scale, NEGATIVE)
    highest = jnp.max(scores, axis=-1, keepdims=True)
    exponent = jnp.exp(scores - highest)
    totals = jnp.sum(exponent, axis=-1, keepdims=True)
    probability = exponent / totals
    probability_low = probability.astype(jnp.bfloat16)
    mixed = heads_last(matmul(probability_low, values_all).astype(jnp.bfloat16))
    branch = matmul(mixed, full_output)
    hidden = inputs + norm_rows(branch, gain_post)
    feed = norm_rows(hidden, gain_mlp).astype(jnp.bfloat16)

    block_output, feed_grad, gain_mlp_post_grad, result_squares, both_term, down_term = feed_forward(
        "feed_forward", 3, feed, full_both, full_down, hidden, cotangent[0], gain_mlp_post[None]
    )

    hidden_extra, gain_mlp_grad = jax.vjp(norm_rows, hidden, gain_mlp)[1](feed_grad)
    hidden_grad = upstream + hidden_extra
    branch_grad, gain_post_grad = jax.vjp(norm_rows, branch, gain_post)[1](hidden_grad)
    branch_low = branch_grad.astype(jnp.bfloat16)
    output_term = matmul_tn(mixed, branch_low).astype(jnp.bfloat16)
    mixed_grad = heads_first(matmul_nt(branch_low, full_output).astype(jnp.bfloat16))
    prob_grad = matmul_nt(mixed_grad, values_all)
    inner_sum = jnp.sum(probability * prob_grad, axis=-1, keepdims=True)
    score_low = (probability * (prob_grad - inner_sum) * scale).astype(jnp.bfloat16)
    query_grad_rot = matmul(score_low, keys_all)
    key_grads = matmul_tn(score_low, query_rot)
    value_grads = matmul_tn(probability_low, mixed_grad)
    kv_grads = jnp.concatenate([key_grads, value_grads], axis=1)
    returned = halo(
        "halo_back", 4, (-2, -1), kv_grads[:WINDOW].astype(jnp.bfloat16).reshape(2, tokens, 2 * HEAD_DIM)
    )
    kv_own = kv_grads[WINDOW:] + returned[0].astype(jnp.float32) + returned[1].astype(jnp.float32)
    query_grad, gain_query_grad = jax.vjp(lambda v, w: head_prep(v, w, angles_q), query_proj, gain_query)[1](
        query_grad_rot
    )
    key_grad, gain_key_grad = jax.vjp(lambda v, w: head_prep(v, w, angles), key_proj, gain_key)[1](
        kv_own[:, :HEAD_DIM]
    )
    qkv_low = jnp.concatenate([heads_last(query_grad), key_grad, kv_own[:, HEAD_DIM:]], axis=1).astype(jnp.bfloat16)
    qkv_term = matmul_tn(normed, qkv_low).astype(jnp.bfloat16)
    normed_grad = matmul_nt(qkv_low, full_qkv)
    input_extra, gain_input_grad = jax.vjp(norm_rows, inputs, gain_input)[1](normed_grad)
    stream_grad = (hidden_grad + input_extra).astype(jnp.bfloat16)

    squares = jnp.stack([jnp.sum(inputs * inputs), jnp.sum(hidden * hidden), jnp.sum(result_squares)])
    small = [g.reshape(16, 72) for g in (gain_input_grad, gain_post_grad, gain_mlp_grad, gain_mlp_post_grad)]
    small += [jnp.pad(g.reshape(16, 16), ((0, 0), (0, 56))) for g in (gain_query_grad, gain_key_grad)]
    small.append(jnp.pad(jnp.broadcast_to(squares[None], (16, 3)), ((0, 0), (0, 69))))
    small = jnp.pad(jnp.stack(small, axis=1), ((0, 0), (0, 1), (0, 56))).reshape(4, 4, 8, 128)
    down_blocks = down_term.reshape(16, SLOT, D)[:, :PIECE].reshape(4, 4, PIECE, D)
    both_sum, small_sum, down_sum, qkv_sum, output_sum = sum_seq(
        "sum_weights", 5, [both_term.reshape(4, 4, 72, 2 * WIDE), small], [down_blocks],
        [(qkv_term.reshape(4, 4, 72, 1536), 768, 768), (output_term.reshape(4, 4, 64, D), 512, 640)],
    )
    small_all, both_rows, qkv_rows, output_rows = exchange_shard(
        "exchange_grads", 6, [small_sum],
        [both_sum.reshape(8, 9, 2 * WIDE), qkv_sum.reshape(8, 9, 768), output_sum.reshape(8, 8, 640)],
    )

    def whole(rows):
        parts = rows.reshape(8, 9, 16, SLOT)[..., :PIECE]
        return parts.transpose(1, 2, 0, 3).reshape(9, FF).astype(jnp.float32)

    qkv_grad = jnp.sum(qkv_rows.reshape(4, 2, 9, 768).astype(jnp.float32), axis=0)
    qkv_grad = jnp.concatenate([qkv_grad[0], qkv_grad[1]], axis=1)
    output_grad = jnp.sum(output_rows.reshape(4, 2, 8, 640).astype(jnp.float32), axis=0)
    output_grad = jnp.concatenate([output_grad[0][:, :512], output_grad[1]], axis=1)
    small_sum = jnp.sum(small_all, axis=0)
    shard = lax.axis_index("shard")
    gain_grads = lax.dynamic_slice_in_dim(small_sum, shard * 9, 9, 1)
    head_grads = lax.dynamic_slice_in_dim(small_sum, shard * 2, 2, 1)
    stream_rms = jnp.sqrt(small_sum[6, :3] / (32768 * D))
    return (
        block_output[None],
        stream_grad[None],
        gain_grads[0],
        qkv_grad[:, :1024],
        qkv_grad[:, 1024:1280],
        qkv_grad[:, 1280:],
        head_grads[4],
        head_grads[5],
        output_grad,
        gain_grads[1],
        gain_grads[2],
        whole(both_rows[:, :, :WIDE]),
        whole(both_rows[:, :, WIDE:]),
        down_sum.astype(jnp.float32),
        gain_grads[3],
        stream_rms,
    )


def solution(mesh):
    rows = P(("seq", "shard"))
    tokens = P("shard", "seq", None)
    table = P(("seq", "shard"), None)
    return jax.shard_map(
        local,
        mesh=mesh,
        in_specs=(
            tokens, P("shard", None), tokens, rows, table, table, table, rows, rows, table, rows, rows, table, table,
            table, rows,
        ),
        out_specs=(
            tokens, tokens, rows, table, table, table, rows, rows, table, rows, rows, table, table, table, rows, P(),
        ),
        check_vma=False,
    )
```

```python
import functools
import math

import jax
import jax.numpy as jnp
from jax import lax
from jax.experimental import pallas as pl
from jax.experimental.pallas import tpu as pltpu
from jax.sharding import PartitionSpec as P

D = 1152
HEADS = 4
HEAD_DIM = 256
WINDOW = 512
FF = 6912
PIECE = 54
SLOT = 56
WIDE = 16 * SLOT

EPSILON = 1e-06
NEGATIVE = -1e30
MESH = pl.DeviceIdType.MESH
MIB = 2**20


def place():
    q, s = lax.axis_index("seq"), lax.axis_index("shard")
    return q // 4, s // 2, q % 4, s % 2


def device(x, y, z, c):
    return {"seq": x % 4 * 4 + z % 4, "shard": y % 4 * 2 + c}


def greet(targets):
    barrier = pltpu.get_barrier_semaphore()
    for target in targets:
        pl.semaphore_signal(barrier, inc=1, device_id=target, device_id_type=MESH)
    pl.semaphore_wait(barrier, len(targets))


class Sems:
    def __init__(self, send, recv):
        self.send, self.recv, self.used = send, recv, 0

    def take(self):
        self.used += 1
        return self.send.at[self.used - 1], self.recv.at[self.used - 1]


class Push:
    def __init__(self, src, dst, sems, to, lands=None):
        send, recv = sems.take()
        self.out = pltpu.make_async_remote_copy(
            src_ref=src, dst_ref=dst, send_sem=send, recv_sem=recv, device_id=to, device_id_type=MESH
        )
        lands = dst if lands is None else lands
        self.back = pltpu.make_async_remote_copy(
            src_ref=lands, dst_ref=lands, send_sem=send, recv_sem=recv, device_id=to, device_id_type=MESH
        )

    def start(self):
        self.out.start()

    def arrived(self):
        self.back.wait_recv()

    def sent(self):
        self.out.wait_send()


class RingGather:
    def __init__(self, own, slot, half, me, peer, sems):
        up, down, far = (me + 1) % 4, (me + 3) % 4, (me + 2) % 4
        self.right = Push(own, slot(me), sems, peer(up), slot(down))
        self.left = Push(own, slot(me), sems, peer(down), slot(up))
        self.right2 = Push(half(down, 0), half(down, 0), sems, peer(up), half(far, 0))
        split = half(up, 1)
        self.left2 = None if split is None else Push(split, split, sems, peer(down), half(far, 1))

    def first(self):
        self.right.start()
        self.left.start()

    def relay(self):
        self.right.arrived()
        self.right2.start()
        self.left.arrived()
        if self.left2 is not None:
            self.left2.start()

    def last(self):
        self.right2.arrived()
        if self.left2 is not None:
            self.left2.arrived()

    def close(self):
        for push in (self.right, self.left, self.right2, self.left2):
            if push is not None:
                push.sent()


class RingSum:
    def __init__(self, chunk, half, inbox, me, peer, sems, add):
        up, down, far = (me + 1) % 4, (me + 3) % 4, (me + 2) % 4
        self.chunk, self.half, self.inbox, self.add = chunk, half, inbox, add
        self.me, self.up, self.down = me, up, down
        near_a, near_b, right, left = inbox
        self.far_a = Push(half(far, 0), near_a, sems, peer(up))
        split = half(far, 1)
        self.far_b = None if split is None else Push(split, near_b, sems, peer(down))
        self.right = Push(chunk(up), right, sems, peer(up))
        self.left = Push(chunk(down), left, sems, peer(down))

    def first(self):
        self.far_a.start()
        if self.far_b is not None:
            self.far_b.start()

    def second(self):
        self.far_a.arrived()
        self.add(self.half(self.up, 0), self.inbox[0])
        self.right.start()
        if self.far_b is not None:
            self.far_b.arrived()
            self.add(self.half(self.down, 1), self.inbox[1])
        self.left.start()

    def third(self):
        self.right.arrived()
        self.add(self.chunk(self.me), self.inbox[2])
        self.left.arrived()
        self.add(self.chunk(self.me), self.inbox[3])

    def close(self):
        for push in (self.far_a, self.far_b, self.right, self.left):
            if push is not None:
                push.sent()


def add_into(total, extra):
    if len(total.shape) == 2:
        summed = total[...].astype(jnp.float32) + extra[...].astype(jnp.float32)
        total[...] = summed.astype(total.dtype)
        return

    @pl.loop(0, total.shape[0])
    def _(step):
        add_into(total.at[step], extra.at[step])


ANY = pl.BlockSpec(memory_space=pl.ANY)
VMEM = pl.BlockSpec(memory_space=pltpu.VMEM)


def call(kernel, name, number, outs, ins, scratch, copies, in_specs=None, out_specs=None, local=0, aliases=None):
    outs = [jax.ShapeDtypeStruct(shape, dtype) for shape, dtype in outs]
    scratch = list(scratch) + [pltpu.SemaphoreType.DMA((copies,)), pltpu.SemaphoreType.DMA((copies,))]
    if local:
        scratch.append(pltpu.SemaphoreType.DMA((local,)))
    return pl.pallas_call(
        kernel,
        name=name,
        out_shape=outs,
        in_specs=in_specs or [ANY] * len(ins),
        out_specs=out_specs or [ANY] * len(outs),
        scratch_shapes=scratch,
        input_output_aliases=aliases or {},
        compiler_params=pltpu.CompilerParams(
            collective_id=number, has_side_effects=True, vmem_limit_bytes=56 * MIB
        ),
    )(*ins)


SHARD_STEPS = [(dy, dc) for dy in range(4) for dc in range(2) if dy or dc]


def exchange_shard(name, number, shared, spread):
    n_shared, n = len(shared), len(shared) + len(spread)

    def kernel(*refs):
        ins, outs, (send, recv, here) = refs[:n], refs[n : 2 * n], refs[2 * n :]
        x, y, z, c = place()
        mine = y * 2 + c
        sems = Sems(send, recv)
        greet([device(x, y + dy, z, (c + dc) % 2) for dy, dc in SHARD_STEPS])
        pushes = []
        for dy, dc in SHARD_STEPS:
            to_y, to_c = (y + dy) % 4, (c + dc) % 2
            from_y, from_c = (y + 4 - dy) % 4, (c + 2 - dc) % 2
            for at in range(n):
                src = ins[at] if at < n_shared else ins[at].at[to_y * 2 + to_c]
                push = Push(
                    src, outs[at].at[mine], sems, device(x, to_y, z, to_c), outs[at].at[from_y * 2 + from_c]
                )
                push.start()
                pushes.append(push)
        own = []
        for at in range(n):
            src = ins[at] if at < n_shared else ins[at].at[mine]
            own.append(pltpu.make_async_copy(src, outs[at].at[mine], here.at[at]))
            own[-1].start()
        for copy in own:
            copy.wait()
        for push in pushes:
            push.arrived()
            push.sent()

    outs = [((8,) + a.shape, a.dtype) for a in shared] + [(a.shape, a.dtype) for a in spread]
    return call(kernel, name, number, outs, list(shared) + list(spread), [], 7 * n, local=n)


def lane_halves(width):
    low = width // 256 * 128 if width % 256 == 0 else (width // 128 + 1) // 2 * 128
    return ((0, low), (low, width - low)) if width > 128 else ((0, width), None)


def gather_seq(name, number, z_first, x_first, shared):
    ins = list(z_first) + list(x_first) + list(shared)
    n = len(ins)
    copies = 8 * n + 4 * len(shared)

    def kernel(*refs):
        sources, outs, (send, recv, here) = refs[:n], refs[n : 2 * n], refs[2 * n :]
        x, y, z, c = place()
        sems = Sems(send, recv)
        greet(
            [device(x, y, z + 1, c), device(x, y, z + 3, c), device(x + 1, y, z, c), device(x + 3, y, z, c)]
            + ([device(x, y, z, 1 - c)] if shared else [])
        )

        def z_peer(k):
            return device(x, y, k, c)

        def x_peer(k):
            return device(k, y, z, c)

        jobs, own = [], []
        for at in range(n):
            source, out = sources[at], outs[at]
            rows, width = source.shape
            is_shared, by_rows = at >= len(z_first) + len(x_first), rows % 32 == 0
            part = lambda ref: ref
            if is_shared and by_rows:
                share = pl.ds(pl.multiple_of(c * (rows // 2), 16), rows // 2)
                part = lambda ref, share=share: ref.at[(slice(None),) * (len(ref.shape) - 2) + (share,)]
            elif is_shared:
                width //= 2
                share = pl.ds(pl.multiple_of(c * width, 128), width)
                part = lambda ref, share=share: ref.at[(slice(None),) * (len(ref.shape) - 1) + (share,)]
            halves = lane_halves(width)

            def lanes(ref, h, halves=halves, part=part):
                return None if halves[h] is None else part(ref).at[:, pl.ds(*halves[h])]

            mine = part(source)
            own.append(pltpu.make_async_copy(mine, part(out.at[x, z]), here.at[at]))
            own[-1].start()
            if at < len(z_first):
                one = RingGather(
                    mine,
                    lambda k, out=out, part=part: part(out.at[x, k]),
                    lambda k, h, out=out, lanes=lanes: lanes(out.at[x, k], h),
                    z, z_peer, sems,
                )
                two = RingGather(
                    part(out.at[x]),
                    lambda k, out=out, part=part: part(out.at[k]),
                    lambda k, h, out=out, part=part: part(out.at[k, pl.ds(2 * h, 2)]),
                    x, x_peer, sems,
                )
                piece = lambda k, out=out, part=part: part(out.at[k])
                me = x
            else:
                one = RingGather(
                    mine,
                    lambda k, out=out, part=part: part(out.at[k, z]),
                    lambda k, h, out=out, lanes=lanes: lanes(out.at[k, z], h),
                    x, x_peer, sems,
                )
                two = RingGather(
                    part(out.at[:, z]),
                    lambda k, out=out, part=part: part(out.at[:, k]),
                    lambda k, h, out=out, part=part: part(out.at[pl.ds(2 * h, 2), k]),
                    z, z_peer, sems,
                )
                piece = lambda k, out=out, part=part: part(out.at[:, k])
                me = z
            crossings = []
            if is_shared:
                half = rows // 2 if by_rows else width
                theirs = pl.ds(pl.multiple_of((1 - c) * half, 16 if by_rows else 128), half)
                for k in (me, (me + 3) % 4, (me + 1) % 4, (me + 2) % 4):
                    lands = out.at[:, k, theirs] if by_rows else out.at[:, k, :, theirs]
                    crossings.append(Push(piece(k), piece(k), sems, device(x, y, z, 1 - c), lands))
            jobs.append((one, two, crossings))
        for one, _, _ in jobs:
            one.first()
        for one, _, _ in jobs:
            one.relay()
        for copy in own:
            copy.wait()
        for one, two, crossings in jobs:
            one.last()
            two.first()
            if crossings:
                crossings[0].start()
        for _, two, crossings in jobs:
            two.relay()
            if crossings:
                crossings[1].start()
                crossings[2].start()
        for one, two, crossings in jobs:
            two.last()
            if crossings:
                crossings[3].start()
        for one, two, crossings in jobs:
            for push in crossings:
                push.arrived()
                push.sent()
            one.close()
            two.close()

    outs = [((4, 4) + a.shape, a.dtype) for a in ins]
    return call(kernel, name, number, outs, ins, [], copies, local=n)


def halo(name, number, steps, value):
    def kernel(src, out, send, recv):
        q, s = lax.axis_index("seq"), lax.axis_index("shard")
        sems = Sems(send, recv)
        there = [{"seq": (q + 16 + d) % 16, "shard": s} for d in steps]
        back = [{"seq": (q + 16 - d) % 16, "shard": s} for d in steps]
        greet(there + back)
        pushes = []
        for at in range(len(steps)):
            piece = src if len(src.shape) == 2 else src.at[at]
            pushes.append(Push(piece, out.at[at], sems, there[at]))
            pushes[-1].start()
        for push in pushes:
            push.arrived()
            push.sent()

    shape = (len(steps),) + value.shape[-2:]
    return call(kernel, name, number, [(shape, value.dtype)], [value], [], len(steps))[0]


def gather_tokens(name, number, value):
    rows, width = value.shape

    def kernel(src, out, send, recv, here):
        x, y, z, c = place()
        sems = Sems(send, recv)
        other = device(x, y, z, 1 - c)
        greet([device(x, y + 1, z, c), device(x, y + 3, z, c), other])
        slot = lambda k: out.at[k * 2 + c]
        ring = RingGather(
            src, slot, lambda k, h: out.at[k * 2 + c, pl.ds(h * (rows // 2), rows // 2)],
            y, lambda k: device(x, k, z, c), sems,
        )
        there = lambda k: out.at[k * 2 + 1 - c]
        cross = [
            Push(src if i == 0 else slot((y + i) % 4), slot((y + i) % 4), sems, other, there((y + i) % 4))
            for i in range(4)
        ]
        ring.first()
        cross[0].start()
        own = pltpu.make_async_copy(src, slot(y), here.at[0])
        own.start()
        ring.relay()
        cross[3].start()
        cross[1].start()
        ring.last()
        cross[2].start()
        own.wait()
        for push in cross:
            push.arrived()
            push.sent()
        ring.close()

    return call(kernel, name, number, [((8, rows, width), value.dtype)], [value], [], 8, local=1)[0]


def sum_tokens(name, number, value):
    _, rows, width = value.shape
    half = rows // 2

    def kernel(src, out, chunks, inbox, near_a, near_b, right, left, send, recv, here):
        x, y, z, c = place()
        sems = Sems(send, recv)
        other = device(x, y, z, 1 - c)
        greet([device(x, y + 1, z, c), device(x, y + 3, z, c), other])
        order = [(y + 2) % 4, (y + 1) % 4, (y + 3) % 4, y]
        cross = [Push(src.at[k * 2 + 1 - c], inbox.at[i], sems, other) for i, k in enumerate(order)]
        for push in cross:
            push.start()
        loads = [pltpu.make_async_copy(src.at[k * 2 + c], chunks.at[i], here.at[i]) for i, k in enumerate(order)]
        for load in loads:
            load.start()
        at = {2: 0, 1: 1, 3: 2, 0: 3}
        to = lambda d: device(x, y + d, z, c)
        far_a = Push(chunks.at[0, pl.ds(0, half)], near_a, sems, to(1))
        far_b = Push(chunks.at[0, pl.ds(half, half)], near_b, sems, to(3))
        go_right = Push(chunks.at[1], right, sems, to(1))
        go_left = Push(chunks.at[2], left, sems, to(3))
        for i in range(4):
            loads[i].wait()
            cross[i].arrived()
            if i < 3:
                add_into(chunks.at[i], inbox.at[i])
            if i == 0:
                far_a.start()
                far_b.start()
        far_a.arrived()
        add_into(chunks.at[1, pl.ds(0, half)], near_a)
        go_right.start()
        far_b.arrived()
        add_into(chunks.at[2, pl.ds(half, half)], near_b)
        go_left.start()
        out[...] = chunks[3].astype(jnp.float32) + inbox[3].astype(jnp.float32)
        go_right.arrived()
        out[...] += right[...].astype(jnp.float32)
        go_left.arrived()
        out[...] += left[...].astype(jnp.float32)
        for push in cross + [far_a, far_b, go_right, go_left]:
            push.sent()

    kind = value.dtype
    scratch = [
        pltpu.VMEM((4, rows, width), kind),
        pltpu.VMEM((4, rows, width), kind),
        pltpu.VMEM((half, width), kind),
        pltpu.VMEM((half, width), kind),
        pltpu.VMEM((rows, width), kind),
        pltpu.VMEM((rows, width), kind),
    ]
    return call(
        kernel, name, number, [((rows, width), jnp.float32)], [value], scratch, 8, out_specs=[VMEM], local=4
    )[0]


def sum_seq(name, number, z_first, x_first, shared):
    ins = list(z_first) + list(x_first) + [a for a, _, _ in shared]
    n, plain = len(ins), len(z_first) + len(x_first)
    shapes = [a.shape for a in z_first + x_first] + [a.shape[:3] + (size,) for a, _, size in shared]
    kinds = [a.dtype for a in ins]
    copies = 8 * n + len(shared)

    def boxes(shape, kind, first_axis):
        rows, width = shape[2:]
        lanes = lane_halves(width)
        out = [pltpu.VMEM((2, rows, width), kind)] * 2 + [pltpu.VMEM((4, rows, width), kind)] * 2
        out += [pltpu.VMEM((rows, lanes[0][1]), kind)]
        out += [pltpu.VMEM((rows, (lanes[1] or lanes[0])[1]), kind)]
        out += [pltpu.VMEM((rows, width), kind)] * 2
        return out

    scratch = []
    for at in range(n):
        scratch.append(pltpu.VMEM(shapes[at], kinds[at]))
        scratch += boxes(shapes[at], kinds[at], 0)
    for at in range(plain, n):
        scratch.append(pltpu.VMEM(shapes[at], kinds[at]))

    def kernel(*refs):
        sources, outs = refs[:n], refs[n : 2 * n]
        room = refs[2 * n : 2 * n + 9 * n]
        extra = refs[11 * n : 11 * n + len(shared)]
        send, recv, here = refs[11 * n + len(shared) :]
        x, y, z, c = place()
        sems = Sems(send, recv)
        greet(
            [device(x, y, z + 1, c), device(x, y, z + 3, c), device(x + 1, y, z, c), device(x + 3, y, z, c)]
            + ([device(x, y, z, 1 - c)] if shared else [])
        )
        z_peer = lambda k: device(x, y, k, c)
        x_peer = lambda k: device(k, y, z, c)
        loads, cross, jobs = [], [], []
        for at in range(n):
            total = room[9 * at]
            source = sources[at]
            if at >= plain:
                _, step, size = shared[at - plain]
                theirs = source.at[:, :, :, pl.ds(pl.multiple_of((1 - c) * step, 128), size)]
                cross.append(Push(theirs, extra[at - plain], sems, device(x, y, z, 1 - c)))
                cross[-1].start()
                source = source.at[:, :, :, pl.ds(pl.multiple_of(c * step, 128), size)]
            loads.append(pltpu.make_async_copy(source, total, here.at[at]))
            loads[-1].start()
            halves = lane_halves(shapes[at][3])

            def lanes(ref, h, halves=halves):
                return None if halves[h] is None else ref.at[:, pl.ds(*halves[h])]

            inbox1, inbox2 = room[9 * at + 1 : 9 * at + 5], room[9 * at + 5 : 9 * at + 9]
            if at < len(z_first):
                one = RingSum(
                    lambda k, t=total: t.at[:, k],
                    lambda k, h, t=total: t.at[pl.ds(2 * h, 2), k],
                    inbox1, z, z_peer, sems, add_into,
                )
                two = RingSum(
                    lambda k, t=total: t.at[k, z],
                    lambda k, h, t=total, lanes=lanes: lanes(t.at[k, z], h),
                    inbox2, x, x_peer, sems, add_into,
                )
            else:
                one = RingSum(
                    lambda k, t=total: t.at[k],
                    lambda k, h, t=total: t.at[k, pl.ds(2 * h, 2)],
                    inbox1, x, x_peer, sems, add_into,
                )
                two = RingSum(
                    lambda k, t=total: t.at[x, k],
                    lambda k, h, t=total, lanes=lanes: lanes(t.at[x, k], h),
                    inbox2, z, z_peer, sems, add_into,
                )
            jobs.append((one, two))
        for at in range(n):
            loads[at].wait()
            if at >= plain:
                cross[at - plain].arrived()
                add_into(room[9 * at], extra[at - plain])
            jobs[at][0].first()
        for one, _ in jobs:
            one.second()
        for one, two in jobs:
            one.third()
            two.first()
        for _, two in jobs:
            two.second()
        for at, (one, two) in enumerate(jobs):
            two.third()
            outs[at][...] = room[9 * at][x, z].astype(outs[at].dtype)
        for one, two in jobs:
            one.close()
            two.close()
        for push in cross:
            push.sent()

    outs = [(shape[2:], kind) for shape, kind in zip(shapes, kinds)]
    return call(kernel, name, number, outs, ins, scratch, copies, out_specs=[VMEM] * n, local=n)


def dot(a, b, contract_a, contract_b):
    return lax.dot_general(a, b, (((contract_a,), (contract_b,)), ((), ())), preferred_element_type=jnp.float32)


SUBS = 2
BACK = (0, 1, 3, 2)


def gelu_terms(gate):
    a, b = math.sqrt(2.0 / math.pi), 0.044715
    square = gate * gate
    bend = jnp.tanh(a * gate * (1.0 + b * square))
    half = 0.5 * (1.0 + bend)
    slope = half + 0.5 * gate * (1.0 - bend * bend) * a * (1.0 + 3.0 * b * square)
    return gate * half, slope


def feed_forward(name, number, feed, full_both, full_down, hidden, cotangent, gain):
    tokens, width = feed.shape
    rows = tokens // SUBS
    half = rows // 2

    def kernel(
        feed_in, both_in, down_in, hidden_in, cotangent_in, gain_in,
        block_out, feed_out, gain_out, square_out, both_out, down_out,
        feeds, downs, both, active, part, inbox, near, right, left, w_both, w_down, send, recv, here,
    ):
        x, y, z, c = place()
        sems = Sems(send, recv)
        other = device(x, y, z, 1 - c)
        to = lambda d: device(x, y + d, z, c)
        greet([to(1), to(3), other])
        loads = [
            pltpu.make_async_copy(both_in, w_both, here.at[0]),
            pltpu.make_async_copy(down_in, w_down, here.at[1]),
        ]

        def gather(source, blocks, s):
            slot = lambda k: blocks.at[s, k * 2 + c]
            ring = RingGather(
                source, slot, lambda k, h: blocks.at[s, k * 2 + c, pl.ds(h * half, half)],
                y, lambda k: device(x, k, z, c), sems,
            )
            cross = []
            for d in range(4):
                k = (y + d) % 4
                cross.append(
                    Push(source if d == 0 else slot(k), slot(k), sems, other, blocks.at[s, k * 2 + 1 - c])
                )

            def first():
                ring.first()
                cross[0].start()

            def relay():
                ring.relay()
                cross[1].start()
                cross[3].start()

            def last():
                ring.last()
                cross[2].start()

            def close():
                ring.close()
                for push in cross:
                    push.sent()

            return first, relay, last, [push.arrived for push in cross], close

        class Total:
            def __init__(self, s):
                self.s = s
                self.cross = {}
                for d in range(4):
                    k = (y + d) % 4
                    self.cross[d] = Push(part.at[s, k * 2 + 1 - c], inbox.at[s, d], sems, other)
                self.own = lambda d: part.at[s, (y + d) % 4 * 2 + c]
                self.far_a = Push(self.own(2).at[pl.ds(0, half)], near.at[s, 0], sems, to(1))
                self.far_b = Push(self.own(2).at[pl.ds(half, half)], near.at[s, 1], sems, to(3))
                self.right = Push(self.own(1), right.at[s], sems, to(1))
                self.left = Push(self.own(3), left.at[s], sems, to(3))

            def far(self):
                self.cross[2].arrived()
                add_into(self.own(2), inbox.at[self.s, 2])
                self.far_a.start()
                self.far_b.start()

            def sides(self):
                for d in (1, 3):
                    self.cross[d].arrived()
                    add_into(self.own(d), inbox.at[self.s, d])

            def go(self):
                self.far_a.arrived()
                add_into(self.own(1).at[pl.ds(0, half)], near.at[self.s, 0])
                self.right.start()
                self.far_b.arrived()
                add_into(self.own(3).at[pl.ds(half, half)], near.at[self.s, 1])
                self.left.start()

            def final(self):
                self.cross[0].arrived()
                self.right.arrived()
                self.left.arrived()
                s = self.s
                pieces = (self.own(0), inbox.at[s, 0], right.at[s], left.at[s])
                return functools.reduce(jnp.add, [p[...].astype(jnp.float32) for p in pieces])

            def close(self):
                for push in list(self.cross.values()) + [self.far_a, self.far_b, self.right, self.left]:
                    push.sent()

        def steps(body, before, totals):
            @pl.loop(0, 4 * SUBS)
            def _(t):
                for at, hook in before.items():
                    pl.when(t == at)(hook)
                s, i = t // 4, t % 4
                d = i + i // 2 - i // 3 * 2
                body(s, pl.ds((y + d) % 4 * 2, 2))
                for at in range(4 * SUBS):
                    push = totals[at // 4].cross[BACK[at % 4]]
                    pl.when(t == at)(push.start)

        def flat(value):
            return value.reshape(2 * rows, value.shape[-1])

        def pair(value):
            return value.reshape(2, rows, value.shape[-1])

        def forward(s, chip):
            sums = dot(flat(feeds[s, chip]), w_both[...], 1, 0)
            both[s, chip] = pair(sums.astype(jnp.bfloat16))
            bent, _ = gelu_terms(sums[:, :WIDE])
            low = (bent * sums[:, WIDE:]).astype(jnp.bfloat16)
            active[s, chip] = pair(low)
            part[s, chip] = pair(dot(low, w_down[...], 1, 0).astype(jnp.bfloat16))

        def backward(s, chip):
            grad = dot(flat(downs[s, chip]), w_down[...], 1, 1)
            sums = flat(both[s, chip]).astype(jnp.float32)
            bent, slope = gelu_terms(sums[:, :WIDE])
            gate_grad = (grad * sums[:, WIDE:] * slope).astype(jnp.bfloat16)
            up_grad = (grad * bent).astype(jnp.bfloat16)
            both[s, chip, :, :WIDE] = pair(gate_grad)
            both[s, chip, :, WIDE:] = pair(up_grad)
            part[s, chip] = pair(dot(flat(both[s, chip]), w_both[...], 1, 1).astype(jnp.bfloat16))

        span = lambda s: pl.ds(s * rows, rows)
        gain_out[...] = jnp.zeros_like(gain_out)
        square_out[...] = jnp.zeros_like(square_out)

        def norm_back(total, s):
            down = total.final()
            gain_row = gain_in[...]
            upstream = cotangent_in[span(s), :].astype(jnp.float32)
            scale = lax.rsqrt(jnp.mean(down * down, axis=-1, keepdims=True) + EPSILON)
            unit = down * scale
            result = hidden_in[span(s), :] + unit * gain_row
            block_out[span(s), :] = result.astype(jnp.bfloat16)
            square_out[...] += jnp.sum(result * result, axis=0, keepdims=True)
            gain_out[...] += jnp.sum(upstream * unit, axis=0, keepdims=True)
            scaled = gain_row * upstream
            grad = scale * (scaled - unit * jnp.mean(unit * scaled, axis=-1, keepdims=True))
            downs[s, y * 2 + c] = grad.astype(jnp.bfloat16)

        a, b = 0, 1
        first_a, relay_a, last_a, met_a, close_a = gather(feed_in.at[span(a)], feeds, a)
        first_b, relay_b, last_b, met_b, close_b = gather(feed_in.at[span(b)], feeds, b)
        sum_a, sum_b = Total(a), Total(b)
        first_a()
        for load in loads:
            load.start()
        own = [pltpu.make_async_copy(feed_in.at[span(s)], feeds.at[s, y * 2 + c], here.at[2 + s]) for s in (a, b)]
        for copy in own:
            copy.start()
        for copy in own + loads:
            copy.wait()

        def at_1():
            relay_a()
            first_b()
            met_a[1]()

        def at_2():
            last_a()
            met_a[3]()

        def at_3():
            relay_b()
            met_a[2]()

        def at_4():
            sum_a.far()
            met_b[0]()

        def at_5():
            last_b()
            sum_a.sides()
            met_b[1]()

        def at_6():
            sum_a.go()
            met_b[3]()

        steps(
            forward,
            {0: met_a[0], 1: at_1, 2: at_2, 3: at_3, 4: at_4, 5: at_5, 6: at_6, 7: met_b[2]},
            (sum_a, sum_b),
        )
        sum_b.far()
        norm_back(sum_a, a)
        sum_a.close()
        close_a()
        first_a, relay_a, last_a, met_a, close_a = gather(downs.at[a, y * 2 + c], downs, a)
        first_a()
        sum_b.sides()
        sum_b.go()
        old_a, old_b, old_close_b = sum_a, sum_b, close_b
        first_b, relay_b, last_b, met_b, close_b = gather(downs.at[b, y * 2 + c], downs, b)
        sum_a, sum_b = Total(a), Total(b)

        def back_1():
            relay_a()
            met_a[1]()

        def back_2():
            last_a()
            norm_back(old_b, b)
            old_b.close()
            old_close_b()
            first_b()
            met_a[3]()

        def back_4():
            sum_a.far()
            met_b[0]()

        def back_5():
            relay_b()
            sum_a.sides()
            met_b[1]()

        def back_6():
            last_b()
            sum_a.go()
            met_b[3]()

        steps(
            backward,
            {0: met_a[0], 1: back_1, 2: back_2, 3: met_a[2], 4: back_4, 5: back_5, 6: back_6, 7: met_b[2]},
            (sum_a, sum_b),
        )
        sum_b.far()
        sum_b.sides()
        every = 8 * tokens

        @pl.loop(0, WIDE // 128)
        def _(i):
            units = pl.ds(pl.multiple_of(i * 128, 128), 128)
            lhs = active[:, :, :, units].reshape(every, 128)
            down_out[units, :] = dot(lhs, downs[...].reshape(every, width), 0, 0).astype(jnp.bfloat16)

        sum_b.go()
        feed_out[span(a), :] = sum_a.final()

        @pl.loop(0, width // 128)
        def _(i):
            lanes = pl.ds(pl.multiple_of(i * 128, 128), 128)
            lhs = feeds[:, :, :, lanes].reshape(every, 128)
            both_out[lanes, :] = dot(lhs, both[...].reshape(every, 2 * WIDE), 0, 0).astype(jnp.bfloat16)

        feed_out[span(b), :] = sum_b.final()
        sum_a.close()
        sum_b.close()
        close_a()
        close_b()

    low, wide = jnp.bfloat16, jnp.float32
    blocks = (SUBS, 8, rows)
    scratch = [
        pltpu.VMEM(blocks + (width,), low),
        pltpu.VMEM(blocks + (width,), low),
        pltpu.VMEM(blocks + (2 * WIDE,), low),
        pltpu.VMEM(blocks + (WIDE,), low),
        pltpu.VMEM(blocks + (width,), low),
        pltpu.VMEM((SUBS, 4, rows, width), low),
        pltpu.VMEM((SUBS, 2, half, width), low),
        pltpu.VMEM((SUBS, rows, width), low),
        pltpu.VMEM((SUBS, rows, width), low),
        pltpu.VMEM((width, 2 * WIDE), low),
        pltpu.VMEM((WIDE, width), low),
    ]
    outs = [
        ((tokens, width), low),
        ((tokens, width), wide),
        ((1, width), wide),
        ((1, width), wide),
        ((width, 2 * WIDE), low),
        ((WIDE, width), low),
    ]
    return call(
        kernel, name, number, outs, [feed, full_both, full_down, hidden, cotangent, gain], scratch, 32 * SUBS,
        in_specs=[ANY, ANY, ANY, VMEM, VMEM, VMEM], out_specs=[VMEM] * 6, local=2 + SUBS,
    )


class Either:
    def __init__(self, core, sems, make):
        self.core, start = core, sems.used
        self.variants = []
        for order in (0, 1):
            sems.used = start
            self.variants.append(make(order))

    def run(self, name):
        for order in (0, 1):
            pl.when(self.core == order)(getattr(self.variants[order], name))

    def first(self):
        self.run("first")

    def relay(self):
        self.run("relay")

    def last(self):
        self.run("last")

    def close(self):
        self.run("close")


def split_lanes(ref, h):
    halves = lane_halves(ref.shape[-1])
    return None if halves[h] is None else ref.at[:, pl.ds(*halves[h])]


def whole_ref(ref):
    return ref


def ring_row(own, out, cut, sems):
    x, y, z, c = place()

    def make(order):
        slot = (lambda k: cut(out.at[x, k])) if order == 0 else (lambda k: cut(out.at[k, z]))
        peer = (lambda k: device(x, y, k, c)) if order == 0 else (lambda k: device(k, y, z, c))
        return RingGather(own, slot, lambda k, h: split_lanes(slot(k), h), (z, x)[order], peer, sems)

    return Either(c, sems, make)


def ring_rest(out, cut, sems):
    x, y, z, c = place()

    def make(order):
        if order == 0:
            slot, half, me = lambda k: cut(out.at[k]), lambda k, h: cut(out.at[k, pl.ds(2 * h, 2)]), x
        else:
            slot, half, me = lambda k: cut(out.at[:, k]), lambda k, h: cut(out.at[pl.ds(2 * h, 2), k]), z
        peer = (lambda k: device(k, y, z, c)) if order == 0 else (lambda k: device(x, y, k, c))
        return RingGather(slot(me), slot, half, me, peer, sems)

    return Either(c, sems, make)


class Crossing:
    def __init__(self, out, cut, other_cut, sems):
        x, y, z, c = place()
        self.pushes = []
        for d in range(4):

            def make(order, d=d):
                quarters = out.at[(x + d) % 4], out.at[:, (z + d) % 4]
                piece, lands = cut(quarters[order]), other_cut(quarters[1 - order])
                return Push(piece, piece, sems, device(x, y, z, 1 - c), lands)

            self.pushes.append(Either(c, sems, make))

    def start(self, d):
        self.pushes[d].run("start")

    def close(self):
        for push in self.pushes:
            push.run("arrived")
            push.run("sent")


def turn(values, cosine, sine):
    middle = values.shape[-1] // 2
    leading, trailing = values[:, :middle], values[:, middle:]
    return jnp.concatenate([leading * cosine - trailing * sine, trailing * cosine + leading * sine], axis=1)


def unit_rows(values):
    scale = lax.rsqrt(jnp.mean(values * values, axis=-1, keepdims=True) + EPSILON)
    return values * scale, scale


def allowed_keys(offset, beginning, rows, span):
    query = offset + lax.broadcasted_iota(jnp.int32, (rows, span), 0)
    key = offset + rows - span + lax.broadcasted_iota(jnp.int32, (rows, span), 1)
    return (key <= query) & (key > query - WINDOW) & (key >= beginning)


def gain_row(table, first, each, width):
    lane = lax.broadcasted_iota(jnp.int32, (128, width), 1)
    row = lax.broadcasted_iota(jnp.int32, (128, width), 0)
    owner = (lane * 7282) >> 16 if each == 9 else lane >> 1
    pick = (row == first + lane - owner * each).astype(jnp.float32).astype(jnp.bfloat16)
    spread = dot(table, pick, 1, 0)
    return jnp.sum(jnp.where(row == owner, spread, 0.0), axis=0, keepdims=True)


def lanes_of(start, size):
    return lambda ref: ref.at[(slice(None),) * (len(ref.shape) - 1) + (pl.ds(start, size),)]


def attend(number, stream, doc_starts, own_qkv, own_gains, own_output, own_both, own_down):
    tokens = stream.shape[0]
    span = tokens + WINDOW

    def kernel(
        stream_in, starts_in, qkv_in, gains_in, output_in, both_in, down_in,
        normed_out, query_out, key_out, turned_out, kv_out, probs_out, mixed_out, branch_out, hidden_out, feed_out,
        gains_out, cosine_out, sine_out, qkv_out, output_out, both_out, down_out,
        qkv_box, gains_box, both_box, flat, merge, qkv_own, gains_own, both_own, qkv_all, gains_all, output_all, kv,
        send, recv, here,
    ):
        x, y, z, c = place()
        q, s = lax.axis_index("seq"), lax.axis_index("shard")
        sems = Sems(send, recv)
        after, before = {"seq": (q + 1) % 16, "shard": s}, {"seq": (q + 15) % 16, "shard": s}
        greet(
            [device(x, y + dy, z, (c + dc) % 2) for dy, dc in SHARD_STEPS]
            + [device(x, y, z + 1, c), device(x, y, z + 3, c), device(x + 1, y, z, c), device(x + 3, y, z, c)]
            + [after, before]
        )
        sent = []

        def spread(source, box, pieces=False):
            pushes = []
            for dy, dc in SHARD_STEPS:
                to, back = (y + dy) % 4 * 2 + (c + dc) % 2, (y + 4 - dy) % 4 * 2 + (c + 2 - dc) % 2
                src = source.at[to] if pieces else source
                push = Push(src, box.at[s], sems, device(x, y + dy, z, (c + dc) % 2), box.at[back])
                push.start()
                pushes.append(push)
            box[s] = source[s] if pieces else source[...]
            sent.extend(pushes)
            return pushes

        def collect(pushes, box, own):
            for push in pushes:
                push.arrived()
            tiles = own.shape[-1] // 128
            for d in range(8):
                flat[: 9 * tiles, :] = box[d].astype(jnp.float32)
                for j in range(tiles):
                    merge[9 * d : 9 * d + 9, 128 * j : 128 * (j + 1)] = flat[pl.ds(j, 9, tiles), :]
            own[...] = merge[:, : own.shape[-1]].astype(own.dtype)

        my_lanes = lanes_of(pl.multiple_of(c * 768, 128), 768)
        their_lanes = lanes_of(pl.multiple_of((1 - c) * 768, 128), 768)
        mine = lambda ref: ref.at[(slice(None),) * (len(ref.shape) - 3) + (s,)]

        got_qkv = spread(qkv_in, qkv_box)
        got_gains = spread(gains_in, gains_box)
        down_ring = ring_row(down_in, down_out, whole_ref, sems)
        output_ring = ring_row(output_in, output_all, mine, sems)
        down_ring.first()
        output_ring.first()
        inputs = stream_in[...].astype(jnp.float32)
        unit = unit_rows(inputs)[0]
        starts = starts_in[...]
        positions = q * tokens + lax.broadcasted_iota(jnp.int32, (tokens, 1), 0)
        beginning = jnp.zeros((tokens, 1), jnp.int32)
        for j in range(8):
            start = starts[0:1, j : j + 1]
            beginning = jnp.maximum(beginning, jnp.where(start <= positions, start, 0))
        steps = lax.broadcasted_iota(jnp.int32, (1, HEAD_DIM // 2), 1).astype(jnp.float32)
        angles = (positions - beginning).astype(jnp.float32) * jnp.exp(steps * (-2.0 * math.log(10000.0) / HEAD_DIM))
        cosine_out[...] = jnp.cos(angles)
        sine_out[...] = jnp.sin(angles)

        own = lambda src, dst, at: pltpu.make_async_copy(src, dst, here.at[at])
        collect(got_qkv, qkv_box, qkv_own)
        qkv_ring = ring_row(my_lanes(qkv_own), qkv_all, my_lanes, sems)
        qkv_ring.first()
        got_both = spread(both_in, both_box, True)
        for push in got_gains:
            push.arrived()
        for d in range(8):
            gains_own[d : d + 1, :] = gains_box[d, 0:1, :]
        gains_ring = ring_row(gains_own, gains_all, whole_ref, sems)
        gains_ring.first()
        copies = [
            own(my_lanes(qkv_own), my_lanes(qkv_all.at[x, z]), 0),
            own(gains_own, gains_all.at[x, z], 1),
            own(down_in, down_out.at[x, z], 2),
            own(output_in, output_all.at[x, z, s], 3),
        ]
        for copy in copies:
            copy.start()
        down_ring.relay()
        output_ring.relay()
        qkv_ring.relay()
        gains_ring.relay()
        for copy in copies:
            copy.wait()
        qkv_ring.last()
        gains_ring.last()
        qkv_rest = ring_rest(qkv_all, my_lanes, sems)
        gains_rest = ring_rest(gains_all, whole_ref, sems)
        qkv_cross = Crossing(qkv_all, my_lanes, their_lanes, sems)
        qkv_rest.first()
        gains_rest.first()
        qkv_cross.start(0)
        down_ring.last()
        output_ring.last()
        down_rest = ring_rest(down_out, whole_ref, sems)
        output_rest = ring_rest(output_all, mine, sems)
        output_rest.first()
        down_rest.first()
        collect(got_both, both_box, both_own)
        both_ring = ring_row(both_own, both_out, whole_ref, sems)
        both_ring.first()
        both_copy = own(both_own, both_out.at[x, z], 4)
        both_copy.start()
        qkv_rest.relay()
        gains_rest.relay()
        qkv_cross.start(3)
        qkv_cross.start(1)
        output_rest.relay()
        both_ring.relay()
        down_rest.relay()
        qkv_rest.last()
        gains_rest.last()
        qkv_cross.start(2)
        output_rest.last()
        other = device(x, y, z, 1 - c)
        column = lambda k: output_all.at[:, :, k * 2 + c]
        output_y = RingGather(
            column(y), column, lambda k, h: output_all.at[pl.ds(2 * h, 2), :, k * 2 + c],
            y, lambda k: device(x, k, z, c), sems,
        )
        output_cross = [
            Push(column((y + d) % 4), column((y + d) % 4), sems, other, output_all.at[:, :, (y + d) % 4 * 2 + 1 - c])
            for d in range(4)
        ]
        output_y.first()
        output_cross[0].start()
        both_ring.last()
        both_copy.wait()
        both_rest = ring_rest(both_out, whole_ref, sems)
        table = gains_all[...].reshape(128, 128).astype(jnp.bfloat16)
        for g in range(4):
            gains_out[g : g + 1, :] = gain_row(table, 16 * g, 9, D)
        for g in range(2):
            gains_out[4 + g : 5 + g, :HEAD_DIM] = gain_row(table, 64 + 16 * g, 2, HEAD_DIM)
        qkv_cross.close()

        @pl.loop(0, 8)
        def _(i):
            pair = [qkv_all[i // 2, i % 2 * 2 + k].astype(jnp.float32) for k in range(2)]
            qkv_out[pl.ds(pl.multiple_of(144 * i, 144), 144), :] = jnp.concatenate(pair, axis=0).astype(jnp.bfloat16)

        near = Push(kv.at[2], kv.at[1], sems, after)
        far = Push(kv.at[1], kv.at[0], sems, after)
        normed = (unit * gains_out[0:1, :]).astype(jnp.bfloat16)
        normed_out[...] = normed
        key_value = dot(normed, qkv_out[:, 1024:], 1, 0)
        key = key_value[:, :HEAD_DIM]
        key_out[...] = key
        key_turned = turn(unit_rows(key)[0] * gains_out[5:6, :HEAD_DIM], cosine_out[...], sine_out[...])
        kv[2, :, :HEAD_DIM] = key_turned.astype(jnp.bfloat16)
        kv[2, :, HEAD_DIM:] = key_value[:, HEAD_DIM:].astype(jnp.bfloat16)
        near.start()
        both_rest.first()
        output_y.relay()
        output_cross[1].start()
        output_cross[3].start()
        for h in range(HEADS):
            lanes = slice(h * HEAD_DIM, (h + 1) * HEAD_DIM)
            span_h = slice(h * tokens, (h + 1) * tokens)
            query = dot(normed, qkv_out[:, lanes], 1, 0)
            query_out[span_h, :] = query
            turned = turn(unit_rows(query)[0] * gains_out[4:5, :HEAD_DIM], cosine_out[...], sine_out[...])
            turned_out[span_h, :] = turned.astype(jnp.bfloat16)
        near.arrived()
        far.start()
        output_y.last()
        output_cross[2].start()
        down_rest.last()
        both_rest.relay()
        for push in output_cross:
            push.arrived()

        @pl.loop(0, 16)
        def _(i):
            for j in range(4):
                pair = [output_all[i // 4, i % 4, 2 * j + k].astype(jnp.float32) for k in range(2)]
                rows = pl.ds(pl.multiple_of(64 * i + 16 * j, 16), 16)
                output_out[rows, :] = jnp.concatenate(pair, axis=0).astype(jnp.bfloat16)

        far.arrived()
        kv_out[...] = kv[...].reshape(span, 2 * HEAD_DIM)
        allowed = allowed_keys(q * tokens, beginning, tokens, span)
        keys, values = kv_out[:, :HEAD_DIM], kv_out[:, HEAD_DIM:]
        for h in range(HEADS):
            span_h = slice(h * tokens, (h + 1) * tokens)
            scores = dot(turned_out[span_h, :], keys, 1, 1) * HEAD_DIM ** (-0.5)
            scores = jnp.where(allowed, scores, NEGATIVE)
            exponent = jnp.exp(scores - jnp.max(scores, axis=-1, keepdims=True))
            probs = exponent / jnp.sum(exponent, axis=-1, keepdims=True)
            probs_out[span_h, :] = probs
            mixed_out[:, h * HEAD_DIM : (h + 1) * HEAD_DIM] = dot(probs.astype(jnp.bfloat16), values, 1, 0).astype(
                jnp.bfloat16
            )
        branch = dot(mixed_out[...], output_out[...], 1, 0)
        branch_out[...] = branch
        hidden = inputs + unit_rows(branch)[0] * gains_out[1:2, :]
        hidden_out[...] = hidden
        feed_out[...] = (unit_rows(hidden)[0] * gains_out[2:3, :]).astype(jnp.bfloat16)
        both_rest.last()
        rings = [qkv_ring, gains_ring, down_ring, output_ring, both_ring]
        rings += [qkv_rest, gains_rest, down_rest, output_rest, both_rest, output_y]
        for ring in rings:
            ring.close()
        for push in sent + output_cross + [near, far]:
            push.sent()

    low, wide = jnp.bfloat16, jnp.float32
    outs = [
        ((tokens, D), low),
        ((HEADS * tokens, HEAD_DIM), wide),
        ((tokens, HEAD_DIM), wide),
        ((HEADS * tokens, HEAD_DIM), low),
        ((span, 2 * HEAD_DIM), low),
        ((HEADS * tokens, span), wide),
        ((tokens, HEADS * HEAD_DIM), low),
        ((tokens, D), wide),
        ((tokens, D), wide),
        ((tokens, D), low),
        ((8, D), wide),
        ((tokens, HEAD_DIM // 2), wide),
        ((tokens, HEAD_DIM // 2), wide),
        ((D, 1536), low),
        ((HEADS * HEAD_DIM, D), low),
        ((4, 4, 72, 2 * WIDE), low),
        ((4, 4, PIECE, D), low),
    ]
    scratch = [
        pltpu.VMEM((8, 108, 128), low),
        pltpu.VMEM((8, 8, 128), wide),
        pltpu.VMEM((8, 126, 128), low),
        pltpu.VMEM((128, 128), wide),
        pltpu.VMEM((72, 2 * WIDE), wide),
        pltpu.VMEM((72, 1536), low),
        pltpu.VMEM((8, 128), wide),
        pltpu.VMEM((72, 2 * WIDE), low),
        pltpu.VMEM((4, 4, 72, 1536), low),
        pltpu.VMEM((4, 4, 8, 128), wide),
        pltpu.VMEM((4, 4, 8, 8, D), low),
        pltpu.VMEM((3, tokens, 2 * HEAD_DIM), low),
    ]
    return call(
        kernel, "attend", number, outs, [stream, doc_starts, own_qkv, own_gains, own_output, own_both, own_down],
        scratch, 21 + 10 * 4 + 4 + 4 + 4 + 2, in_specs=[VMEM] * 7, out_specs=[VMEM] * 15 + [ANY] * 2, local=5,
    )


def norm_rows(values, weight):
    return values * lax.rsqrt(jnp.mean(values * values, axis=-1, keepdims=True) + EPSILON) * weight


def head_prep(values, weight, cosine, sine):
    return turn(norm_rows(values, weight), cosine, sine)


def matmul(a, b):
    return jnp.dot(a, b, preferred_element_type=jnp.float32)


def matmul_tn(a, b):
    return lax.dot_general(a, b, (((0,), (0,)), ((), ())), preferred_element_type=jnp.float32)


def matmul_nt(a, b):
    return lax.dot_general(a, b, (((1,), (1,)), ((), ())), preferred_element_type=jnp.float32)


def heads_first(values):
    return jnp.concatenate([values[:, h * HEAD_DIM : (h + 1) * HEAD_DIM] for h in range(HEADS)], axis=0)


def heads_last(values):
    rows = values.shape[0] // HEADS
    return jnp.concatenate([values[h * rows : (h + 1) * rows] for h in range(HEADS)], axis=1)


def pad_rows(values, rows):
    return jnp.pad(values, ((0, rows - values.shape[0]), (0, 128 - values.shape[1])))


def split_hidden(weight):
    parts = weight.reshape(9, 16, 8, PIECE).transpose(2, 0, 1, 3)
    return jnp.pad(parts, ((0, 0), (0, 0), (0, 0), (0, SLOT - PIECE))).reshape(8, 9, WIDE)


def local(
    stream, doc_starts, cotangent, attention_norm, query_weight, key_weight, value_weight, query_norm, key_norm,
    output_weight, attention_post_norm, mlp_norm, gate_weight, up_weight, down_weight, mlp_post_norm,
):
    tokens = stream.shape[1]
    scale = HEAD_DIM ** (-0.5)
    inputs = stream[0].astype(jnp.float32)
    upstream = cotangent[0].astype(jnp.float32)
    own_qkv = jnp.concatenate([query_weight, key_weight, value_weight], axis=1)
    norms = (attention_norm, attention_post_norm, mlp_norm, mlp_post_norm, query_norm, key_norm)
    own_gains = jnp.concatenate([jnp.pad(g, (0, 16 - g.shape[0])) for g in norms] + [jnp.zeros((32,), jnp.bfloat16)])
    own_gains = jnp.broadcast_to(own_gains.astype(jnp.float32)[None], (8, 128))
    own_both = jnp.concatenate([split_hidden(gate_weight), split_hidden(up_weight)], axis=2)
    (
        normed, query_proj, key_proj, query_rot, kv, probability, mixed, branch, hidden, feed,
        gain_rows, cosine, sine, full_qkv, full_output, both16, down16,
    ) = attend(
        0, stream[0], doc_starts, own_qkv.reshape(108, 128), own_gains, output_weight, own_both.reshape(8, 126, 128),
        down_weight,
    )
    gain_input, gain_post, gain_mlp, gain_mlp_post = (gain_rows[i] for i in range(4))
    gain_query, gain_key = gain_rows[4, :HEAD_DIM], gain_rows[5, :HEAD_DIM]
    keys_all, values_all = kv[:, :HEAD_DIM], kv[:, HEAD_DIM:]
    probability_low = probability.astype(jnp.bfloat16)
    full_both = both16.reshape(D, 2 * WIDE)
    full_down = jnp.pad(down16.reshape(16, PIECE, D), ((0, 0), (0, SLOT - PIECE), (0, 0))).reshape(WIDE, D)

    block_output, feed_grad, gain_mlp_post_grad, result_squares, both_term, down_term = feed_forward(
        "feed_forward", 2, feed, full_both, full_down, hidden, cotangent[0], gain_mlp_post[None]
    )

    hidden_extra, gain_mlp_grad = jax.vjp(norm_rows, hidden, gain_mlp)[1](feed_grad)
    hidden_grad = upstream + hidden_extra
    branch_grad, gain_post_grad = jax.vjp(norm_rows, branch, gain_post)[1](hidden_grad)
    branch_low = branch_grad.astype(jnp.bfloat16)
    output_term = matmul_tn(mixed, branch_low).astype(jnp.bfloat16)
    mixed_grad = heads_first(matmul_nt(branch_low, full_output).astype(jnp.bfloat16))
    prob_grad = matmul_nt(mixed_grad, values_all)
    inner_sum = jnp.sum(probability * prob_grad, axis=-1, keepdims=True)
    score_low = (probability * (prob_grad - inner_sum) * scale).astype(jnp.bfloat16)
    query_grad_rot = matmul(score_low, keys_all)
    key_grads = matmul_tn(score_low, query_rot)
    value_grads = matmul_tn(probability_low, mixed_grad)
    kv_grads = jnp.concatenate([key_grads, value_grads], axis=1)
    returned = halo(
        "halo_back", 3, (-2, -1), kv_grads[:WINDOW].astype(jnp.bfloat16).reshape(2, tokens, 2 * HEAD_DIM)
    )
    kv_own = kv_grads[WINDOW:] + returned[0].astype(jnp.float32) + returned[1].astype(jnp.float32)
    query_grad, gain_query_grad = jax.vjp(lambda v, w: head_prep(v, w, jnp.concatenate([cosine] * HEADS), jnp.concatenate([sine] * HEADS)), query_proj, gain_query)[1](
        query_grad_rot
    )
    key_grad, gain_key_grad = jax.vjp(lambda v, w: head_prep(v, w, cosine, sine), key_proj, gain_key)[1](
        kv_own[:, :HEAD_DIM]
    )
    qkv_low = jnp.concatenate([heads_last(query_grad), key_grad, kv_own[:, HEAD_DIM:]], axis=1).astype(jnp.bfloat16)
    qkv_term = matmul_tn(normed, qkv_low).astype(jnp.bfloat16)
    normed_grad = matmul_nt(qkv_low, full_qkv)
    input_extra, gain_input_grad = jax.vjp(norm_rows, inputs, gain_input)[1](normed_grad)
    stream_grad = (hidden_grad + input_extra).astype(jnp.bfloat16)

    squares = jnp.stack([jnp.sum(inputs * inputs), jnp.sum(hidden * hidden), jnp.sum(result_squares)])
    small = [g.reshape(16, 72) for g in (gain_input_grad, gain_post_grad, gain_mlp_grad, gain_mlp_post_grad)]
    small += [jnp.pad(g.reshape(16, 16), ((0, 0), (0, 56))) for g in (gain_query_grad, gain_key_grad)]
    small.append(jnp.pad(jnp.broadcast_to(squares[None], (16, 3)), ((0, 0), (0, 69))))
    small = jnp.pad(jnp.stack(small, axis=1), ((0, 0), (0, 1), (0, 56))).reshape(4, 4, 8, 128)
    down_blocks = down_term.reshape(16, SLOT, D)[:, :PIECE].reshape(4, 4, PIECE, D)
    both_sum, small_sum, down_sum, qkv_sum, output_sum = sum_seq(
        "sum_weights", 4, [both_term.reshape(4, 4, 72, 2 * WIDE), small], [down_blocks],
        [(qkv_term.reshape(4, 4, 72, 1536), 768, 768), (output_term.reshape(4, 4, 64, D), 512, 640)],
    )
    small_all, both_rows, qkv_rows, output_rows = exchange_shard(
        "exchange_grads", 5, [small_sum],
        [both_sum.reshape(8, 9, 2 * WIDE), qkv_sum.reshape(8, 9, 768), output_sum.reshape(8, 8, 640)],
    )

    def whole(rows):
        parts = rows.reshape(8, 9, 16, SLOT)[..., :PIECE]
        return parts.transpose(1, 2, 0, 3).reshape(9, FF).astype(jnp.float32)

    qkv_grad = jnp.sum(qkv_rows.reshape(4, 2, 9, 768).astype(jnp.float32), axis=0)
    qkv_grad = jnp.concatenate([qkv_grad[0], qkv_grad[1]], axis=1)
    output_grad = jnp.sum(output_rows.reshape(4, 2, 8, 640).astype(jnp.float32), axis=0)
    output_grad = jnp.concatenate([output_grad[0][:, :512], output_grad[1]], axis=1)
    small_sum = jnp.sum(small_all, axis=0)
    shard = lax.axis_index("shard")
    gain_grads = lax.dynamic_slice_in_dim(small_sum, shard * 9, 9, 1)
    head_grads = lax.dynamic_slice_in_dim(small_sum, shard * 2, 2, 1)
    stream_rms = jnp.sqrt(small_sum[6, :3] / (32768 * D))
    return (
        block_output[None],
        stream_grad[None],
        gain_grads[0],
        qkv_grad[:, :1024],
        qkv_grad[:, 1024:1280],
        qkv_grad[:, 1280:],
        head_grads[4],
        head_grads[5],
        output_grad,
        gain_grads[1],
        gain_grads[2],
        whole(both_rows[:, :, :WIDE]),
        whole(both_rows[:, :, WIDE:]),
        down_sum.astype(jnp.float32),
        gain_grads[3],
        stream_rms,
    )


def solution(mesh):
    rows = P(("seq", "shard"))
    tokens = P("shard", "seq", None)
    table = P(("seq", "shard"), None)
    return jax.shard_map(
        local,
        mesh=mesh,
        in_specs=(
            tokens, P("shard", None), tokens, rows, table, table, table, rows, rows, table, rows, rows, table, table,
            table, rows,
        ),
        out_specs=(
            tokens, tokens, rows, table, table, table, rows, rows, table, rows, rows, table, table, table, rows, P(),
        ),
        check_vma=False,
    )
```

```python
import functools
import math
from types import SimpleNamespace

import jax
import jax.numpy as jnp
from jax import lax
from jax.experimental import pallas as pl
from jax.experimental.pallas import tpu as pltpu
from jax.sharding import PartitionSpec as P

D = 1152
HEADS = 4
HEAD_DIM = 256
WINDOW = 512
FF = 6912
PIECE = 54
SLOT = 56
WIDE = 16 * SLOT

EPSILON = 1e-06
NEGATIVE = -1e30
MESH = pl.DeviceIdType.MESH
MIB = 2**20


def place():
    q, s = lax.axis_index("seq"), lax.axis_index("shard")
    return q // 4, s // 2, q % 4, s % 2


def device(x, y, z, c):
    return {"seq": x % 4 * 4 + z % 4, "shard": y % 4 * 2 + c}


def greet(targets):
    barrier = pltpu.get_barrier_semaphore()
    for target in targets:
        pl.semaphore_signal(barrier, inc=1, device_id=target, device_id_type=MESH)
    pl.semaphore_wait(barrier, len(targets))


class Sems:
    def __init__(self, send, recv):
        self.send, self.recv, self.used = send, recv, 0

    def take(self):
        self.used += 1
        return self.send.at[self.used - 1], self.recv.at[self.used - 1]


class Push:
    def __init__(self, src, dst, sems, to, lands=None):
        send, recv = sems.take()
        self.out = pltpu.make_async_remote_copy(
            src_ref=src, dst_ref=dst, send_sem=send, recv_sem=recv, device_id=to, device_id_type=MESH
        )
        lands = dst if lands is None else lands
        self.back = pltpu.make_async_remote_copy(
            src_ref=lands, dst_ref=lands, send_sem=send, recv_sem=recv, device_id=to, device_id_type=MESH
        )

    def start(self):
        self.out.start()

    def arrived(self):
        self.back.wait_recv()

    def sent(self):
        self.out.wait_send()


class RingGather:
    def __init__(self, own, slot, half, me, peer, sems):
        up, down, far = (me + 1) % 4, (me + 3) % 4, (me + 2) % 4
        self.right = Push(own, slot(me), sems, peer(up), slot(down))
        self.left = Push(own, slot(me), sems, peer(down), slot(up))
        self.right2 = Push(half(down, 0), half(down, 0), sems, peer(up), half(far, 0))
        split = half(up, 1)
        self.left2 = None if split is None else Push(split, split, sems, peer(down), half(far, 1))

    def first(self):
        self.right.start()
        self.left.start()

    def relay(self):
        self.right.arrived()
        self.right2.start()
        self.left.arrived()
        if self.left2 is not None:
            self.left2.start()

    def last(self):
        self.right2.arrived()
        if self.left2 is not None:
            self.left2.arrived()

    def close(self):
        for push in (self.right, self.left, self.right2, self.left2):
            if push is not None:
                push.sent()


class RingSum:
    def __init__(self, chunk, half, inbox, me, peer, sems, add):
        up, down, far = (me + 1) % 4, (me + 3) % 4, (me + 2) % 4
        self.chunk, self.half, self.inbox, self.add = chunk, half, inbox, add
        self.me, self.up, self.down = me, up, down
        near_a, near_b, right, left = inbox
        self.far_a = Push(half(far, 0), near_a, sems, peer(up))
        split = half(far, 1)
        self.far_b = None if split is None else Push(split, near_b, sems, peer(down))
        self.right = Push(chunk(up), right, sems, peer(up))
        self.left = Push(chunk(down), left, sems, peer(down))

    def first(self):
        self.far_a.start()
        if self.far_b is not None:
            self.far_b.start()

    def second(self):
        self.far_a.arrived()
        self.add(self.half(self.up, 0), self.inbox[0])
        self.right.start()
        if self.far_b is not None:
            self.far_b.arrived()
            self.add(self.half(self.down, 1), self.inbox[1])
        self.left.start()

    def third(self):
        self.right.arrived()
        self.add(self.chunk(self.me), self.inbox[2])
        self.left.arrived()
        self.add(self.chunk(self.me), self.inbox[3])

    def close(self):
        for push in (self.far_a, self.far_b, self.right, self.left):
            if push is not None:
                push.sent()


def add_into(total, extra):
    if len(total.shape) == 2:
        summed = total[...].astype(jnp.float32) + extra[...].astype(jnp.float32)
        total[...] = summed.astype(total.dtype)
        return

    @pl.loop(0, total.shape[0])
    def _(step):
        add_into(total.at[step], extra.at[step])


ANY = pl.BlockSpec(memory_space=pl.ANY)
VMEM = pl.BlockSpec(memory_space=pltpu.VMEM)


def call(kernel, name, number, outs, ins, scratch, copies, in_specs=None, out_specs=None, local=0, aliases=None):
    outs = [jax.ShapeDtypeStruct(shape, dtype) for shape, dtype in outs]
    scratch = list(scratch) + [pltpu.SemaphoreType.DMA((copies,)), pltpu.SemaphoreType.DMA((copies,))]
    if local:
        scratch.append(pltpu.SemaphoreType.DMA((local,)))
    return pl.pallas_call(
        kernel,
        name=name,
        out_shape=outs,
        in_specs=in_specs or [ANY] * len(ins),
        out_specs=out_specs or [ANY] * len(outs),
        scratch_shapes=scratch,
        input_output_aliases=aliases or {},
        compiler_params=pltpu.CompilerParams(
            collective_id=number, has_side_effects=True, vmem_limit_bytes=60 * MIB
        ),
    )(*ins)


SHARD_STEPS = [(dy, dc) for dy in range(4) for dc in range(2) if dy or dc]


def lane_halves(width):
    low = width // 256 * 128 if width % 256 == 0 else (width // 128 + 1) // 2 * 128
    return ((0, low), (low, width - low)) if width > 128 else ((0, width), None)


def dot(a, b, contract_a, contract_b):
    return lax.dot_general(a, b, (((contract_a,), (contract_b,)), ((), ())), preferred_element_type=jnp.float32)


SUBS = 2
BACK = (0, 1, 3, 2)


def gelu_terms(gate):
    a, b = math.sqrt(2.0 / math.pi), 0.044715
    square = gate * gate
    bend = jnp.tanh(a * gate * (1.0 + b * square))
    half = 0.5 * (1.0 + bend)
    slope = half + 0.5 * gate * (1.0 - bend * bend) * a * (1.0 + 3.0 * b * square)
    return gate * half, slope


def feed_forward(name, number, feed, full_both, full_down, hidden, cotangent, gain):
    tokens, width = feed.shape
    rows = tokens // SUBS
    half = rows // 2

    def kernel(
        feed_in, both_in, down_in, hidden_in, cotangent_in, gain_in,
        block_out, feed_out, gain_out, square_out, both_out, down_out,
        feeds, downs, both, active, part, inbox, near, right, left, w_both, w_down, send, recv, here,
    ):
        x, y, z, c = place()
        sems = Sems(send, recv)
        other = device(x, y, z, 1 - c)
        to = lambda d: device(x, y + d, z, c)
        greet([to(1), to(3), other])
        loads = [
            pltpu.make_async_copy(both_in, w_both, here.at[0]),
            pltpu.make_async_copy(down_in, w_down, here.at[1]),
        ]

        def gather(source, blocks, s):
            slot = lambda k: blocks.at[s, k * 2 + c]
            ring = RingGather(
                source, slot, lambda k, h: blocks.at[s, k * 2 + c, pl.ds(h * half, half)],
                y, lambda k: device(x, k, z, c), sems,
            )
            cross = []
            for d in range(4):
                k = (y + d) % 4
                cross.append(
                    Push(source if d == 0 else slot(k), slot(k), sems, other, blocks.at[s, k * 2 + 1 - c])
                )

            def first():
                ring.first()
                cross[0].start()

            def relay():
                ring.relay()
                cross[1].start()
                cross[3].start()

            def last():
                ring.last()
                cross[2].start()

            def close():
                ring.close()
                for push in cross:
                    push.sent()

            return first, relay, last, [push.arrived for push in cross], close

        class Total:
            def __init__(self, s):
                self.s = s
                self.cross = {}
                for d in range(4):
                    k = (y + d) % 4
                    self.cross[d] = Push(part.at[s, k * 2 + 1 - c], inbox.at[s, d], sems, other)
                self.own = lambda d: part.at[s, (y + d) % 4 * 2 + c]
                self.far_a = Push(self.own(2).at[pl.ds(0, half)], near.at[s, 0], sems, to(1))
                self.far_b = Push(self.own(2).at[pl.ds(half, half)], near.at[s, 1], sems, to(3))
                self.right = Push(self.own(1), right.at[s], sems, to(1))
                self.left = Push(self.own(3), left.at[s], sems, to(3))

            def far(self):
                self.cross[2].arrived()
                add_into(self.own(2), inbox.at[self.s, 2])
                self.far_a.start()
                self.far_b.start()

            def sides(self):
                for d in (1, 3):
                    self.cross[d].arrived()
                    add_into(self.own(d), inbox.at[self.s, d])

            def go(self):
                self.far_a.arrived()
                add_into(self.own(1).at[pl.ds(0, half)], near.at[self.s, 0])
                self.right.start()
                self.far_b.arrived()
                add_into(self.own(3).at[pl.ds(half, half)], near.at[self.s, 1])
                self.left.start()

            def final(self):
                self.cross[0].arrived()
                self.right.arrived()
                self.left.arrived()
                s = self.s
                pieces = (self.own(0), inbox.at[s, 0], right.at[s], left.at[s])
                return functools.reduce(jnp.add, [p[...].astype(jnp.float32) for p in pieces])

            def close(self):
                for push in list(self.cross.values()) + [self.far_a, self.far_b, self.right, self.left]:
                    push.sent()

        def steps(body, before, totals):
            @pl.loop(0, 4 * SUBS)
            def _(t):
                for at, hook in before.items():
                    pl.when(t == at)(hook)
                s, i = t // 4, t % 4
                d = i + i // 2 - i // 3 * 2
                body(s, pl.ds((y + d) % 4 * 2, 2))
                for at in range(4 * SUBS):
                    push = totals[at // 4].cross[BACK[at % 4]]
                    pl.when(t == at)(push.start)

        def flat(value):
            return value.reshape(2 * rows, value.shape[-1])

        def pair(value):
            return value.reshape(2, rows, value.shape[-1])

        def forward(s, chip):
            sums = dot(flat(feeds[s, chip]), w_both[...], 1, 0)
            both[s, chip] = pair(sums.astype(jnp.bfloat16))
            bent, _ = gelu_terms(sums[:, :WIDE])
            low = (bent * sums[:, WIDE:]).astype(jnp.bfloat16)
            active[s, chip] = pair(low)
            part[s, chip] = pair(dot(low, w_down[...], 1, 0).astype(jnp.bfloat16))

        def backward(s, chip):
            grad = dot(flat(downs[s, chip]), w_down[...], 1, 1)
            sums = flat(both[s, chip]).astype(jnp.float32)
            bent, slope = gelu_terms(sums[:, :WIDE])
            gate_grad = (grad * sums[:, WIDE:] * slope).astype(jnp.bfloat16)
            up_grad = (grad * bent).astype(jnp.bfloat16)
            both[s, chip, :, :WIDE] = pair(gate_grad)
            both[s, chip, :, WIDE:] = pair(up_grad)
            part[s, chip] = pair(dot(flat(both[s, chip]), w_both[...], 1, 1).astype(jnp.bfloat16))

        span = lambda s: pl.ds(s * rows, rows)
        gain_out[...] = jnp.zeros_like(gain_out)
        square_out[...] = jnp.zeros_like(square_out)

        def norm_back(total, s):
            down = total.final()
            gain_row = gain_in[...]
            upstream = cotangent_in[span(s), :].astype(jnp.float32)
            scale = lax.rsqrt(jnp.mean(down * down, axis=-1, keepdims=True) + EPSILON)
            unit = down * scale
            result = hidden_in[span(s), :] + unit * gain_row
            block_out[span(s), :] = result.astype(jnp.bfloat16)
            square_out[...] += jnp.sum(result * result, axis=0, keepdims=True)
            gain_out[...] += jnp.sum(upstream * unit, axis=0, keepdims=True)
            scaled = gain_row * upstream
            grad = scale * (scaled - unit * jnp.mean(unit * scaled, axis=-1, keepdims=True))
            downs[s, y * 2 + c] = grad.astype(jnp.bfloat16)

        a, b = 0, 1
        first_a, relay_a, last_a, met_a, close_a = gather(feed_in.at[span(a)], feeds, a)
        first_b, relay_b, last_b, met_b, close_b = gather(feed_in.at[span(b)], feeds, b)
        sum_a, sum_b = Total(a), Total(b)
        first_a()
        for load in loads:
            load.start()
        own = [pltpu.make_async_copy(feed_in.at[span(s)], feeds.at[s, y * 2 + c], here.at[2 + s]) for s in (a, b)]
        for copy in own:
            copy.start()
        for copy in own + loads:
            copy.wait()

        def at_1():
            relay_a()
            first_b()
            met_a[1]()

        def at_2():
            last_a()
            met_a[3]()

        def at_3():
            relay_b()
            met_a[2]()

        def at_4():
            sum_a.far()
            met_b[0]()

        def at_5():
            last_b()
            sum_a.sides()
            met_b[1]()

        def at_6():
            sum_a.go()
            met_b[3]()

        steps(
            forward,
            {0: met_a[0], 1: at_1, 2: at_2, 3: at_3, 4: at_4, 5: at_5, 6: at_6, 7: met_b[2]},
            (sum_a, sum_b),
        )
        sum_b.far()
        norm_back(sum_a, a)
        sum_a.close()
        close_a()
        first_a, relay_a, last_a, met_a, close_a = gather(downs.at[a, y * 2 + c], downs, a)
        first_a()
        sum_b.sides()
        sum_b.go()
        old_a, old_b, old_close_b = sum_a, sum_b, close_b
        first_b, relay_b, last_b, met_b, close_b = gather(downs.at[b, y * 2 + c], downs, b)
        sum_a, sum_b = Total(a), Total(b)

        def back_1():
            relay_a()
            met_a[1]()

        def back_2():
            last_a()
            norm_back(old_b, b)
            old_b.close()
            old_close_b()
            first_b()
            met_a[3]()

        def back_4():
            sum_a.far()
            met_b[0]()

        def back_5():
            relay_b()
            sum_a.sides()
            met_b[1]()

        def back_6():
            last_b()
            sum_a.go()
            met_b[3]()

        steps(
            backward,
            {0: met_a[0], 1: back_1, 2: back_2, 3: met_a[2], 4: back_4, 5: back_5, 6: back_6, 7: met_b[2]},
            (sum_a, sum_b),
        )
        sum_b.far()
        sum_b.sides()
        every = 8 * tokens

        @pl.loop(0, WIDE // 128)
        def _(i):
            units = pl.ds(pl.multiple_of(i * 128, 128), 128)
            lhs = active[:, :, :, units].reshape(every, 128)
            down_out[units, :] = dot(lhs, downs[...].reshape(every, width), 0, 0).astype(jnp.bfloat16)

        sum_b.go()
        feed_out[span(a), :] = sum_a.final()

        @pl.loop(0, width // 128)
        def _(i):
            lanes = pl.ds(pl.multiple_of(i * 128, 128), 128)
            lhs = feeds[:, :, :, lanes].reshape(every, 128)
            both_out[lanes, :] = dot(lhs, both[...].reshape(every, 2 * WIDE), 0, 0).astype(jnp.bfloat16)

        feed_out[span(b), :] = sum_b.final()
        sum_a.close()
        sum_b.close()
        close_a()
        close_b()

    low, wide = jnp.bfloat16, jnp.float32
    blocks = (SUBS, 8, rows)
    scratch = [
        pltpu.VMEM(blocks + (width,), low),
        pltpu.VMEM(blocks + (width,), low),
        pltpu.VMEM(blocks + (2 * WIDE,), low),
        pltpu.VMEM(blocks + (WIDE,), low),
        pltpu.VMEM(blocks + (width,), low),
        pltpu.VMEM((SUBS, 4, rows, width), low),
        pltpu.VMEM((SUBS, 2, half, width), low),
        pltpu.VMEM((SUBS, rows, width), low),
        pltpu.VMEM((SUBS, rows, width), low),
        pltpu.VMEM((width, 2 * WIDE), low),
        pltpu.VMEM((WIDE, width), low),
    ]
    outs = [
        ((tokens, width), low),
        ((tokens, width), wide),
        ((1, width), wide),
        ((1, width), wide),
        ((width, 2 * WIDE), low),
        ((WIDE, width), low),
    ]
    return call(
        kernel, name, number, outs, [feed, full_both, full_down, hidden, cotangent, gain], scratch, 32 * SUBS,
        in_specs=[ANY, ANY, ANY, VMEM, VMEM, VMEM], out_specs=[VMEM] * 6, local=2 + SUBS,
    )


class Either:
    def __init__(self, core, sems, make):
        self.core, start = core, sems.used
        self.variants = []
        for order in (0, 1):
            sems.used = start
            self.variants.append(make(order))

    def __getattr__(self, name):
        def run():
            for order in (0, 1):
                pl.when(self.core == order)(getattr(self.variants[order], name))

        return run


def split_lanes(ref, h):
    halves = lane_halves(ref.shape[-1])
    return None if halves[h] is None else ref.at[:, pl.ds(*halves[h])]


def whole_ref(ref):
    return ref


def ring_row(own, out, cut, sems):
    x, y, z, c = place()

    def make(order):
        slot = (lambda k: cut(out.at[x, k])) if order == 0 else (lambda k: cut(out.at[k, z]))
        peer = (lambda k: device(x, y, k, c)) if order == 0 else (lambda k: device(k, y, z, c))
        return RingGather(own, slot, lambda k, h: split_lanes(slot(k), h), (z, x)[order], peer, sems)

    return Either(c, sems, make)


def ring_rest(out, cut, sems):
    x, y, z, c = place()

    def make(order):
        if order == 0:
            slot, half, me = lambda k: cut(out.at[k]), lambda k, h: cut(out.at[k, pl.ds(2 * h, 2)]), x
        else:
            slot, half, me = lambda k: cut(out.at[:, k]), lambda k, h: cut(out.at[pl.ds(2 * h, 2), k]), z
        peer = (lambda k: device(k, y, z, c)) if order == 0 else (lambda k: device(x, y, k, c))
        return RingGather(slot(me), slot, half, me, peer, sems)

    return Either(c, sems, make)


class Crossing:
    def __init__(self, out, cut, other_cut, sems):
        x, y, z, c = place()
        self.pushes = []
        for d in range(4):

            def make(order, d=d):
                quarters = out.at[(x + d) % 4], out.at[:, (z + d) % 4]
                piece, lands = cut(quarters[order]), other_cut(quarters[1 - order])
                return Push(piece, piece, sems, device(x, y, z, 1 - c), lands)

            self.pushes.append(Either(c, sems, make))

    def start(self, d):
        self.pushes[d].start()

    def close(self):
        for push in self.pushes:
            push.arrived()
            push.sent()


def turn(values, cosine, sine):
    middle = values.shape[-1] // 2
    leading, trailing = values[:, :middle], values[:, middle:]
    return jnp.concatenate([leading * cosine - trailing * sine, trailing * cosine + leading * sine], axis=1)


def unit_rows(values):
    scale = lax.rsqrt(jnp.mean(values * values, axis=-1, keepdims=True) + EPSILON)
    return values * scale, scale


def allowed_keys(offset, beginning, rows, span):
    query = offset + lax.broadcasted_iota(jnp.int32, (rows, span), 0)
    key = offset + rows - span + lax.broadcasted_iota(jnp.int32, (rows, span), 1)
    return (key <= query) & (key > query - WINDOW) & (key >= beginning)


def gain_row(table, first, each, width):
    lane = lax.broadcasted_iota(jnp.int32, (128, width), 1)
    row = lax.broadcasted_iota(jnp.int32, (128, width), 0)
    owner = (lane * 7282) >> 16 if each == 9 else lane >> 1
    pick = (row == first + lane - owner * each).astype(jnp.float32).astype(jnp.bfloat16)
    spread = dot(table, pick, 1, 0)
    return jnp.sum(jnp.where(row == owner, spread, 0.0), axis=0, keepdims=True)


def lanes_of(start, size):
    return lambda ref: ref.at[(slice(None),) * (len(ref.shape) - 1) + (pl.ds(start, size),)]


def attend(number, stream, doc_starts, own_qkv, own_gains, own_output, own_both, own_down):
    tokens = stream.shape[0]
    span = tokens + WINDOW

    def kernel(
        stream_in, starts_in, qkv_in, gains_in, output_in, both_in, down_in,
        normed_out, query_out, key_out, turned_out, kv_out, probs_out, mixed_out, branch_out, hidden_out, feed_out,
        gains_out, cosine_out, sine_out, qkv_out, output_out, both_out, down_out,
        qkv_box, gains_box, both_box, flat, merge, qkv_own, gains_own, both_own, qkv_all, gains_all, output_all, kv,
        send, recv, here,
    ):
        x, y, z, c = place()
        q, s = lax.axis_index("seq"), lax.axis_index("shard")
        sems = Sems(send, recv)
        after, before = {"seq": (q + 1) % 16, "shard": s}, {"seq": (q + 15) % 16, "shard": s}
        greet(
            [device(x, y + dy, z, (c + dc) % 2) for dy, dc in SHARD_STEPS]
            + [device(x, y, z + 1, c), device(x, y, z + 3, c), device(x + 1, y, z, c), device(x + 3, y, z, c)]
            + [after, before]
        )
        sent = []

        def spread(source, box, pieces=False):
            pushes = []
            for dy, dc in SHARD_STEPS:
                to, back = (y + dy) % 4 * 2 + (c + dc) % 2, (y + 4 - dy) % 4 * 2 + (c + 2 - dc) % 2
                src = source.at[to] if pieces else source
                push = Push(src, box.at[s], sems, device(x, y + dy, z, (c + dc) % 2), box.at[back])
                push.start()
                pushes.append(push)
            box[s] = source[s] if pieces else source[...]
            sent.extend(pushes)
            return pushes

        def collect(pushes, box, own):
            for push in pushes:
                push.arrived()
            tiles = own.shape[-1] // 128
            for d in range(8):
                flat[: 9 * tiles, :] = box[d].astype(jnp.float32)
                for j in range(tiles):
                    merge[9 * d : 9 * d + 9, 128 * j : 128 * (j + 1)] = flat[pl.ds(j, 9, tiles), :]
            own[...] = merge[:, : own.shape[-1]].astype(own.dtype)

        my_lanes = lanes_of(pl.multiple_of(c * 768, 128), 768)
        their_lanes = lanes_of(pl.multiple_of((1 - c) * 768, 128), 768)
        mine = lambda ref: ref.at[(slice(None),) * (len(ref.shape) - 3) + (s,)]

        got_qkv = spread(qkv_in, qkv_box)
        got_gains = spread(gains_in, gains_box)
        down_ring = ring_row(down_in, down_out, whole_ref, sems)
        output_ring = ring_row(output_in, output_all, mine, sems)
        down_ring.first()
        output_ring.first()
        inputs = stream_in[...].astype(jnp.float32)
        unit = unit_rows(inputs)[0]
        starts = starts_in[...]
        positions = q * tokens + lax.broadcasted_iota(jnp.int32, (tokens, 1), 0)
        beginning = jnp.zeros((tokens, 1), jnp.int32)
        for j in range(8):
            start = starts[0:1, j : j + 1]
            beginning = jnp.maximum(beginning, jnp.where(start <= positions, start, 0))
        steps = lax.broadcasted_iota(jnp.int32, (1, HEAD_DIM // 2), 1).astype(jnp.float32)
        angles = (positions - beginning).astype(jnp.float32) * jnp.exp(steps * (-2.0 * math.log(10000.0) / HEAD_DIM))
        cosine_out[...] = jnp.cos(angles)
        sine_out[...] = jnp.sin(angles)

        own = lambda src, dst, at: pltpu.make_async_copy(src, dst, here.at[at])
        collect(got_qkv, qkv_box, qkv_own)
        qkv_ring = ring_row(my_lanes(qkv_own), qkv_all, my_lanes, sems)
        qkv_ring.first()
        got_both = spread(both_in, both_box, True)
        for push in got_gains:
            push.arrived()
        for d in range(8):
            gains_own[d : d + 1, :] = gains_box[d, 0:1, :]
        gains_ring = ring_row(gains_own, gains_all, whole_ref, sems)
        gains_ring.first()
        copies = [
            own(my_lanes(qkv_own), my_lanes(qkv_all.at[x, z]), 0),
            own(gains_own, gains_all.at[x, z], 1),
            own(down_in, down_out.at[x, z], 2),
            own(output_in, output_all.at[x, z, s], 3),
        ]
        for copy in copies:
            copy.start()
        down_ring.relay()
        output_ring.relay()
        qkv_ring.relay()
        gains_ring.relay()
        for copy in copies:
            copy.wait()
        qkv_ring.last()
        gains_ring.last()
        qkv_rest = ring_rest(qkv_all, my_lanes, sems)
        gains_rest = ring_rest(gains_all, whole_ref, sems)
        qkv_cross = Crossing(qkv_all, my_lanes, their_lanes, sems)
        qkv_rest.first()
        gains_rest.first()
        qkv_cross.start(0)
        down_ring.last()
        output_ring.last()
        down_rest = ring_rest(down_out, whole_ref, sems)
        output_rest = ring_rest(output_all, mine, sems)
        output_rest.first()
        down_rest.first()
        collect(got_both, both_box, both_own)
        both_ring = ring_row(both_own, both_out, whole_ref, sems)
        both_ring.first()
        both_copy = own(both_own, both_out.at[x, z], 4)
        both_copy.start()
        qkv_rest.relay()
        gains_rest.relay()
        qkv_cross.start(3)
        qkv_cross.start(1)
        output_rest.relay()
        both_ring.relay()
        down_rest.relay()
        qkv_rest.last()
        gains_rest.last()
        qkv_cross.start(2)
        output_rest.last()
        other = device(x, y, z, 1 - c)
        column = lambda k: output_all.at[:, :, k * 2 + c]
        output_y = RingGather(
            column(y), column, lambda k, h: output_all.at[pl.ds(2 * h, 2), :, k * 2 + c],
            y, lambda k: device(x, k, z, c), sems,
        )
        output_cross = [
            Push(column((y + d) % 4), column((y + d) % 4), sems, other, output_all.at[:, :, (y + d) % 4 * 2 + 1 - c])
            for d in range(4)
        ]
        output_y.first()
        output_cross[0].start()
        both_ring.last()
        both_copy.wait()
        both_rest = ring_rest(both_out, whole_ref, sems)
        table = gains_all[...].reshape(128, 128).astype(jnp.bfloat16)
        for g in range(4):
            gains_out[g : g + 1, :] = gain_row(table, 16 * g, 9, D)
        for g in range(2):
            gains_out[4 + g : 5 + g, :HEAD_DIM] = gain_row(table, 64 + 16 * g, 2, HEAD_DIM)
        qkv_cross.close()

        @pl.loop(0, 8)
        def _(i):
            pair = [qkv_all[i // 2, i % 2 * 2 + k].astype(jnp.float32) for k in range(2)]
            qkv_out[pl.ds(pl.multiple_of(144 * i, 144), 144), :] = jnp.concatenate(pair, axis=0).astype(jnp.bfloat16)

        near = Push(kv.at[2], kv.at[1], sems, after)
        far = Push(kv.at[1], kv.at[0], sems, after)
        normed = (unit * gains_out[0:1, :]).astype(jnp.bfloat16)
        normed_out[...] = normed
        key_value = dot(normed, qkv_out[:, 1024:], 1, 0)
        key = key_value[:, :HEAD_DIM]
        key_out[...] = key
        key_turned = turn(unit_rows(key)[0] * gains_out[5:6, :HEAD_DIM], cosine_out[...], sine_out[...])
        kv[2, :, :HEAD_DIM] = key_turned.astype(jnp.bfloat16)
        kv[2, :, HEAD_DIM:] = key_value[:, HEAD_DIM:].astype(jnp.bfloat16)
        near.start()
        both_rest.first()
        output_y.relay()
        output_cross[1].start()
        output_cross[3].start()
        for h in range(HEADS):
            lanes = slice(h * HEAD_DIM, (h + 1) * HEAD_DIM)
            span_h = slice(h * tokens, (h + 1) * tokens)
            query = dot(normed, qkv_out[:, lanes], 1, 0)
            query_out[span_h, :] = query
            turned = turn(unit_rows(query)[0] * gains_out[4:5, :HEAD_DIM], cosine_out[...], sine_out[...])
            turned_out[span_h, :] = turned.astype(jnp.bfloat16)
        near.arrived()
        far.start()
        output_y.last()
        output_cross[2].start()
        down_rest.last()
        both_rest.relay()
        for push in output_cross:
            push.arrived()

        @pl.loop(0, 16)
        def _(i):
            for j in range(4):
                pair = [output_all[i // 4, i % 4, 2 * j + k].astype(jnp.float32) for k in range(2)]
                rows = pl.ds(pl.multiple_of(64 * i + 16 * j, 16), 16)
                output_out[rows, :] = jnp.concatenate(pair, axis=0).astype(jnp.bfloat16)

        far.arrived()
        kv_out[...] = kv[...].reshape(span, 2 * HEAD_DIM)
        allowed = allowed_keys(q * tokens, beginning, tokens, span)
        keys, values = kv_out[:, :HEAD_DIM], kv_out[:, HEAD_DIM:]
        for h in range(HEADS):
            span_h = slice(h * tokens, (h + 1) * tokens)
            scores = dot(turned_out[span_h, :], keys, 1, 1) * HEAD_DIM ** (-0.5)
            scores = jnp.where(allowed, scores, NEGATIVE)
            exponent = jnp.exp(scores - jnp.max(scores, axis=-1, keepdims=True))
            probs = exponent / jnp.sum(exponent, axis=-1, keepdims=True)
            probs_out[span_h, :] = probs
            mixed_out[:, h * HEAD_DIM : (h + 1) * HEAD_DIM] = dot(probs.astype(jnp.bfloat16), values, 1, 0).astype(
                jnp.bfloat16
            )
        branch = dot(mixed_out[...], output_out[...], 1, 0)
        branch_out[...] = branch
        hidden = inputs + unit_rows(branch)[0] * gains_out[1:2, :]
        hidden_out[...] = hidden
        feed_out[...] = (unit_rows(hidden)[0] * gains_out[2:3, :]).astype(jnp.bfloat16)
        both_rest.last()
        rings = [qkv_ring, gains_ring, down_ring, output_ring, both_ring]
        rings += [qkv_rest, gains_rest, down_rest, output_rest, both_rest, output_y]
        for ring in rings:
            ring.close()
        for push in sent + output_cross + [near, far]:
            push.sent()

    low, wide = jnp.bfloat16, jnp.float32
    outs = [
        ((tokens, D), low),
        ((HEADS * tokens, HEAD_DIM), wide),
        ((tokens, HEAD_DIM), wide),
        ((HEADS * tokens, HEAD_DIM), low),
        ((span, 2 * HEAD_DIM), low),
        ((HEADS * tokens, span), wide),
        ((tokens, HEADS * HEAD_DIM), low),
        ((tokens, D), wide),
        ((tokens, D), wide),
        ((tokens, D), low),
        ((8, D), wide),
        ((tokens, HEAD_DIM // 2), wide),
        ((tokens, HEAD_DIM // 2), wide),
        ((D, 1536), low),
        ((HEADS * HEAD_DIM, D), low),
        ((4, 4, 72, 2 * WIDE), low),
        ((4, 4, PIECE, D), low),
    ]
    scratch = [
        pltpu.VMEM((8, 108, 128), low),
        pltpu.VMEM((8, 8, 128), wide),
        pltpu.VMEM((8, 126, 128), low),
        pltpu.VMEM((128, 128), wide),
        pltpu.VMEM((72, 2 * WIDE), wide),
        pltpu.VMEM((72, 1536), low),
        pltpu.VMEM((8, 128), wide),
        pltpu.VMEM((72, 2 * WIDE), low),
        pltpu.VMEM((4, 4, 72, 1536), low),
        pltpu.VMEM((4, 4, 8, 128), wide),
        pltpu.VMEM((4, 4, 8, 8, D), low),
        pltpu.VMEM((3, tokens, 2 * HEAD_DIM), low),
    ]
    return call(
        kernel, "attend", number, outs, [stream, doc_starts, own_qkv, own_gains, own_output, own_both, own_down],
        scratch, 21 + 10 * 4 + 4 + 4 + 4 + 2, in_specs=[VMEM] * 7, out_specs=[VMEM] * 15 + [ANY] * 2, local=5,
    )


def norm_grad(values, gain, grad):
    unit, scale = unit_rows(values)
    scaled = gain * grad
    return (
        scale * (scaled - unit * jnp.mean(unit * scaled, axis=-1, keepdims=True)),
        jnp.sum(grad * unit, axis=0, keepdims=True),
    )


def scatter_rings(total, boxes, sems):
    x, y, z, c = place()
    z_peer, x_peer = (lambda k: device(x, y, k, c)), (lambda k: device(k, y, z, c))

    def one(order):
        if order == 0:
            chunk, half = lambda k: total.at[:, k], lambda k, h: total.at[pl.ds(2 * h, 2), k]
        else:
            chunk, half = lambda k: total.at[k], lambda k, h: total.at[k, pl.ds(2 * h, 2)]
        return RingSum(chunk, half, boxes[:4], (z, x)[order], (z_peer, x_peer)[order], sems, add_into)

    def two(order):
        chunk = (lambda k: total.at[k, z]) if order == 0 else (lambda k: total.at[x, k])
        half = lambda k, h: split_lanes(chunk(k), h)
        return RingSum(chunk, half, boxes[4:], (x, z)[order], (x_peer, z_peer)[order], sems, add_into)

    return Either(c, sems, one), Either(c, sems, two)


def scatter_boxes(rows, width, kind):
    lanes = lane_halves(width)
    return (
        [pltpu.VMEM((4, 4, rows, width), kind)]
        + [pltpu.VMEM((2, rows, width), kind)] * 2
        + [pltpu.VMEM((4, rows, width), kind)] * 2
        + [pltpu.VMEM((rows, size), kind) for _, size in lanes]
        + [pltpu.VMEM((rows, width), kind)] * 2
    )


BOTH, DOWN, OUTPUT, QUERY, KV = range(5)
SHARED = (OUTPUT, QUERY, KV)
GIVE, TAKE = 9, 10


def attend_back(number, arrays):
    tokens = arrays["hidden"].shape[0]
    span = tokens + WINDOW
    names = list(arrays)
    low, wide = jnp.bfloat16, jnp.float32
    results = dict(
        stream_grad=((tokens, D), low),
        both_rows=((8, 126, 128), low),
        query_grad=((9, 1024), wide),
        key_grad=((9, 256), wide),
        value_grad=((9, 256), wide),
        output_grad=((8, D), wide),
        down_grad=((PIECE, D), wide),
        sums=((8, D), wide),
    )
    sizes = {BOTH: (72, 2 * WIDE), DOWN: (PIECE, D), OUTPUT: (64, 640), QUERY: (72, 512), KV: (72, 256)}
    stores = []
    for name, (rows, width) in sizes.items():
        stores.append(scatter_boxes(rows, width, low))
        if name in SHARED:
            stores[-1] += [pltpu.VMEM((4, 4, rows, width), low)] * 2
    room = SimpleNamespace(
        hidden_grad=pltpu.VMEM((tokens, D), wide),
        branch_low=pltpu.VMEM((tokens, D), low),
        mixed_grad=pltpu.VMEM((HEADS * tokens, HEAD_DIM), low),
        score_low=pltpu.VMEM((HEADS * tokens, span), low),
        probs_low=pltpu.VMEM((HEADS * tokens, span), low),
        kv_grad=pltpu.VMEM((span, 2 * HEAD_DIM), wide),
        halo_out=pltpu.VMEM((2, tokens, 2 * HEAD_DIM), low),
        halo_in=pltpu.VMEM((2, tokens, 2 * HEAD_DIM), low),
        qkv_low=pltpu.VMEM((tokens, 1536), low),
        term=pltpu.VMEM((D, 1024), wide),
        merge=pltpu.VMEM((72, 2 * WIDE), wide),
        flat=pltpu.VMEM((128, 128), wide),
        both_give=pltpu.VMEM((8, 126, 128), low),
        query_give=pltpu.VMEM((8, 36, 128), low),
        query_take=pltpu.VMEM((8, 36, 128), low),
        kv_give=pltpu.VMEM((8, 18, 128), low),
        kv_take=pltpu.VMEM((8, 18, 128), low),
        output_give=pltpu.VMEM((8, 8, 640), low),
        output_take=pltpu.VMEM((8, 8, 640), low),
        own_sums=pltpu.VMEM((3, 8, D), wide),
        shard_sums=pltpu.VMEM((8, 8, D), wide),
        z_sums=pltpu.VMEM((4, 8, D), wide),
        x_sums=pltpu.VMEM((4, 8, D), wide),
    )
    room = vars(room)

    def kernel(*refs):
        refs = list(refs)

        def take(count):
            taken, refs[:] = refs[:count], refs[count:]
            return taken

        a = SimpleNamespace(**dict(zip(names, take(len(names)))))
        o = SimpleNamespace(**dict(zip(results, take(len(results)))))
        b = SimpleNamespace(**dict(zip(room, take(len(room)))))
        held = {n: take(len(store)) for n, store in zip(sizes, stores)}
        send, recv, here = refs
        x, y, z, c = place()
        q, s = lax.axis_index("seq"), lax.axis_index("shard")
        sems = Sems(send, recv)
        other = device(x, y, z, 1 - c)
        after, before = {"seq": (q + 1) % 16, "shard": s}, {"seq": (q + 15) % 16, "shard": s}
        greet(
            [device(x, y + dy, z, (c + dc) % 2) for dy, dc in SHARD_STEPS]
            + [device(x, y, z + d, c) for d in (1, 2, 3)]
            + [device(x + d, y, z, c) for d in (1, 2, 3)]
            + [after, before]
        )
        rings = {n: scatter_rings(held[n][0], held[n][1:9], sems) for n in sizes}
        cross = {n: Push(held[n][GIVE], held[n][TAKE], sems, other) for n in SHARED}
        loads = [
            pltpu.make_async_copy(a.both_term, held[BOTH][0], here.at[0]),
            pltpu.make_async_copy(a.down_term, held[DOWN][0], here.at[1]),
        ]
        for load in loads:
            load.start()
        gains = a.gains
        cosine, sine = a.cosine, a.sine
        own = b.own_sums.at[0]
        own[...] = jnp.zeros(own.shape, wide)
        pending = []

        upstream = a.cotangent[...].astype(wide)
        extra, own[2:3, :] = norm_grad(a.hidden[...], gains[2:3, :], a.feed_grad[...])
        hidden_grad = upstream + extra
        b.hidden_grad[...] = hidden_grad
        branch_grad, own[1:2, :] = norm_grad(a.branch[...], gains[1:2, :], hidden_grad)
        b.branch_low[...] = branch_grad.astype(low)
        own[3:4, :] = a.post_grad[...]
        for at, squares in enumerate((
            jnp.sum(jnp.square(a.stream[...].astype(wide)), axis=0, keepdims=True),
            jnp.sum(jnp.square(a.hidden[...]), axis=0, keepdims=True),
            a.result_squares[...],
        )):
            folded = functools.reduce(jnp.add, [squares[:, 128 * j : 128 * (j + 1)] for j in range(D // 128)])
            own[4:5, 512 + 128 * at : 640 + 128 * at] = folded
        for n, load in zip((BOTH, DOWN), loads):
            load.wait()
            rings[n][0].first()
        for h in range(HEADS):
            rows, lanes = slice(h * tokens, (h + 1) * tokens), slice(h * HEAD_DIM, (h + 1) * HEAD_DIM)
            b.mixed_grad[rows, :] = dot(b.branch_low[...], a.output_weight[lanes, :], 1, 1).astype(low)
        keys, values = a.kv[:, :HEAD_DIM], a.kv[:, HEAD_DIM:]
        for h in range(HEADS):
            rows = slice(h * tokens, (h + 1) * tokens)
            probs = a.probs[rows, :]
            prob_grad = dot(b.mixed_grad[rows, :], values, 1, 1)
            inner = jnp.sum(probs * prob_grad, axis=-1, keepdims=True)
            b.score_low[rows, :] = (probs * (prob_grad - inner) * HEAD_DIM ** (-0.5)).astype(low)
            b.probs_low[rows, :] = probs.astype(low)
        b.kv_grad[:, :HEAD_DIM] = dot(b.score_low[...], a.turned[...], 0, 0)
        b.kv_grad[:, HEAD_DIM:] = dot(b.probs_low[...], b.mixed_grad[...], 0, 0)

        halo_far = Push(b.halo_out.at[0], b.halo_in.at[0], sems, before)
        halo_near = Push(b.halo_out.at[1], b.halo_in.at[1], sems, before)
        b.halo_out[0] = b.kv_grad[:tokens, :].astype(low)
        halo_far.start()

        gain_grad = jnp.zeros((1, HEAD_DIM), wide)
        for h in range(HEADS):
            rows, lanes = slice(h * tokens, (h + 1) * tokens), slice(h * HEAD_DIM, (h + 1) * HEAD_DIM)
            turned_grad = dot(b.score_low[rows, :], keys, 1, 0)
            back = turn(turned_grad, cosine[...], -sine[...])
            grad, extra = norm_grad(a.query[rows, :], gains[4:5, :HEAD_DIM], back)
            gain_grad += extra
            b.qkv_low[:, lanes] = grad.astype(low)
        own[4:5, :HEAD_DIM] = gain_grad

        def term(start, width, give, take):
            out = b.term

            @pl.loop(0, D // 128)
            def _(i):
                lanes = pl.ds(pl.multiple_of(i * 128, 128), 128)
                out[lanes, : 2 * width] = dot(a.normed[:, lanes], b.qkv_low[:, start : start + 2 * width], 0, 0)

            @pl.loop(0, 16)
            def _(i):
                rows = pl.ds(pl.multiple_of(72 * i, 8), 72)
                for ref, core in ((take, c), (give, 1 - c)):
                    lanes = pl.ds(pl.multiple_of(core * width, 128), width)
                    ref[i // 4, i % 4] = out[rows, lanes].astype(low)

        term(0, 512, held[QUERY][GIVE], held[QUERY][0])
        cross[QUERY].start()

        @pl.loop(0, 8)
        def _(i):
            lanes = pl.ds(pl.multiple_of(i * 128, 128), 128)
            part = dot(a.mixed[:, lanes], b.branch_low[...], 0, 0).astype(low)
            for k in range(2):
                block = (2 * i + k) // 4, (2 * i + k) % 4
                for core in range(2):
                    lanes_out = slice(512 * core, 512 * core + 640)
                    value = part[64 * k : 64 * (k + 1), lanes_out]

                    @pl.when(c == core)
                    def _():
                        held[OUTPUT][0][block] = value

                    @pl.when(c != core)
                    def _():
                        held[OUTPUT][GIVE][block] = value

        cross[OUTPUT].start()
        halo_far.arrived()
        b.halo_out[1] = (b.kv_grad[tokens : 2 * tokens, :] + b.halo_in[0].astype(wide)).astype(low)
        halo_near.start()
        for n in (BOTH, DOWN):
            rings[n][0].second()
        for n in (QUERY, OUTPUT):
            cross[n].arrived()
            add_into(held[n][0], held[n][TAKE])
            rings[n][0].first()
        for n in (BOTH, DOWN):
            rings[n][0].third()
            rings[n][1].first()
        halo_near.arrived()
        kv_grad = b.kv_grad[2 * tokens :, :] + b.halo_in[1].astype(wide)
        back = turn(kv_grad[:, :HEAD_DIM], cosine[...], -sine[...])
        grad, own[4:5, HEAD_DIM : 2 * HEAD_DIM] = norm_grad(a.key[...], gains[5:6, :HEAD_DIM], back)
        b.qkv_low[:, 1024:1280] = grad.astype(low)
        b.qkv_low[:, 1280:] = kv_grad[:, HEAD_DIM:].astype(low)
        term(1024, 256, held[KV][GIVE], held[KV][0])
        cross[KV].start()
        for n in (QUERY, OUTPUT):
            rings[n][0].second()
        cross[KV].arrived()
        add_into(held[KV][0], held[KV][TAKE])
        rings[KV][0].first()
        normed_grad = dot(b.qkv_low[...], a.qkv_weight[...], 1, 1)
        extra, own[0:1, :] = norm_grad(a.stream[...].astype(wide), gains[0:1, :], normed_grad)
        o.stream_grad[...] = (b.hidden_grad[...] + extra).astype(low)

        def all_sum(stage, box, me, steps, target):
            source = b.own_sums.at[stage]
            pushes = []
            for to, back in steps:
                push = Push(source, box.at[me], sems, target(to), box.at[back])
                push.start()
                pushes.append(push)
            pending.extend(pushes)
            box[me] = source[...]

            def finish():
                for push in pushes:
                    push.arrived()
                return functools.reduce(jnp.add, [box[k] for k in range(box.shape[0])])

            return finish

        steps = []
        for dy, dc in SHARD_STEPS:
            there = (y + dy) % 4, (c + dc) % 2
            steps.append((there, (y + 4 - dy) % 4 * 2 + (c + 2 - dc) % 2))
        finish = all_sum(0, b.shard_sums, s, steps, lambda t: device(x, t[0], z, t[1]))
        for n in (BOTH, DOWN):
            rings[n][1].second()
        for n in (QUERY, OUTPUT):
            rings[n][0].third()
            rings[n][1].first()
        b.own_sums[1] = finish()
        turns = lambda at: [((at + d) % 4, (at + 4 - d) % 4) for d in (1, 2, 3)]
        finish = all_sum(1, b.z_sums, z, turns(z), lambda t: device(x, y, t, c))
        rings[KV][0].second()

        def spread(source, box):
            pushes = []
            for dy, dc in SHARD_STEPS:
                to, back = (y + dy) % 4 * 2 + (c + dc) % 2, (y + 4 - dy) % 4 * 2 + (c + 2 - dc) % 2
                push = Push(source.at[to], box.at[s], sems, device(x, y + dy, z, (c + dc) % 2), box.at[back])
                push.start()
                pushes.append(push)
            box[s] = source[s]
            pending.extend(pushes)
            return pushes

        def flatten(block, give):
            width = block.shape[-1]
            tiles = width // 128
            merge, flat = b.merge, b.flat
            merge[:, :width] = block[...].astype(wide)
            for d in range(8):
                for j in range(tiles):
                    flat[pl.ds(j, 9, tiles), :] = merge[9 * d : 9 * d + 9, 128 * j : 128 * (j + 1)]
                give[d] = flat[: 9 * tiles, :].astype(low)

        def unflatten(value, tiles, write):
            b.flat[: 9 * tiles, :] = value
            for j in range(tiles):
                write(j, b.flat[pl.ds(j, 9, tiles), :])

        for n in (BOTH, DOWN):
            rings[n][1].third()
        flatten(held[BOTH][0].at[x, z], b.both_give)
        got_both = spread(b.both_give, o.both_rows)
        o.down_grad[...] = held[DOWN][0][x, z].astype(wide)
        b.own_sums[2] = finish()
        finish = all_sum(2, b.x_sums, x, turns(x), lambda t: device(t, y, z, c))
        rings[KV][0].third()
        rings[KV][1].first()
        for n in (QUERY, OUTPUT):
            rings[n][1].second()
        rings[KV][1].second()
        for n in (QUERY, OUTPUT):
            rings[n][1].third()
        flatten(held[QUERY][0].at[x, z], b.query_give)
        got_query = spread(b.query_give, b.query_take)
        for d in range(8):
            b.output_give[d] = held[OUTPUT][0][x, z, 8 * d : 8 * d + 8, :]
        got_output = spread(b.output_give, b.output_take)
        rings[KV][1].third()
        flatten(held[KV][0].at[x, z], b.kv_give)
        got_kv = spread(b.kv_give, b.kv_take)
        o.sums[...] = finish()

        def over_y(box, core):
            return functools.reduce(jnp.add, [box[2 * k + core].astype(wide) for k in range(4)])

        for push in got_query:
            push.arrived()
        for core in range(2):
            def write(j, value, core=core):
                o.query_grad[:, 512 * core + 128 * j : 512 * core + 128 * (j + 1)] = value

            unflatten(over_y(b.query_take, core), 4, write)
        for push in got_output:
            push.arrived()
        o.output_grad[:, :512] = over_y(b.output_take, 0)[:, :512]
        o.output_grad[:, 512:] = over_y(b.output_take, 1)
        for push in got_kv:
            push.arrived()
        for core, out in enumerate((o.key_grad, o.value_grad)):
            def write(j, value, out=out):
                out[:, 128 * j : 128 * (j + 1)] = value

            unflatten(over_y(b.kv_take, core), 2, write)
        for push in got_both:
            push.arrived()
        for pair in rings.values():
            for ring in pair:
                ring.close()
        for push in list(cross.values()) + pending + [halo_far, halo_near]:
            push.sent()

    ins = list(arrays.values())
    out = call(
        kernel, "attend_back", number, list(results.values()), ins, list(room.values()) + sum(stores, []), 5 * 8 + 3 + 2 + 13 + 28,
        in_specs=[VMEM] * (len(ins) - 2) + [ANY] * 2, out_specs=[VMEM] * len(results), local=2,
    )
    return dict(zip(results, out))


def split_hidden(weight):
    parts = weight.reshape(9, 16, 8, PIECE).transpose(2, 0, 1, 3)
    return jnp.pad(parts, ((0, 0), (0, 0), (0, 0), (0, SLOT - PIECE))).reshape(8, 9, WIDE)


def local(
    stream, doc_starts, cotangent, attention_norm, query_weight, key_weight, value_weight, query_norm, key_norm,
    output_weight, attention_post_norm, mlp_norm, gate_weight, up_weight, down_weight, mlp_post_norm,
):
    own_qkv = jnp.concatenate([query_weight, key_weight, value_weight], axis=1)
    norms = (attention_norm, attention_post_norm, mlp_norm, mlp_post_norm, query_norm, key_norm)
    own_gains = jnp.concatenate([jnp.pad(g, (0, 16 - g.shape[0])) for g in norms] + [jnp.zeros((32,), jnp.bfloat16)])
    own_gains = jnp.broadcast_to(own_gains.astype(jnp.float32)[None], (8, 128))
    own_both = jnp.concatenate([split_hidden(gate_weight), split_hidden(up_weight)], axis=2)
    (
        normed, query_proj, key_proj, query_rot, kv, probability, mixed, branch, hidden, feed,
        gain_rows, cosine, sine, full_qkv, full_output, both16, down16,
    ) = attend(
        0, stream[0], doc_starts, own_qkv.reshape(108, 128), own_gains, output_weight, own_both.reshape(8, 126, 128),
        down_weight,
    )
    full_both = both16.reshape(D, 2 * WIDE)
    full_down = jnp.pad(down16.reshape(16, PIECE, D), ((0, 0), (0, SLOT - PIECE), (0, 0))).reshape(WIDE, D)

    block_output, feed_grad, gain_mlp_post_grad, result_squares, both_term, down_term = feed_forward(
        "feed_forward", 1, feed, full_both, full_down, hidden, cotangent[0], gain_rows[3:4]
    )

    back = SimpleNamespace(**attend_back(
        2,
        dict(
            feed_grad=feed_grad, hidden=hidden, branch=branch, cotangent=cotangent[0], stream=stream[0],
            normed=normed, query=query_proj, key=key_proj, turned=query_rot, kv=kv, probs=probability, mixed=mixed,
            gains=gain_rows, cosine=cosine, sine=sine, qkv_weight=full_qkv, output_weight=full_output,
            post_grad=gain_mlp_post_grad, result_squares=result_squares,
            both_term=both_term.reshape(4, 4, 72, 2 * WIDE),
            down_term=down_term.reshape(16, SLOT, D)[:, :PIECE].reshape(4, 4, PIECE, D),
        ),
    ))

    def whole(rows):
        parts = rows.reshape(8, 9, 16, SLOT)[..., :PIECE]
        return parts.transpose(1, 2, 0, 3).reshape(9, FF).astype(jnp.float32)

    both_rows = back.both_rows.reshape(8, 9, 2 * WIDE)
    sums = back.sums
    own = lax.axis_index("seq") * 8 + lax.axis_index("shard")
    gain_grads = lax.dynamic_slice_in_dim(sums[:4], own * 9, 9, 1)
    query_gain_grad = lax.dynamic_slice_in_dim(sums[4, :HEAD_DIM], own * 2, 2, 0)
    key_gain_grad = lax.dynamic_slice_in_dim(sums[4, HEAD_DIM : 2 * HEAD_DIM], own * 2, 2, 0)
    stream_rms = jnp.sqrt(jnp.sum(sums[4, 512:896].reshape(3, 128), axis=1) / (32768 * D))
    return (
        block_output[None],
        back.stream_grad[None],
        gain_grads[0],
        back.query_grad,
        back.key_grad,
        back.value_grad,
        query_gain_grad,
        key_gain_grad,
        back.output_grad,
        gain_grads[1],
        gain_grads[2],
        whole(both_rows[:, :, :WIDE]),
        whole(both_rows[:, :, WIDE:]),
        back.down_grad,
        gain_grads[3],
        stream_rms,
    )


def solution(mesh):
    rows = P(("seq", "shard"))
    tokens = P("shard", "seq", None)
    table = P(("seq", "shard"), None)
    return jax.shard_map(
        local,
        mesh=mesh,
        in_specs=(
            tokens, P("shard", None), tokens, rows, table, table, table, rows, rows, table, rows, rows, table, table,
            table, rows,
        ),
        out_specs=(
            tokens, tokens, rows, table, table, table, rows, rows, table, rows, rows, table, table, table, rows, P(),
        ),
        check_vma=False,
    )
```

```python
import functools
import math
from types import SimpleNamespace

import jax
import jax.numpy as jnp
from jax import lax
from jax.experimental import pallas as pl
from jax.experimental.pallas import tpu as pltpu
from jax.sharding import PartitionSpec as P

D = 1152
HEADS = 4
HEAD_DIM = 256
WINDOW = 512
FF = 6912
PIECE = 54
SLOT = 56
WIDE = 16 * SLOT

EPSILON = 1e-06
NEGATIVE = -1e30
MESH = pl.DeviceIdType.MESH
MIB = 2**20


def place():
    q, s = lax.axis_index("seq"), lax.axis_index("shard")
    return q // 4, s // 2, q % 4, s % 2


def device(x, y, z, c):
    return {"seq": x % 4 * 4 + z % 4, "shard": y % 4 * 2 + c}


def greet(targets):
    barrier = pltpu.get_barrier_semaphore()
    for target in targets:
        pl.semaphore_signal(barrier, inc=1, device_id=target, device_id_type=MESH)
    pl.semaphore_wait(barrier, len(targets))


class Sems:
    def __init__(self, send, recv):
        self.send, self.recv, self.used = send, recv, 0

    def take(self):
        self.used += 1
        return self.send.at[self.used - 1], self.recv.at[self.used - 1]


class Push:
    def __init__(self, src, dst, sems, to, lands=None):
        send, recv = sems.take()
        self.out = pltpu.make_async_remote_copy(
            src_ref=src, dst_ref=dst, send_sem=send, recv_sem=recv, device_id=to, device_id_type=MESH
        )
        lands = dst if lands is None else lands
        self.back = pltpu.make_async_remote_copy(
            src_ref=lands, dst_ref=lands, send_sem=send, recv_sem=recv, device_id=to, device_id_type=MESH
        )

    def start(self):
        self.out.start()

    def arrived(self):
        self.back.wait_recv()

    def sent(self):
        self.out.wait_send()


class RingGather:
    def __init__(self, own, slot, half, me, peer, sems):
        up, down, far = (me + 1) % 4, (me + 3) % 4, (me + 2) % 4
        self.right = Push(own, slot(me), sems, peer(up), slot(down))
        self.left = Push(own, slot(me), sems, peer(down), slot(up))
        split = half(down, 0)
        self.right2 = None if split is None else Push(split, split, sems, peer(up), half(far, 0))
        split = half(up, 1)
        self.left2 = None if split is None else Push(split, split, sems, peer(down), half(far, 1))

    def first(self):
        self.right.start()
        self.left.start()

    def relay(self):
        self.right.arrived()
        if self.right2 is not None:
            self.right2.start()
        self.left.arrived()
        if self.left2 is not None:
            self.left2.start()

    def last(self):
        if self.right2 is not None:
            self.right2.arrived()
        if self.left2 is not None:
            self.left2.arrived()

    def close(self):
        for push in (self.right, self.left, self.right2, self.left2):
            if push is not None:
                push.sent()


class RingSum:
    def __init__(self, chunk, half, inbox, me, peer, sems, add):
        up, down, far = (me + 1) % 4, (me + 3) % 4, (me + 2) % 4
        self.chunk, self.half, self.inbox, self.add = chunk, half, inbox, add
        self.me, self.up, self.down = me, up, down
        near_a, near_b, right, left = inbox
        self.far_a = Push(half(far, 0), near_a, sems, peer(up))
        split = half(far, 1)
        self.far_b = None if split is None else Push(split, near_b, sems, peer(down))
        self.right = Push(chunk(up), right, sems, peer(up))
        self.left = Push(chunk(down), left, sems, peer(down))

    def first(self):
        self.far_a.start()
        if self.far_b is not None:
            self.far_b.start()

    def second(self):
        self.far_a.arrived()
        self.add(self.half(self.up, 0), self.inbox[0])
        self.right.start()
        if self.far_b is not None:
            self.far_b.arrived()
            self.add(self.half(self.down, 1), self.inbox[1])
        self.left.start()

    def third(self):
        self.right.arrived()
        self.add(self.chunk(self.me), self.inbox[2])
        self.left.arrived()
        self.add(self.chunk(self.me), self.inbox[3])

    def close(self):
        for push in (self.far_a, self.far_b, self.right, self.left):
            if push is not None:
                push.sent()


def add_into(total, extra):
    if len(total.shape) == 2:
        summed = total[...].astype(jnp.float32) + extra[...].astype(jnp.float32)
        total[...] = summed.astype(total.dtype)
        return

    @pl.loop(0, total.shape[0])
    def _(step):
        add_into(total.at[step], extra.at[step])


ANY = pl.BlockSpec(memory_space=pl.ANY)
VMEM = pl.BlockSpec(memory_space=pltpu.VMEM)


def call(kernel, name, number, outs, ins, scratch, copies, in_specs=None, out_specs=None, local=0, aliases=None):
    outs = [jax.ShapeDtypeStruct(shape, dtype) for shape, dtype in outs]
    scratch = list(scratch) + [pltpu.SemaphoreType.DMA((copies,)), pltpu.SemaphoreType.DMA((copies,))]
    if local:
        scratch.append(pltpu.SemaphoreType.DMA((local,)))
    return pl.pallas_call(
        kernel,
        name=name,
        out_shape=outs,
        in_specs=in_specs or [ANY] * len(ins),
        out_specs=out_specs or [ANY] * len(outs),
        scratch_shapes=scratch,
        input_output_aliases=aliases or {},
        compiler_params=pltpu.CompilerParams(
            collective_id=number, has_side_effects=True, vmem_limit_bytes=60 * MIB
        ),
    )(*ins)


SHARD_STEPS = [(dy, dc) for dy in range(4) for dc in range(2) if dy or dc]


def lane_halves(width):
    low = width // 256 * 128 if width % 256 == 0 else (width // 128 + 1) // 2 * 128
    return ((0, low), (low, width - low)) if width > 128 else ((0, width), None)


def dot(a, b, contract_a, contract_b):
    return lax.dot_general(a, b, (((contract_a,), (contract_b,)), ((), ())), preferred_element_type=jnp.float32)


SUBS = 2
BACK = (0, 1, 3, 2)


def gelu_terms(gate):
    a, b = math.sqrt(2.0 / math.pi), 0.044715
    square = gate * gate
    bend = jnp.tanh(a * gate * (1.0 + b * square))
    half = 0.5 * (1.0 + bend)
    slope = half + 0.5 * gate * (1.0 - bend * bend) * a * (1.0 + 3.0 * b * square)
    return gate * half, slope


def feed_forward(number, feed, feeds_a, full_both, down16, hidden, cotangent, gains):
    tokens, width = feed.shape
    rows = tokens // SUBS
    half = rows // 2

    def kernel(
        feed_in, feeds_in, both_in, down_in, hidden_in, cotangent_in, gains_in,
        block_out, feed_out, gain_out, square_out, both_out, down_out,
        feeds, downs, both, active, part, inbox, near, right, left, w_both, w_down, raw, pad, both_term, down_term,
        send, recv, here,
    ):
        x, y, z, c = place()
        sems = Sems(send, recv)
        other = device(x, y, z, 1 - c)
        to = lambda d: device(x, y + d, z, c)
        span = lambda s: pl.ds(s * rows, rows)
        a, b = 0, 1
        loads = [
            pltpu.make_async_copy(feeds_in, feeds.at[a], here.at[0]),
            pltpu.make_async_copy(both_in, w_both, here.at[1]),
            pltpu.make_async_copy(down_in, raw, here.at[2]),
            pltpu.make_async_copy(feed_in.at[span(b)], feeds.at[b, y * 2 + c], here.at[3]),
        ]
        for load in loads:
            load.start()
        greet([to(1), to(3), other])

        def gather(source, blocks, s):
            slot = lambda k: blocks.at[s, k * 2 + c]
            ring = RingGather(
                source, slot, lambda k, h: blocks.at[s, k * 2 + c, pl.ds(h * half, half)],
                y, lambda k: device(x, k, z, c), sems,
            )
            cross = []
            for d in range(4):
                k = (y + d) % 4
                cross.append(
                    Push(source if d == 0 else slot(k), slot(k), sems, other, blocks.at[s, k * 2 + 1 - c])
                )

            def first():
                ring.first()
                cross[0].start()

            def relay():
                ring.relay()
                cross[1].start()
                cross[3].start()

            def last():
                ring.last()
                cross[2].start()

            def close():
                ring.close()
                for push in cross:
                    push.sent()

            return first, relay, last, [push.arrived for push in cross], close

        class Total:
            def __init__(self, s):
                self.s = s
                self.cross = {}
                for d in range(4):
                    k = (y + d) % 4
                    self.cross[d] = Push(part.at[s, k * 2 + 1 - c], inbox.at[s, d], sems, other)
                self.own = lambda d: part.at[s, (y + d) % 4 * 2 + c]
                self.far_a = Push(self.own(2).at[pl.ds(0, half)], near.at[s, 0], sems, to(1))
                self.far_b = Push(self.own(2).at[pl.ds(half, half)], near.at[s, 1], sems, to(3))
                self.right = Push(self.own(1), right.at[s], sems, to(1))
                self.left = Push(self.own(3), left.at[s], sems, to(3))

            def far(self):
                self.cross[2].arrived()
                add_into(self.own(2), inbox.at[self.s, 2])
                self.far_a.start()
                self.far_b.start()

            def sides(self):
                for d in (1, 3):
                    self.cross[d].arrived()
                    add_into(self.own(d), inbox.at[self.s, d])

            def go(self):
                self.far_a.arrived()
                add_into(self.own(1).at[pl.ds(0, half)], near.at[self.s, 0])
                self.right.start()
                self.far_b.arrived()
                add_into(self.own(3).at[pl.ds(half, half)], near.at[self.s, 1])
                self.left.start()

            def final(self):
                self.cross[0].arrived()
                self.right.arrived()
                self.left.arrived()
                s = self.s
                pieces = (self.own(0), inbox.at[s, 0], right.at[s], left.at[s])
                return functools.reduce(jnp.add, [p[...].astype(jnp.float32) for p in pieces])

            def close(self):
                for push in list(self.cross.values()) + [self.far_a, self.far_b, self.right, self.left]:
                    push.sent()

        def steps(body, before, totals):
            @pl.loop(0, 4 * SUBS)
            def _(t):
                for at, hook in before.items():
                    pl.when(t == at)(hook)
                s, i = t // 4, t % 4
                d = i + i // 2 - i // 3 * 2
                body(s, pl.ds((y + d) % 4 * 2, 2))
                for at in range(4 * SUBS):
                    push = totals[at // 4].cross[BACK[at % 4]]
                    pl.when(t == at)(push.start)

        def flat(value):
            return value.reshape(2 * rows, value.shape[-1])

        def pair(value):
            return value.reshape(2, rows, value.shape[-1])

        def forward(s, chip):
            sums = dot(flat(feeds[s, chip]), w_both[...], 1, 0)
            both[s, chip] = pair(sums.astype(jnp.bfloat16))
            bent, _ = gelu_terms(sums[:, :WIDE])
            low = (bent * sums[:, WIDE:]).astype(jnp.bfloat16)
            active[s, chip] = pair(low)
            part[s, chip] = pair(dot(low, w_down[...], 1, 0).astype(jnp.bfloat16))

        def backward(s, chip):
            grad = dot(flat(downs[s, chip]), w_down[...], 1, 1)
            sums = flat(both[s, chip]).astype(jnp.float32)
            bent, slope = gelu_terms(sums[:, :WIDE])
            gate_grad = (grad * sums[:, WIDE:] * slope).astype(jnp.bfloat16)
            up_grad = (grad * bent).astype(jnp.bfloat16)
            both[s, chip, :, :WIDE] = pair(gate_grad)
            both[s, chip, :, WIDE:] = pair(up_grad)
            part[s, chip] = pair(dot(flat(both[s, chip]), w_both[...], 1, 1).astype(jnp.bfloat16))

        gain_out[...] = jnp.zeros_like(gain_out)
        square_out[...] = jnp.zeros_like(square_out)

        def norm_back(total, s):
            down = total.final()
            gain_row = gains_in[3:4, :]
            upstream = cotangent_in[span(s), :].astype(jnp.float32)
            scale = lax.rsqrt(jnp.mean(down * down, axis=-1, keepdims=True) + EPSILON)
            unit = down * scale
            result = hidden_in[span(s), :] + unit * gain_row
            block_out[span(s), :] = result.astype(jnp.bfloat16)
            square_out[...] += jnp.sum(result * result, axis=0, keepdims=True)
            gain_out[...] += jnp.sum(upstream * unit, axis=0, keepdims=True)
            scaled = gain_row * upstream
            grad = scale * (scaled - unit * jnp.mean(unit * scaled, axis=-1, keepdims=True))
            downs[s, y * 2 + c] = grad.astype(jnp.bfloat16)

        first_b, relay_b, last_b, met_b, close_b = gather(feed_in.at[span(b)], feeds, b)
        sum_a, sum_b = Total(a), Total(b)
        first_b()
        pad[...] = jnp.zeros_like(pad)
        for load in loads:
            load.wait()

        @pl.loop(0, 8)
        def _(i):
            for k in range(2):
                pad[SLOT * k : SLOT * k + PIECE, :] = raw[i // 2, i % 2 * 2 + k].astype(jnp.float32)
            w_down[pl.ds(pl.multiple_of(2 * SLOT * i, 16), 2 * SLOT), :] = pad[...].astype(jnp.bfloat16)

        def at_4():
            sum_a.far()
            met_b[0]()

        def at_5():
            last_b()
            sum_a.sides()
            met_b[1]()

        def at_6():
            sum_a.go()
            met_b[3]()

        steps(forward, {3: relay_b, 4: at_4, 5: at_5, 6: at_6, 7: met_b[2]}, (sum_a, sum_b))
        sum_b.far()
        norm_back(sum_a, a)
        sum_a.close()
        first_a, relay_a, last_a, met_a, close_a = gather(downs.at[a, y * 2 + c], downs, a)
        first_a()
        sum_b.sides()
        sum_b.go()
        old_b, old_close_b = sum_b, close_b
        first_b, relay_b, last_b, met_b, close_b = gather(downs.at[b, y * 2 + c], downs, b)
        sum_a, sum_b = Total(a), Total(b)

        def down_terms(s):
            every = 8 * rows

            @pl.loop(0, WIDE // 128)
            def _(i):
                units = pl.ds(pl.multiple_of(i * 128, 128), 128)
                value = dot(active[s, :, :, units].reshape(every, 128), downs[s].reshape(every, width), 0, 0)
                if s == b:
                    value += down_term[units, :].astype(jnp.float32)
                down_term[units, :] = value.astype(jnp.bfloat16)

        def both_terms(s):
            every = 8 * rows

            @pl.loop(0, width // 128)
            def _(i):
                lanes = pl.ds(pl.multiple_of(i * 128, 128), 128)
                value = dot(feeds[s, :, :, lanes].reshape(every, 128), both[s].reshape(every, 2 * WIDE), 0, 0)
                if s == b:
                    value += both_term[lanes, :].astype(jnp.float32)
                both_term[lanes, :] = value.astype(jnp.bfloat16)

        def back_1():
            relay_a()
            met_a[1]()

        def back_2():
            last_a()
            met_a[3]()

        def back_4():
            norm_back(old_b, b)
            old_b.close()
            old_close_b()
            first_b()
            sum_a.far()
            met_b[0]()

        def back_5():
            down_terms(a)
            sum_a.sides()
            relay_b()
            both_terms(a)
            sum_a.go()
            last_b()
            met_b[1]()

        steps(
            backward,
            {0: met_a[0], 1: back_1, 2: back_2, 3: met_a[2], 4: back_4, 5: back_5, 6: met_b[3], 7: met_b[2]},
            (sum_a, sum_b),
        )
        sum_b.far()
        sum_b.sides()
        down_terms(b)
        saves = [
            pltpu.make_async_copy(down_term, down_out, here.at[0]),
            pltpu.make_async_copy(both_term, both_out, here.at[1]),
        ]
        saves[0].start()
        sum_b.go()
        feed_out[span(a), :] = sum_a.final()
        both_terms(b)
        saves[1].start()
        feed_out[span(b), :] = sum_b.final()
        sum_a.close()
        sum_b.close()
        close_a()
        close_b()
        for save in saves:
            save.wait()

    low, wide = jnp.bfloat16, jnp.float32
    blocks = (SUBS, 8, rows)
    scratch = [
        pltpu.VMEM(blocks + (width,), low),
        pltpu.VMEM(blocks + (width,), low),
        pltpu.VMEM(blocks + (2 * WIDE,), low),
        pltpu.VMEM(blocks + (WIDE,), low),
        pltpu.VMEM(blocks + (width,), low),
        pltpu.VMEM((SUBS, 4, rows, width), low),
        pltpu.VMEM((SUBS, 2, half, width), low),
        pltpu.VMEM((SUBS, rows, width), low),
        pltpu.VMEM((SUBS, rows, width), low),
        pltpu.VMEM((width, 2 * WIDE), low),
        pltpu.VMEM((WIDE, width), low),
        pltpu.VMEM((4, 4, PIECE, width), low),
        pltpu.VMEM((2 * SLOT, width), wide),
        pltpu.VMEM((width, 2 * WIDE), low),
        pltpu.VMEM((WIDE, width), low),
    ]
    outs = [
        ((tokens, width), low),
        ((tokens, width), wide),
        ((1, width), wide),
        ((1, width), wide),
        ((width, 2 * WIDE), low),
        ((WIDE, width), low),
    ]
    return call(
        kernel, "feed_forward", number, outs, [feed, feeds_a, full_both, down16, hidden, cotangent, gains], scratch,
        32 * SUBS - 8, in_specs=[ANY] * 4 + [VMEM] * 3, out_specs=[VMEM] * 4 + [ANY] * 2, local=4,
    )


class Either:
    def __init__(self, core, sems, make):
        self.core, start, most = core, sems.used, 0
        self.variants = []
        for order in (0, 1):
            sems.used = start
            self.variants.append(make(order))
            most = max(most, sems.used)
        sems.used = most

    def __getattr__(self, name):
        def run():
            for order in (0, 1):
                pl.when(self.core == order)(getattr(self.variants[order], name))

        return run


def split_lanes(ref, h):
    halves = lane_halves(ref.shape[-1])
    return None if halves[h] is None else ref.at[:, pl.ds(*halves[h])]


def whole_ref(ref):
    return ref


def ring_row(own, out, cut, sems):
    x, y, z, c = place()

    def make(order):
        slot = (lambda k: cut(out.at[x, k])) if order == 0 else (lambda k: cut(out.at[k, z]))
        peer = (lambda k: device(x, y, k, c)) if order == 0 else (lambda k: device(k, y, z, c))
        return RingGather(own, slot, lambda k, h: split_lanes(slot(k), h), (z, x)[order], peer, sems)

    return Either(c, sems, make)


def ring_rest(out, cut, sems, lean=False):
    x, y, z, c = place()

    def make(order):
        if order == 0:
            slot, half, me = lambda k: cut(out.at[k]), lambda k, h: cut(out.at[k, pl.ds(2 * h, 2)]), x
        else:
            slot, half, me = lambda k: cut(out.at[:, k]), lambda k, h: cut(out.at[pl.ds(2 * h, 2), k]), z
            if lean:
                half = lambda k, h: slot(k) if h else None
        peer = (lambda k: device(k, y, z, c)) if order == 0 else (lambda k: device(x, y, k, c))
        return RingGather(slot(me), slot, half, me, peer, sems)

    return Either(c, sems, make)


class Crossing:
    def __init__(self, out, cut, other_cut, sems):
        x, y, z, c = place()
        self.pushes = []
        for d in range(4):

            def make(order, d=d):
                quarters = out.at[(x + d) % 4], out.at[:, (z + d) % 4]
                piece, lands = cut(quarters[order]), other_cut(quarters[1 - order])
                return Push(piece, piece, sems, device(x, y, z, 1 - c), lands)

            self.pushes.append(Either(c, sems, make))

    def start(self, d):
        self.pushes[d].start()

    def close(self):
        for push in self.pushes:
            push.arrived()
            push.sent()


def turn(values, cosine, sine):
    middle = values.shape[-1] // 2
    leading, trailing = values[:, :middle], values[:, middle:]
    return jnp.concatenate([leading * cosine - trailing * sine, trailing * cosine + leading * sine], axis=1)


def unit_rows(values):
    scale = lax.rsqrt(jnp.mean(values * values, axis=-1, keepdims=True) + EPSILON)
    return values * scale, scale


def allowed_keys(offset, beginning, rows, span):
    query = offset + lax.broadcasted_iota(jnp.int32, (rows, span), 0)
    key = offset + rows - span + lax.broadcasted_iota(jnp.int32, (rows, span), 1)
    return (key <= query) & (key > query - WINDOW) & (key >= beginning)


def gain_picks(each, width):
    lane = lax.broadcasted_iota(jnp.int32, (16, width), 1)
    owner = (lane * 7282) >> 16 if each == 9 else lane >> 1
    pick = lax.broadcasted_iota(jnp.int32, (16, width), 0) == lane - owner * each
    lane = lax.broadcasted_iota(jnp.int32, (128, width), 1)
    owner = (lane * 7282) >> 16 if each == 9 else lane >> 1
    owns = lax.broadcasted_iota(jnp.int32, (128, width), 0) == owner
    return pick.astype(jnp.float32).astype(jnp.bfloat16), owns.astype(jnp.float32)


def gain_row(table, first, pick, owns):
    spread = dot(table[:, first : first + 16], pick, 1, 0)
    return jnp.sum(spread * owns, axis=0, keepdims=True)


def lanes_of(start, size):
    return lambda ref: ref.at[(slice(None),) * (len(ref.shape) - 1) + (pl.ds(start, size),)]


def attend(number, stream, doc_starts, own_query, own_kv, own_output, own_both, own_down):
    tokens = stream.shape[0]
    span = tokens + WINDOW

    low, wide = jnp.bfloat16, jnp.float32
    keep = dict(
        normed=((tokens, D), low),
        query=((HEADS * tokens, HEAD_DIM), wide),
        key=((tokens, HEAD_DIM), wide),
        turned=((HEADS * tokens, HEAD_DIM), low),
        kv=((span, 2 * HEAD_DIM), low),
        probs=((HEADS * tokens, span), wide),
        mixed=((tokens, HEADS * HEAD_DIM), low),
        branch=((tokens, D), wide),
        hidden=((tokens, D), wide),
        feed=((tokens, D), low),
        gains=((8, D), wide),
        cosine=((tokens, HEAD_DIM // 2), wide),
        sine=((tokens, HEAD_DIM // 2), wide),
        qkv_weight=((D, 1536), low),
        output_weight=((HEADS * HEAD_DIM, D), low),
    )

    def kernel(
        stream_in, starts_in, query_in, kv_in, output_in, both_in, down_in, *refs
    ):
        refs = list(refs)

        def take(count):
            taken, refs[:] = refs[:count], refs[count:]
            return taken

        saved = SimpleNamespace(**dict(zip(keep, take(len(keep)))))
        both_out, down_out, feeds_out = take(3)
        v = SimpleNamespace(**dict(zip(keep, take(len(keep)))))
        (
            query_box, kv_box, both_box, flat, merge, query_own, kv_own, both_own, query_all, kv_all, output_all, kv,
            owns9, owns2,
            send, recv, here,
        ) = refs
        saves = []

        def save(src, dst):
            saves.append(pltpu.make_async_copy(src, dst, here.at[5 + len(saves)]))
            saves[-1].start()

        x, y, z, c = place()
        q, s = lax.axis_index("seq"), lax.axis_index("shard")
        sems = Sems(send, recv)
        after, before = {"seq": (q + 1) % 16, "shard": s}, {"seq": (q + 15) % 16, "shard": s}
        greet(
            [device(x, y + dy, z, (c + dc) % 2) for dy, dc in SHARD_STEPS]
            + [device(x, y, z + 1, c), device(x, y, z + 3, c), device(x + 1, y, z, c), device(x + 3, y, z, c)]
            + [after, before]
        )
        sent = []

        def spread(source, box, pieces=False):
            pushes = []
            for dy, dc in SHARD_STEPS:
                to, back = (y + dy) % 4 * 2 + (c + dc) % 2, (y + 4 - dy) % 4 * 2 + (c + 2 - dc) % 2
                src = source.at[to] if pieces else source
                push = Push(src, box.at[s], sems, device(x, y + dy, z, (c + dc) % 2), box.at[back])
                push.start()
                pushes.append(push)
            box[s] = source[s] if pieces else source[...]
            sent.extend(pushes)
            return pushes

        def collect(pushes, box, own):
            for push in pushes:
                push.arrived()
            tiles = own.shape[-1] // 128
            for d in range(8):
                flat[: box.shape[1], :] = box[d].astype(jnp.float32)
                for j in range(tiles):
                    merge[9 * d : 9 * d + 9, 128 * j : 128 * (j + 1)] = flat[pl.ds(j, 9, tiles), :]
                if box.shape[1] > 9 * tiles:
                    for start in (0, 256):
                        merge[72 + d : 73 + d, start : start + 128] = flat[9 * tiles : 9 * tiles + 1, :]
            own[...] = merge[: own.shape[0], : own.shape[-1]].astype(own.dtype)

        def halves(size):
            return [lanes_of(pl.multiple_of(core * size, 128), size) for core in (c, 1 - c)]

        my_query, their_query = halves(512)
        my_kv, their_kv = halves(256)
        mine = lambda ref: ref.at[(slice(None),) * (len(ref.shape) - 3) + (s,)]

        got_kv = spread(kv_in, kv_box)
        got_query = spread(query_in, query_box)
        down_ring = ring_row(down_in, down_out, whole_ref, sems)
        output_ring = ring_row(output_in, output_all, mine, sems)
        down_ring.first()
        output_ring.first()
        inputs = stream_in[...].astype(jnp.float32)
        unit = unit_rows(inputs)[0]
        starts = starts_in[...]
        positions = q * tokens + lax.broadcasted_iota(jnp.int32, (tokens, 1), 0)
        beginning = jnp.zeros((tokens, 1), jnp.int32)
        for j in range(8):
            start = starts[0:1, j : j + 1]
            beginning = jnp.maximum(beginning, jnp.where(start <= positions, start, 0))
        steps = lax.broadcasted_iota(jnp.int32, (1, HEAD_DIM // 2), 1).astype(jnp.float32)
        angles = (positions - beginning).astype(jnp.float32) * jnp.exp(steps * (-2.0 * math.log(10000.0) / HEAD_DIM))
        v.cosine[...] = jnp.cos(angles)
        v.sine[...] = jnp.sin(angles)
        pick9, owns9[...] = gain_picks(9, D)
        pick2, owns2[...] = gain_picks(2, HEAD_DIM)
        v.gains[...] = jnp.zeros_like(v.gains)
        merge[72:80, :] = jnp.zeros((8, merge.shape[1]), jnp.float32)

        own = lambda src, dst, at: pltpu.make_async_copy(src, dst, here.at[at])
        collect(got_kv, kv_box, kv_own)
        kv_ring = ring_row(my_kv(kv_own), kv_all, my_kv, sems)
        kv_ring.first()
        collect(got_query, query_box, query_own)
        query_ring = ring_row(my_query(query_own), query_all, my_query, sems)
        query_ring.first()
        got_both = spread(both_in, both_box, True)
        copies = [
            own(my_kv(kv_own), my_kv(kv_all.at[x, z]), 0),
            own(down_in, down_out.at[x, z], 1),
            own(output_in, output_all.at[x, z, s], 2),
            own(my_query(query_own), my_query(query_all.at[x, z]), 3),
        ]
        for copy in copies:
            copy.start()
        down_ring.relay()
        output_ring.relay()
        kv_ring.relay()
        query_ring.relay()
        for copy in copies:
            copy.wait()
        kv_ring.last()
        kv_rest = ring_rest(kv_all, my_kv, sems)
        kv_cross = Crossing(kv_all, my_kv, their_kv, sems)
        kv_rest.first()
        kv_cross.start(0)
        query_ring.last()
        query_rest = ring_rest(query_all, my_query, sems)
        query_cross = Crossing(query_all, my_query, their_query, sems)
        query_rest.first()
        query_cross.start(0)
        down_ring.last()
        output_ring.last()
        down_rest = ring_rest(down_out, whole_ref, sems, True)
        output_rest = ring_rest(output_all, mine, sems)
        kv_rest.relay()
        kv_cross.start(3)
        kv_cross.start(1)
        output_rest.first()
        collect(got_both, both_box, both_own)
        both_ring = ring_row(both_own, both_out, whole_ref, sems)
        both_ring.first()
        both_copy = own(both_own, both_out.at[x, z], 4)
        both_copy.start()
        kv_rest.last()
        kv_cross.start(2)
        query_rest.relay()
        query_cross.start(3)
        query_cross.start(1)
        output_rest.relay()
        down_rest.first()
        table = kv_all[:, :, 72:80, pl.ds(pl.multiple_of(c * 256, 128), 128)].reshape(128, 128)
        for g in range(4):
            v.gains[g : g + 1, :] = gain_row(table, 16 * g, pick9, owns9[...])
        for g in range(2):
            v.gains[4 + g : 5 + g, :HEAD_DIM] = gain_row(table, 64 + 16 * g, pick2, owns2[...])
        normed = (unit * v.gains[0:1, :]).astype(jnp.bfloat16)
        v.normed[...] = normed

        def assemble(blocks, lanes):
            @pl.loop(0, 8)
            def _(i):
                pair = [blocks[i // 2, i % 2 * 2 + k, :72].astype(jnp.float32) for k in range(2)]
                rows = pl.ds(pl.multiple_of(144 * i, 144), 144)
                v.qkv_weight[rows, lanes] = jnp.concatenate(pair, axis=0).astype(jnp.bfloat16)

        kv_cross.close()
        assemble(kv_all, slice(1024, 1536))

        near = Push(kv.at[2], kv.at[1], sems, after)
        far = Push(kv.at[1], kv.at[0], sems, after)
        key_value = dot(normed, v.qkv_weight[:, 1024:], 1, 0)
        key = key_value[:, :HEAD_DIM]
        v.key[...] = key
        key_turned = turn(unit_rows(key)[0] * v.gains[5:6, :HEAD_DIM], v.cosine[...], v.sine[...])
        kv[2, :, :HEAD_DIM] = key_turned.astype(jnp.bfloat16)
        kv[2, :, HEAD_DIM:] = key_value[:, HEAD_DIM:].astype(jnp.bfloat16)
        near.start()
        query_rest.last()
        query_cross.start(2)
        both_ring.relay()
        output_rest.last()
        other = device(x, y, z, 1 - c)
        column = lambda k: output_all.at[:, :, k * 2 + c]
        output_y = RingGather(
            column(y), column, lambda k, h: output_all.at[pl.ds(2 * h, 2), :, k * 2 + c],
            y, lambda k: device(x, k, z, c), sems,
        )
        output_cross = [
            Push(column((y + d) % 4), column((y + d) % 4), sems, other, output_all.at[:, :, (y + d) % 4 * 2 + 1 - c])
            for d in range(4)
        ]
        output_y.first()
        output_cross[0].start()
        for src, dst in ((v.gains, saved.gains), (v.cosine, saved.cosine), (v.sine, saved.sine)):
            save(src, dst)
        query_cross.close()
        assemble(query_all, slice(0, 1024))
        save(v.qkv_weight, saved.qkv_weight)
        both_ring.last()
        both_copy.wait()
        both_rest = ring_rest(both_out, whole_ref, sems, True)
        both_rest.first()
        down_rest.relay()
        for h in range(HEADS):
            lanes = slice(h * HEAD_DIM, (h + 1) * HEAD_DIM)
            span_h = slice(h * tokens, (h + 1) * tokens)
            query = dot(normed, v.qkv_weight[:, lanes], 1, 0)
            v.query[span_h, :] = query
            turned = turn(unit_rows(query)[0] * v.gains[4:5, :HEAD_DIM], v.cosine[...], v.sine[...])
            v.turned[span_h, :] = turned.astype(jnp.bfloat16)
        save(v.query, saved.query)
        save(v.turned, saved.turned)
        save(v.normed, saved.normed)
        save(v.key, saved.key)
        near.arrived()
        far.start()
        output_y.relay()
        output_cross[1].start()
        output_cross[3].start()
        both_rest.relay()
        output_y.last()
        output_cross[2].start()
        down_rest.last()
        for push in output_cross:
            push.arrived()

        @pl.loop(0, 16)
        def _(i):
            for j in range(4):
                pair = [output_all[i // 4, i % 4, 2 * j + k].astype(jnp.float32) for k in range(2)]
                rows = pl.ds(pl.multiple_of(64 * i + 16 * j, 16), 16)
                v.output_weight[rows, :] = jnp.concatenate(pair, axis=0).astype(jnp.bfloat16)

        save(v.output_weight, saved.output_weight)
        far.arrived()
        v.kv[...] = kv[...].reshape(span, 2 * HEAD_DIM)
        save(v.kv, saved.kv)
        allowed = allowed_keys(q * tokens, beginning, tokens, span)
        keys, values = v.kv[:, :HEAD_DIM], v.kv[:, HEAD_DIM:]
        rows = tokens // SUBS

        def attend_part(part):
            here_rows = slice(part * rows, (part + 1) * rows)
            for h in range(HEADS):
                span_h = slice(h * tokens + part * rows, h * tokens + (part + 1) * rows)
                scores = dot(v.turned[span_h, :], keys, 1, 1) * HEAD_DIM ** (-0.5)
                scores = jnp.where(allowed[here_rows], scores, NEGATIVE)
                exponent = jnp.exp(scores - jnp.max(scores, axis=-1, keepdims=True))
                probs = exponent / jnp.sum(exponent, axis=-1, keepdims=True)
                v.probs[span_h, :] = probs
                mixed = dot(probs.astype(jnp.bfloat16), values, 1, 0)
                v.mixed[here_rows, h * HEAD_DIM : (h + 1) * HEAD_DIM] = mixed.astype(jnp.bfloat16)
            branch = dot(v.mixed[here_rows, :], v.output_weight[...], 1, 0)
            v.branch[here_rows, :] = branch
            hidden = inputs[here_rows] + unit_rows(branch)[0] * v.gains[1:2, :]
            v.hidden[here_rows, :] = hidden
            v.feed[here_rows, :] = (unit_rows(hidden)[0] * v.gains[2:3, :]).astype(jnp.bfloat16)

        attend_part(0)
        first_rows = v.feed.at[pl.ds(0, rows)]
        block = lambda k: feeds_out.at[k * 2 + c]
        feed_y = RingGather(
            first_rows, block, lambda k, h: feeds_out.at[k * 2 + c, pl.ds(h * (rows // 2), rows // 2)],
            y, lambda k: device(x, k, z, c), sems,
        )
        feed_cross = [
            Push(
                first_rows if d == 0 else block((y + d) % 4), block((y + d) % 4), sems, other,
                feeds_out.at[(y + d) % 4 * 2 + 1 - c],
            )
            for d in range(4)
        ]
        feed_y.first()
        feed_cross[0].start()
        save(first_rows, feeds_out.at[s])
        attend_part(1)
        for src, dst in (
            (v.probs, saved.probs), (v.branch, saved.branch), (v.hidden, saved.hidden), (v.mixed, saved.mixed),
            (v.feed, saved.feed),
        ):
            save(src, dst)
        feed_y.relay()
        feed_cross[1].start()
        feed_cross[3].start()
        both_rest.last()
        feed_y.last()
        feed_cross[2].start()
        for push in feed_cross:
            push.arrived()
        rings = [query_ring, kv_ring, down_ring, output_ring, both_ring]
        rings += [query_rest, kv_rest, down_rest, output_rest, both_rest, output_y, feed_y]
        for ring in rings:
            ring.close()
        for push in sent + output_cross + feed_cross + [near, far]:
            push.sent()
        for copy in saves:
            copy.wait()

    outs = list(keep.values()) + [
        ((4, 4, 72, 2 * WIDE), low),
        ((4, 4, PIECE, D), low),
        ((8, tokens // SUBS, D), low),
    ]
    scratch = [pltpu.VMEM(shape, kind) for shape, kind in keep.values()] + [
        pltpu.VMEM((8, 72, 128), low),
        pltpu.VMEM((8, 40, 128), low),
        pltpu.VMEM((8, 126, 128), low),
        pltpu.VMEM((128, 128), wide),
        pltpu.VMEM((80, 2 * WIDE), wide),
        pltpu.VMEM((72, 1024), low),
        pltpu.VMEM((80, 512), low),
        pltpu.VMEM((72, 2 * WIDE), low),
        pltpu.VMEM((4, 4, 72, 1024), low),
        pltpu.VMEM((4, 4, 80, 512), low),
        pltpu.VMEM((4, 4, 8, 8, D), low),
        pltpu.VMEM((3, tokens, 2 * HEAD_DIM), low),
        pltpu.VMEM((128, D), wide),
        pltpu.VMEM((128, HEAD_DIM), wide),
    ]
    out = call(
        kernel, "attend", number, outs, [stream, doc_starts, own_query, own_kv, own_output, own_both, own_down],
        scratch, 3 * 7 + 11 * 4 + 2 * 4 + 4 + 2 + 4 + 4, in_specs=[VMEM] * 7, local=5 + 16,
    )
    return SimpleNamespace(**dict(zip(keep, out))), out[len(keep) :]


def norm_grad(values, gain, grad):
    unit, scale = unit_rows(values)
    scaled = gain * grad
    return (
        scale * (scaled - unit * jnp.mean(unit * scaled, axis=-1, keepdims=True)),
        jnp.sum(grad * unit, axis=0, keepdims=True),
    )


def scatter_rings(total, boxes, sems):
    x, y, z, c = place()
    z_peer, x_peer = (lambda k: device(x, y, k, c)), (lambda k: device(k, y, z, c))

    def one(order):
        if order == 0:
            chunk, half = lambda k: total.at[:, k], lambda k, h: total.at[pl.ds(2 * h, 2), k]
        else:
            chunk, half = lambda k: total.at[k], lambda k, h: total.at[k, pl.ds(2 * h, 2)]
        return RingSum(chunk, half, boxes[:4], (z, x)[order], (z_peer, x_peer)[order], sems, add_into)

    def two(order):
        chunk = (lambda k: total.at[k, z]) if order == 0 else (lambda k: total.at[x, k])
        half = lambda k, h: split_lanes(chunk(k), h)
        return RingSum(chunk, half, boxes[4:], (x, z)[order], (x_peer, z_peer)[order], sems, add_into)

    return Either(c, sems, one), Either(c, sems, two)


def scatter_boxes(rows, width, kind):
    lanes = lane_halves(width)
    return (
        [pltpu.VMEM((4, 4, rows, width), kind)]
        + [pltpu.VMEM((2, rows, width), kind)] * 2
        + [pltpu.VMEM((4, rows, width), kind)] * 2
        + [pltpu.VMEM((rows, size), kind) for _, size in lanes]
        + [pltpu.VMEM((rows, width), kind)] * 2
    )


BOTH, DOWN, OUTPUT, QUERY, KV = range(5)
SHARED = (OUTPUT, QUERY, KV)
GIVE, TAKE = 9, 10


def attend_back(number, arrays):
    tokens = arrays["hidden"].shape[0]
    span = tokens + WINDOW
    names = list(arrays)
    low, wide = jnp.bfloat16, jnp.float32
    results = dict(
        stream_grad=((tokens, D), low),
        both_rows=((8, 126, 128), low),
        query_grad=((9, 1024), wide),
        key_grad=((9, 256), wide),
        value_grad=((9, 256), wide),
        output_grad=((8, D), wide),
        down_grad=((PIECE, D), wide),
        sums=((8, D), wide),
    )
    sizes = {BOTH: (72, 2 * WIDE), DOWN: (PIECE, D), OUTPUT: (64, 640), QUERY: (72, 512), KV: (72, 256)}
    stores = []
    for name, (rows, width) in sizes.items():
        stores.append(scatter_boxes(rows, width, low))
        if name in SHARED:
            stores[-1] += [pltpu.VMEM((4, 4, rows, width), low)] * 2
    room = SimpleNamespace(
        hidden_grad=pltpu.VMEM((tokens, D), wide),
        branch_low=pltpu.VMEM((tokens, D), low),
        mixed_grad=pltpu.VMEM((HEADS * tokens, HEAD_DIM), low),
        score_low=pltpu.VMEM((HEADS * tokens, span), low),
        probs_low=pltpu.VMEM((HEADS * tokens, span), low),
        kv_grad=pltpu.VMEM((span, 2 * HEAD_DIM), wide),
        halo_out=pltpu.VMEM((2, tokens, 2 * HEAD_DIM), low),
        halo_in=pltpu.VMEM((2, tokens, 2 * HEAD_DIM), low),
        qkv_low=pltpu.VMEM((tokens, 1536), low),
        term=pltpu.VMEM((D, 1024), wide),
        merge=pltpu.VMEM((72, 2 * WIDE), wide),
        flat=pltpu.VMEM((128, 128), wide),
        both_give=pltpu.VMEM((8, 126, 128), low),
        query_give=pltpu.VMEM((8, 36, 128), low),
        query_take=pltpu.VMEM((8, 36, 128), low),
        kv_give=pltpu.VMEM((8, 18, 128), low),
        kv_take=pltpu.VMEM((8, 18, 128), low),
        output_give=pltpu.VMEM((8, 8, 640), low),
        output_take=pltpu.VMEM((8, 8, 640), low),
        own_sums=pltpu.VMEM((3, 8, D), wide),
        shard_sums=pltpu.VMEM((8, 8, D), wide),
        z_sums=pltpu.VMEM((4, 8, D), wide),
        x_sums=pltpu.VMEM((4, 8, D), wide),
    )
    room = vars(room)
    held_names = names[:-2]

    def kernel(*refs):
        refs = list(refs)

        def take(count):
            taken, refs[:] = refs[:count], refs[count:]
            return taken

        given = dict(zip(names, take(len(names))))
        o = SimpleNamespace(**dict(zip(results, take(len(results)))))
        a = SimpleNamespace(**dict(zip(held_names, take(len(held_names)))))
        b = SimpleNamespace(**dict(zip(room, take(len(room)))))
        held = {n: take(len(store)) for n, store in zip(sizes, stores)}
        send, recv, here = refs
        x, y, z, c = place()
        q, s = lax.axis_index("seq"), lax.axis_index("shard")
        sems = Sems(send, recv)
        other = device(x, y, z, 1 - c)
        after, before = {"seq": (q + 1) % 16, "shard": s}, {"seq": (q + 15) % 16, "shard": s}
        rings = {n: scatter_rings(held[n][0], held[n][1:9], sems) for n in sizes}
        cross = {n: Push(held[n][GIVE], held[n][TAKE], sems, other) for n in SHARED}
        loads = [
            pltpu.make_async_copy(given[names[-2]], held[BOTH][0], here.at[0]),
            pltpu.make_async_copy(given[names[-1]], held[DOWN][0], here.at[1]),
        ]
        for at, name in enumerate(held_names):
            loads.append(pltpu.make_async_copy(given[name], getattr(a, name), here.at[2 + at]))
        for load in loads:
            load.start()
        greet(
            [device(x, y + dy, z, (c + dc) % 2) for dy, dc in SHARD_STEPS]
            + [device(x, y, z + d, c) for d in (1, 2, 3)]
            + [device(x + d, y, z, c) for d in (1, 2, 3)]
            + [after, before]
        )
        for n, load in zip((BOTH, DOWN), loads):
            load.wait()
            rings[n][0].first()
        for load in loads[2:]:
            load.wait()
        gains = a.gains
        cosine, sine = a.cosine, a.sine
        own = b.own_sums.at[0]
        own[...] = jnp.zeros(own.shape, wide)
        pending = []

        upstream = a.cotangent[...].astype(wide)
        extra, own[2:3, :] = norm_grad(a.hidden[...], gains[2:3, :], a.feed_grad[...])
        hidden_grad = upstream + extra
        b.hidden_grad[...] = hidden_grad
        branch_grad, own[1:2, :] = norm_grad(a.branch[...], gains[1:2, :], hidden_grad)
        b.branch_low[...] = branch_grad.astype(low)
        own[3:4, :] = a.post_grad[...]
        for at, squares in enumerate((
            jnp.sum(jnp.square(a.stream[...].astype(wide)), axis=0, keepdims=True),
            jnp.sum(jnp.square(a.hidden[...]), axis=0, keepdims=True),
            a.result_squares[...],
        )):
            folded = functools.reduce(jnp.add, [squares[:, 128 * j : 128 * (j + 1)] for j in range(D // 128)])
            own[4:5, 512 + 128 * at : 640 + 128 * at] = folded
        for h in range(HEADS):
            rows, lanes = slice(h * tokens, (h + 1) * tokens), slice(h * HEAD_DIM, (h + 1) * HEAD_DIM)
            b.mixed_grad[rows, :] = dot(b.branch_low[...], a.output_weight[lanes, :], 1, 1).astype(low)
        keys, values = a.kv[:, :HEAD_DIM], a.kv[:, HEAD_DIM:]
        for h in range(HEADS):
            rows = slice(h * tokens, (h + 1) * tokens)
            probs = a.probs[rows, :]
            prob_grad = dot(b.mixed_grad[rows, :], values, 1, 1)
            inner = jnp.sum(probs * prob_grad, axis=-1, keepdims=True)
            b.score_low[rows, :] = (probs * (prob_grad - inner) * HEAD_DIM ** (-0.5)).astype(low)
            b.probs_low[rows, :] = probs.astype(low)
        b.kv_grad[:, :HEAD_DIM] = dot(b.score_low[...], a.turned[...], 0, 0)
        b.kv_grad[:, HEAD_DIM:] = dot(b.probs_low[...], b.mixed_grad[...], 0, 0)

        halo_far = Push(b.halo_out.at[0], b.halo_in.at[0], sems, before)
        halo_near = Push(b.halo_out.at[1], b.halo_in.at[1], sems, before)
        b.halo_out[0] = b.kv_grad[:tokens, :].astype(low)
        halo_far.start()

        gain_grad = jnp.zeros((1, HEAD_DIM), wide)
        for h in range(HEADS):
            rows, lanes = slice(h * tokens, (h + 1) * tokens), slice(h * HEAD_DIM, (h + 1) * HEAD_DIM)
            turned_grad = dot(b.score_low[rows, :], keys, 1, 0)
            back = turn(turned_grad, cosine[...], -sine[...])
            grad, extra = norm_grad(a.query[rows, :], gains[4:5, :HEAD_DIM], back)
            gain_grad += extra
            b.qkv_low[:, lanes] = grad.astype(low)
        own[4:5, :HEAD_DIM] = gain_grad

        def term(start, width, give, take):
            out = b.term

            @pl.loop(0, D // 128)
            def _(i):
                lanes = pl.ds(pl.multiple_of(i * 128, 128), 128)
                out[lanes, : 2 * width] = dot(a.normed[:, lanes], b.qkv_low[:, start : start + 2 * width], 0, 0)

            @pl.loop(0, 16)
            def _(i):
                rows = pl.ds(pl.multiple_of(72 * i, 8), 72)
                for ref, core in ((take, c), (give, 1 - c)):
                    lanes = pl.ds(pl.multiple_of(core * width, 128), width)
                    ref[i // 4, i % 4] = out[rows, lanes].astype(low)

        term(0, 512, held[QUERY][GIVE], held[QUERY][0])
        cross[QUERY].start()

        @pl.loop(0, 8)
        def _(i):
            lanes = pl.ds(pl.multiple_of(i * 128, 128), 128)
            part = dot(a.mixed[:, lanes], b.branch_low[...], 0, 0).astype(low)
            for k in range(2):
                block = (2 * i + k) // 4, (2 * i + k) % 4
                for core in range(2):
                    lanes_out = slice(512 * core, 512 * core + 640)
                    value = part[64 * k : 64 * (k + 1), lanes_out]

                    @pl.when(c == core)
                    def _():
                        held[OUTPUT][0][block] = value

                    @pl.when(c != core)
                    def _():
                        held[OUTPUT][GIVE][block] = value

        cross[OUTPUT].start()
        for n in (BOTH, DOWN):
            rings[n][0].second()
        halo_far.arrived()
        b.halo_out[1] = (b.kv_grad[tokens : 2 * tokens, :] + b.halo_in[0].astype(wide)).astype(low)
        halo_near.start()
        for n in (QUERY, OUTPUT):
            cross[n].arrived()
            add_into(held[n][0], held[n][TAKE])
            rings[n][0].first()
        halo_near.arrived()
        kv_grad = b.kv_grad[2 * tokens :, :] + b.halo_in[1].astype(wide)
        back = turn(kv_grad[:, :HEAD_DIM], cosine[...], -sine[...])
        grad, own[4:5, HEAD_DIM : 2 * HEAD_DIM] = norm_grad(a.key[...], gains[5:6, :HEAD_DIM], back)
        b.qkv_low[:, 1024:1280] = grad.astype(low)
        b.qkv_low[:, 1280:] = kv_grad[:, HEAD_DIM:].astype(low)
        term(1024, 256, held[KV][GIVE], held[KV][0])
        cross[KV].start()
        for n in (QUERY, OUTPUT):
            rings[n][0].second()
        cross[KV].arrived()
        add_into(held[KV][0], held[KV][TAKE])
        rings[KV][0].first()
        for n in (BOTH, DOWN):
            rings[n][0].third()
            rings[n][1].first()
        normed_grad = dot(b.qkv_low[...], a.qkv_weight[...], 1, 1)
        extra, own[0:1, :] = norm_grad(a.stream[...].astype(wide), gains[0:1, :], normed_grad)
        o.stream_grad[...] = (b.hidden_grad[...] + extra).astype(low)

        def all_sum(stage, box, me, steps, target):
            source = b.own_sums.at[stage]
            pushes = []
            for to, back in steps:
                push = Push(source, box.at[me], sems, target(to), box.at[back])
                push.start()
                pushes.append(push)
            pending.extend(pushes)
            box[me] = source[...]

            def finish():
                for push in pushes:
                    push.arrived()
                return functools.reduce(jnp.add, [box[k] for k in range(box.shape[0])])

            return finish

        steps = []
        for dy, dc in SHARD_STEPS:
            there = (y + dy) % 4, (c + dc) % 2
            steps.append((there, (y + 4 - dy) % 4 * 2 + (c + 2 - dc) % 2))
        finish = all_sum(0, b.shard_sums, s, steps, lambda t: device(x, t[0], z, t[1]))
        rings[KV][0].second()
        for n in (QUERY, OUTPUT):
            rings[n][0].third()
            rings[n][1].first()
        for n in (BOTH, DOWN):
            rings[n][1].second()
        b.own_sums[1] = finish()
        turns = lambda at: [((at + d) % 4, (at + 4 - d) % 4) for d in (1, 2, 3)]
        finish = all_sum(1, b.z_sums, z, turns(z), lambda t: device(x, y, t, c))
        rings[KV][0].third()
        rings[KV][1].first()
        for n in (QUERY, OUTPUT):
            rings[n][1].second()

        def spread(source, box):
            pushes = []
            for dy, dc in SHARD_STEPS:
                to, back = (y + dy) % 4 * 2 + (c + dc) % 2, (y + 4 - dy) % 4 * 2 + (c + 2 - dc) % 2
                push = Push(source.at[to], box.at[s], sems, device(x, y + dy, z, (c + dc) % 2), box.at[back])
                push.start()
                pushes.append(push)
            box[s] = source[s]
            pending.extend(pushes)
            return pushes

        def flatten(block, give):
            width = block.shape[-1]
            tiles = width // 128
            merge, flat = b.merge, b.flat
            merge[:, :width] = block[...].astype(wide)
            for d in range(8):
                for j in range(tiles):
                    flat[pl.ds(j, 9, tiles), :] = merge[9 * d : 9 * d + 9, 128 * j : 128 * (j + 1)]
                give[d] = flat[: 9 * tiles, :].astype(low)

        def unflatten(value, tiles, write):
            b.flat[: 9 * tiles, :] = value
            for j in range(tiles):
                write(j, b.flat[pl.ds(j, 9, tiles), :])

        rings[KV][1].second()
        for n in (BOTH, DOWN):
            rings[n][1].third()
        flatten(held[BOTH][0].at[x, z], b.both_give)
        got_both = spread(b.both_give, o.both_rows)
        for n in (QUERY, OUTPUT):
            rings[n][1].third()
        b.own_sums[2] = finish()
        finish = all_sum(2, b.x_sums, x, turns(x), lambda t: device(t, y, z, c))
        flatten(held[QUERY][0].at[x, z], b.query_give)
        got_query = spread(b.query_give, b.query_take)
        for d in range(8):
            b.output_give[d] = held[OUTPUT][0][x, z, 8 * d : 8 * d + 8, :]
        got_output = spread(b.output_give, b.output_take)
        rings[KV][1].third()
        flatten(held[KV][0].at[x, z], b.kv_give)
        got_kv = spread(b.kv_give, b.kv_take)
        o.down_grad[...] = held[DOWN][0][x, z].astype(wide)
        o.sums[...] = finish()

        def over_y(box, core):
            return functools.reduce(jnp.add, [box[2 * k + core].astype(wide) for k in range(4)])

        for push in got_query:
            push.arrived()
        for core in range(2):
            def write(j, value, core=core):
                o.query_grad[:, 512 * core + 128 * j : 512 * core + 128 * (j + 1)] = value

            unflatten(over_y(b.query_take, core), 4, write)
        for push in got_output:
            push.arrived()
        o.output_grad[:, :512] = over_y(b.output_take, 0)[:, :512]
        o.output_grad[:, 512:] = over_y(b.output_take, 1)
        for push in got_kv:
            push.arrived()
        for core, out in enumerate((o.key_grad, o.value_grad)):
            def write(j, value, out=out):
                out[:, 128 * j : 128 * (j + 1)] = value

            unflatten(over_y(b.kv_take, core), 2, write)
        for push in got_both:
            push.arrived()
        for pair in rings.values():
            for ring in pair:
                ring.close()
        for push in list(cross.values()) + pending + [halo_far, halo_near]:
            push.sent()

    ins = list(arrays.values())
    out = call(
        kernel, "attend_back", number, list(results.values()), ins, [pltpu.VMEM(arrays[n].shape, arrays[n].dtype) for n in held_names] + list(room.values()) + sum(stores, []), 5 * 8 + 3 + 2 + 13 + 28,
        out_specs=[VMEM] * len(results), local=len(ins),
    )
    return dict(zip(results, out))


def split_hidden(weight):
    parts = weight.reshape(9, 16, 8, PIECE).transpose(2, 0, 1, 3)
    return jnp.pad(parts, ((0, 0), (0, 0), (0, 0), (0, SLOT - PIECE))).reshape(8, 9, WIDE)


def local(
    stream, doc_starts, cotangent, attention_norm, query_weight, key_weight, value_weight, query_norm, key_norm,
    output_weight, attention_post_norm, mlp_norm, gate_weight, up_weight, down_weight, mlp_post_norm,
):
    norms = (attention_norm, attention_post_norm, mlp_norm, mlp_post_norm, query_norm, key_norm)
    own_gains = jnp.concatenate([jnp.pad(g, (0, 16 - g.shape[0])) for g in norms] + [jnp.zeros((32 + 3 * 128,), jnp.bfloat16)])
    own_kv = jnp.concatenate([key_weight, value_weight], axis=1).reshape(36, 128)
    own_kv = jnp.concatenate([own_kv, own_gains.reshape(4, 128)], axis=0)
    own_both = jnp.concatenate([split_hidden(gate_weight), split_hidden(up_weight)], axis=2)
    ahead, (both16, down16, feeds_a) = attend(
        0, stream[0], doc_starts, query_weight.reshape(72, 128), own_kv, output_weight,
        own_both.reshape(8, 126, 128), down_weight,
    )

    block_output, feed_grad, gain_mlp_post_grad, result_squares, both_term, down_term = feed_forward(
        1, ahead.feed, feeds_a, both16.reshape(D, 2 * WIDE), down16, ahead.hidden, cotangent[0], ahead.gains
    )

    named = vars(ahead)
    del named["feed"]
    back = SimpleNamespace(**attend_back(
        2,
        dict(
            **named, feed_grad=feed_grad, cotangent=cotangent[0], stream=stream[0],
            post_grad=gain_mlp_post_grad, result_squares=result_squares,
            both_term=both_term.reshape(4, 4, 72, 2 * WIDE),
            down_term=down_term.reshape(16, SLOT, D)[:, :PIECE].reshape(4, 4, PIECE, D),
        ),
    ))

    def whole(rows):
        parts = rows.reshape(8, 9, 16, SLOT)[..., :PIECE]
        return parts.transpose(1, 2, 0, 3).reshape(9, FF).astype(jnp.float32)

    both_rows = back.both_rows.reshape(8, 9, 2 * WIDE)
    sums = back.sums
    own = lax.axis_index("seq") * 8 + lax.axis_index("shard")
    gain_grads = lax.dynamic_slice_in_dim(sums[:4], own * 9, 9, 1)
    query_gain_grad = lax.dynamic_slice_in_dim(sums[4, :HEAD_DIM], own * 2, 2, 0)
    key_gain_grad = lax.dynamic_slice_in_dim(sums[4, HEAD_DIM : 2 * HEAD_DIM], own * 2, 2, 0)
    stream_rms = jnp.sqrt(jnp.sum(sums[4, 512:896].reshape(3, 128), axis=1) / (32768 * D))
    return (
        block_output[None],
        back.stream_grad[None],
        gain_grads[0],
        back.query_grad,
        back.key_grad,
        back.value_grad,
        query_gain_grad,
        key_gain_grad,
        back.output_grad,
        gain_grads[1],
        gain_grads[2],
        whole(both_rows[:, :, :WIDE]),
        whole(both_rows[:, :, WIDE:]),
        back.down_grad,
        gain_grads[3],
        stream_rms,
    )


def solution(mesh):
    rows = P(("seq", "shard"))
    tokens = P("shard", "seq", None)
    table = P(("seq", "shard"), None)
    return jax.shard_map(
        local,
        mesh=mesh,
        in_specs=(
            tokens, P("shard", None), tokens, rows, table, table, table, rows, rows, table, rows, rows, table, table,
            table, rows,
        ),
        out_specs=(
            tokens, tokens, rows, table, table, table, rows, rows, table, rows, rows, table, table, table, rows, P(),
        ),
        check_vma=False,
    )
```

```python
import functools
import math
from types import SimpleNamespace

import jax
import jax.numpy as jnp
from jax import lax
from jax.experimental import pallas as pl
from jax.experimental.pallas import tpu as pltpu
from jax.sharding import PartitionSpec as P

D = 1152
HEADS = 4
HEAD_DIM = 256
WINDOW = 512
FF = 6912
PIECE = 54
SLOT = 56
WIDE = 16 * SLOT

EPSILON = 1e-06
NEGATIVE = -1e30
MESH = pl.DeviceIdType.MESH
MIB = 2**20


def place():
    q, s = lax.axis_index("seq"), lax.axis_index("shard")
    return q // 4, s // 2, q % 4, s % 2


def device(x, y, z, c):
    return {"seq": x % 4 * 4 + z % 4, "shard": y % 4 * 2 + c}


def greet(targets):
    barrier = pltpu.get_barrier_semaphore()
    for target in targets:
        pl.semaphore_signal(barrier, inc=1, device_id=target, device_id_type=MESH)
    pl.semaphore_wait(barrier, len(targets))


class Sems:
    def __init__(self, send, recv):
        self.send, self.recv, self.used = send, recv, 0

    def take(self):
        self.used += 1
        return self.send.at[self.used - 1], self.recv.at[self.used - 1]


class Push:
    def __init__(self, src, dst, sems, to, lands=None):
        send, recv = sems.take()
        self.out = pltpu.make_async_remote_copy(
            src_ref=src, dst_ref=dst, send_sem=send, recv_sem=recv, device_id=to, device_id_type=MESH
        )
        lands = dst if lands is None else lands
        self.back = pltpu.make_async_remote_copy(
            src_ref=lands, dst_ref=lands, send_sem=send, recv_sem=recv, device_id=to, device_id_type=MESH
        )

    def start(self):
        self.out.start()

    def arrived(self):
        self.back.wait_recv()

    def sent(self):
        self.out.wait_send()


class RingGather:
    def __init__(self, own, slot, half, me, peer, sems):
        up, down, far = (me + 1) % 4, (me + 3) % 4, (me + 2) % 4
        self.right = Push(own, slot(me), sems, peer(up), slot(down))
        self.left = Push(own, slot(me), sems, peer(down), slot(up))
        split = half(down, 0)
        self.right2 = None if split is None else Push(split, split, sems, peer(up), half(far, 0))
        split = half(up, 1)
        self.left2 = None if split is None else Push(split, split, sems, peer(down), half(far, 1))

    def first(self):
        self.right.start()
        self.left.start()

    def relay(self):
        self.right.arrived()
        if self.right2 is not None:
            self.right2.start()
        self.left.arrived()
        if self.left2 is not None:
            self.left2.start()

    def last(self):
        if self.right2 is not None:
            self.right2.arrived()
        if self.left2 is not None:
            self.left2.arrived()

    def close(self):
        for push in (self.right, self.left, self.right2, self.left2):
            if push is not None:
                push.sent()


class DirectGather:
    def __init__(self, own, slot, half, me, peer, sems):
        self.pushes = [
            Push(own, slot(me), sems, peer((me + d) % 4), slot((me + 4 - d) % 4)) for d in (1, 3, 2)
        ]

    def first(self):
        for push in self.pushes:
            push.start()

    def relay(self):
        for push in self.pushes[:2]:
            push.arrived()

    def last(self):
        self.pushes[2].arrived()

    def close(self):
        for push in self.pushes:
            push.sent()


class DirectSum:
    def __init__(self, chunk, half, inbox, me, peer, sems, add):
        self.total, self.inbox, self.add = chunk(me), inbox[:3], add
        self.pushes = [
            Push(chunk((me + d) % 4), box, sems, peer((me + d) % 4)) for d, box in zip((2, 1, 3), self.inbox)
        ]

    def first(self):
        for push in self.pushes:
            push.start()

    def second(self):
        pass

    def third(self):
        for push, box in zip(self.pushes, self.inbox):
            push.arrived()
            self.add(self.total, box)

    def close(self):
        for push in self.pushes:
            push.sent()


class RingSum:
    def __init__(self, chunk, half, inbox, me, peer, sems, add):
        up, down, far = (me + 1) % 4, (me + 3) % 4, (me + 2) % 4
        self.chunk, self.half, self.inbox, self.add = chunk, half, inbox, add
        self.me, self.up, self.down = me, up, down
        near_a, near_b, right, left = inbox
        self.far_a = Push(half(far, 0), near_a, sems, peer(up))
        split = half(far, 1)
        self.far_b = None if split is None else Push(split, near_b, sems, peer(down))
        self.right = Push(chunk(up), right, sems, peer(up))
        self.left = Push(chunk(down), left, sems, peer(down))

    def first(self):
        self.far_a.start()
        if self.far_b is not None:
            self.far_b.start()

    def second(self):
        self.far_a.arrived()
        self.add(self.half(self.up, 0), self.inbox[0])
        self.right.start()
        if self.far_b is not None:
            self.far_b.arrived()
            self.add(self.half(self.down, 1), self.inbox[1])
        self.left.start()

    def third(self):
        self.right.arrived()
        self.add(self.chunk(self.me), self.inbox[2])
        self.left.arrived()
        self.add(self.chunk(self.me), self.inbox[3])

    def close(self):
        for push in (self.far_a, self.far_b, self.right, self.left):
            if push is not None:
                push.sent()


def add_into(total, extra):
    if len(total.shape) == 2:
        summed = total[...].astype(jnp.float32) + extra[...].astype(jnp.float32)
        total[...] = summed.astype(total.dtype)
        return

    @pl.loop(0, total.shape[0])
    def _(step):
        add_into(total.at[step], extra.at[step])


ANY = pl.BlockSpec(memory_space=pl.ANY)
VMEM = pl.BlockSpec(memory_space=pltpu.VMEM)


def call(kernel, name, number, outs, ins, scratch, copies, in_specs=None, out_specs=None, local=0, aliases=None):
    outs = [jax.ShapeDtypeStruct(shape, dtype) for shape, dtype in outs]
    scratch = list(scratch) + [pltpu.SemaphoreType.DMA((copies,)), pltpu.SemaphoreType.DMA((copies,))]
    if local:
        scratch.append(pltpu.SemaphoreType.DMA((local,)))
    return pl.pallas_call(
        kernel,
        name=name,
        out_shape=outs,
        in_specs=in_specs or [ANY] * len(ins),
        out_specs=out_specs or [ANY] * len(outs),
        scratch_shapes=scratch,
        input_output_aliases=aliases or {},
        compiler_params=pltpu.CompilerParams(
            collective_id=number, has_side_effects=True, vmem_limit_bytes=60 * MIB
        ),
    )(*ins)


SHARD_STEPS = [(dy, dc) for dy in range(4) for dc in range(2) if dy or dc]


def lane_halves(width):
    low = width // 256 * 128 if width % 256 == 0 else (width // 128 + 1) // 2 * 128
    return ((0, low), (low, width - low)) if width > 128 else ((0, width), None)


def dot(a, b, contract_a, contract_b):
    return lax.dot_general(a, b, (((contract_a,), (contract_b,)), ((), ())), preferred_element_type=jnp.float32)


SUBS = 2
BACK = (0, 1, 3, 2)


def gelu_terms(gate):
    a, b = math.sqrt(2.0 / math.pi), 0.044715
    square = gate * gate
    bend = jnp.tanh(a * gate * (1.0 + b * square))
    half = 0.5 * (1.0 + bend)
    slope = half + 0.5 * gate * (1.0 - bend * bend) * a * (1.0 + 3.0 * b * square)
    return gate * half, slope


def feed_forward(number, feed, feeds_a, full_both, down16, hidden, cotangent, gains):
    tokens, width = feed.shape
    rows = tokens // SUBS
    half = rows // 2

    def kernel(
        feed_in, feeds_in, both_in, down_in, hidden_in, cotangent_in, gains_in,
        block_out, feed_out, gain_out, square_out, both_out, down_out,
        feeds, downs, both, active, part, inbox, near, right, left, w_both, w_down, raw, pad, both_term, down_term,
        far_a, far_b, right4, left4, send, recv, here,
    ):
        x, y, z, c = place()
        sems = Sems(send, recv)
        other = device(x, y, z, 1 - c)
        to = lambda d: device(x, y + d, z, c)
        span = lambda s: pl.ds(s * rows, rows)
        a, b = 0, 1
        loads = [
            pltpu.make_async_copy(feeds_in, feeds.at[a], here.at[0]),
            pltpu.make_async_copy(both_in, w_both, here.at[1]),
            pltpu.make_async_copy(down_in, raw, here.at[2]),
            pltpu.make_async_copy(feed_in.at[span(b)], feeds.at[b, y * 2 + c], here.at[3]),
        ]
        for load in loads:
            load.start()
        greet(
            [to(1), to(3), other, device(x, y, z + 1, c), device(x, y, z + 3, c)]
            + [device(x + 1, y, z, c), device(x + 3, y, z, c)]
        )

        def gather(source, blocks, s):
            slot = lambda k: blocks.at[s, k * 2 + c]
            ring = RingGather(
                source, slot, lambda k, h: blocks.at[s, k * 2 + c, pl.ds(h * half, half)],
                y, lambda k: device(x, k, z, c), sems,
            )
            cross = []
            for d in range(4):
                k = (y + d) % 4
                cross.append(
                    Push(source if d == 0 else slot(k), slot(k), sems, other, blocks.at[s, k * 2 + 1 - c])
                )

            def first():
                ring.first()
                cross[0].start()

            def relay():
                ring.relay()
                cross[1].start()
                cross[3].start()

            def last():
                ring.last()
                cross[2].start()

            def close():
                ring.close()
                for push in cross:
                    push.sent()

            return first, relay, last, [push.arrived for push in cross], close

        class Total:
            def __init__(self, s):
                self.s = s
                self.cross = {}
                for d in range(4):
                    k = (y + d) % 4
                    self.cross[d] = Push(part.at[s, k * 2 + 1 - c], inbox.at[s, d], sems, other)
                self.own = lambda d: part.at[s, (y + d) % 4 * 2 + c]
                self.far_a = Push(self.own(2).at[pl.ds(0, half)], near.at[s, 0], sems, to(1))
                self.far_b = Push(self.own(2).at[pl.ds(half, half)], near.at[s, 1], sems, to(3))
                self.right = Push(self.own(1), right.at[s], sems, to(1))
                self.left = Push(self.own(3), left.at[s], sems, to(3))

            def far(self):
                self.cross[2].arrived()
                add_into(self.own(2), inbox.at[self.s, 2])
                self.far_a.start()
                self.far_b.start()

            def sides(self):
                for d in (1, 3):
                    self.cross[d].arrived()
                    add_into(self.own(d), inbox.at[self.s, d])

            def go(self):
                self.far_a.arrived()
                add_into(self.own(1).at[pl.ds(0, half)], near.at[self.s, 0])
                self.right.start()
                self.far_b.arrived()
                add_into(self.own(3).at[pl.ds(half, half)], near.at[self.s, 1])
                self.left.start()

            def final(self):
                self.cross[0].arrived()
                self.right.arrived()
                self.left.arrived()
                s = self.s
                pieces = (self.own(0), inbox.at[s, 0], right.at[s], left.at[s])
                return functools.reduce(jnp.add, [p[...].astype(jnp.float32) for p in pieces])

            def close(self):
                for push in list(self.cross.values()) + [self.far_a, self.far_b, self.right, self.left]:
                    push.sent()

        def steps(body, before, totals):
            @pl.loop(0, 4 * SUBS)
            def _(t):
                for at, hook in before.items():
                    pl.when(t == at)(hook)
                s, i = t // 4, t % 4
                d = i + i // 2 - i // 3 * 2
                body(s, pl.ds((y + d) % 4 * 2, 2))
                for at in range(4 * SUBS):
                    push = totals[at // 4].cross[BACK[at % 4]]
                    pl.when(t == at)(push.start)

        def flat(value):
            return value.reshape(2 * rows, value.shape[-1])

        def pair(value):
            return value.reshape(2, rows, value.shape[-1])

        def forward(s, chip):
            sums = dot(flat(feeds[s, chip]), w_both[...], 1, 0)
            both[s, chip] = pair(sums.astype(jnp.bfloat16))
            bent, _ = gelu_terms(sums[:, :WIDE])
            low = (bent * sums[:, WIDE:]).astype(jnp.bfloat16)
            active[s, chip] = pair(low)
            part[s, chip] = pair(dot(low, w_down[...], 1, 0).astype(jnp.bfloat16))

        def backward(s, chip):
            grad = dot(flat(downs[s, chip]), w_down[...], 1, 1)
            sums = flat(both[s, chip]).astype(jnp.float32)
            bent, slope = gelu_terms(sums[:, :WIDE])
            gate_grad = (grad * sums[:, WIDE:] * slope).astype(jnp.bfloat16)
            up_grad = (grad * bent).astype(jnp.bfloat16)
            both[s, chip, :, :WIDE] = pair(gate_grad)
            both[s, chip, :, WIDE:] = pair(up_grad)
            part[s, chip] = pair(dot(flat(both[s, chip]), w_both[...], 1, 1).astype(jnp.bfloat16))

        gain_out[...] = jnp.zeros_like(gain_out)
        square_out[...] = jnp.zeros_like(square_out)

        def norm_back(total, s):
            down = total.final()
            gain_row = gains_in[3:4, :]
            upstream = cotangent_in[span(s), :].astype(jnp.float32)
            scale = lax.rsqrt(jnp.mean(down * down, axis=-1, keepdims=True) + EPSILON)
            unit = down * scale
            result = hidden_in[span(s), :] + unit * gain_row
            block_out[span(s), :] = result.astype(jnp.bfloat16)
            square_out[...] += jnp.sum(result * result, axis=0, keepdims=True)
            gain_out[...] += jnp.sum(upstream * unit, axis=0, keepdims=True)
            scaled = gain_row * upstream
            grad = scale * (scaled - unit * jnp.mean(unit * scaled, axis=-1, keepdims=True))
            downs[s, y * 2 + c] = grad.astype(jnp.bfloat16)

        first_b, relay_b, last_b, met_b, close_b = gather(feed_in.at[span(b)], feeds, b)
        sum_a, sum_b = Total(a), Total(b)
        first_b()
        pad[...] = jnp.zeros_like(pad)
        for load in loads:
            load.wait()

        @pl.loop(0, 8)
        def _(i):
            for k in range(2):
                pad[SLOT * k : SLOT * k + PIECE, :] = raw[i // 2, i % 2 * 2 + k].astype(jnp.float32)
            w_down[pl.ds(pl.multiple_of(2 * SLOT * i, 16), 2 * SLOT), :] = pad[...].astype(jnp.bfloat16)

        def at_4():
            sum_a.far()
            met_b[0]()

        def at_5():
            last_b()
            sum_a.sides()
            met_b[1]()

        def at_6():
            sum_a.go()
            met_b[3]()

        steps(forward, {3: relay_b, 4: at_4, 5: at_5, 6: at_6, 7: met_b[2]}, (sum_a, sum_b))
        sum_b.far()
        norm_back(sum_a, a)
        sum_a.close()
        first_a, relay_a, last_a, met_a, close_a = gather(downs.at[a, y * 2 + c], downs, a)
        first_a()
        sum_b.sides()
        sum_b.go()
        old_b, old_close_b = sum_b, close_b
        first_b, relay_b, last_b, met_b, close_b = gather(downs.at[b, y * 2 + c], downs, b)
        sum_a, sum_b = Total(a), Total(b)

        def down_terms(s):
            every = 8 * rows

            @pl.loop(0, WIDE // 128)
            def _(i):
                units = pl.ds(pl.multiple_of(i * 128, 128), 128)
                value = dot(active[s, :, :, units].reshape(every, 128), downs[s].reshape(every, width), 0, 0)
                if s == b:
                    value += down_term[units, :].astype(jnp.float32)
                down_term[units, :] = value.astype(jnp.bfloat16)

        def both_terms(s, low=0, high=width // 128):
            every = 8 * rows

            @pl.loop(low, high)
            def _(i):
                lanes = pl.ds(pl.multiple_of(i * 128, 128), 128)
                value = dot(feeds[s, :, :, lanes].reshape(every, 128), both[s].reshape(every, 2 * WIDE), 0, 0)
                if s == b:
                    value += both_term[lanes, :].astype(jnp.float32)
                both_term[lanes, :] = value.astype(jnp.bfloat16)

        def back_1():
            relay_a()
            met_a[1]()

        def back_2():
            last_a()
            met_a[3]()

        def back_4():
            norm_back(old_b, b)
            old_b.close()
            old_close_b()
            first_b()
            sum_a.far()
            met_b[0]()

        def back_5():
            down_terms(a)
            sum_a.sides()
            relay_b()
            both_terms(a)
            sum_a.go()
            last_b()
            met_b[1]()

        down_ring = sum_row(raw, (far_a, far_b, right4, left4), sems)

        def start_down():
            down_terms(b)

            @pl.loop(0, 8)
            def _(i):
                both_slots = down_term[pl.ds(pl.multiple_of(2 * SLOT * i, 16), 2 * SLOT), :].astype(jnp.float32)
                for k in range(2):
                    slot = both_slots[SLOT * k : SLOT * k + PIECE].astype(jnp.bfloat16)
                    raw[i // 2, i % 2 * 2 + k] = slot

            down_ring.first()

        steps(
            backward,
            {0: met_a[0], 1: back_1, 2: back_2, 3: met_a[2], 4: back_4, 5: back_5, 6: met_b[3], 7: met_b[2]},
            (sum_a, sum_b),
        )
        sum_b.far()
        sum_b.sides()
        start_down()
        sum_b.go()
        feed_out[span(a), :] = sum_a.final()
        both_terms(b, 0, 4)
        down_ring.second()
        both_terms(b, 4)
        save = pltpu.make_async_copy(both_term, both_out, here.at[1])
        save.start()
        feed_out[span(b), :] = sum_b.final()
        down_ring.third()
        rows_out = [pltpu.make_async_copy(row, down_out, here.at[0]) for row in (raw.at[:, z], raw.at[x])]
        for core in (0, 1):
            pl.when(c == core)(rows_out[core].start)
        down_ring.close()
        sum_a.close()
        sum_b.close()
        close_a()
        close_b()
        save.wait()
        for core in (0, 1):
            pl.when(c == core)(rows_out[core].wait)

    low, wide = jnp.bfloat16, jnp.float32
    blocks = (SUBS, 8, rows)
    scratch = [
        pltpu.VMEM(blocks + (width,), low),
        pltpu.VMEM(blocks + (width,), low),
        pltpu.VMEM(blocks + (2 * WIDE,), low),
        pltpu.VMEM(blocks + (WIDE,), low),
        pltpu.VMEM(blocks + (width,), low),
        pltpu.VMEM((SUBS, 4, rows, width), low),
        pltpu.VMEM((SUBS, 2, half, width), low),
        pltpu.VMEM((SUBS, rows, width), low),
        pltpu.VMEM((SUBS, rows, width), low),
        pltpu.VMEM((width, 2 * WIDE), low),
        pltpu.VMEM((WIDE, width), low),
        pltpu.VMEM((4, 4, PIECE, width), low),
        pltpu.VMEM((2 * SLOT, width), wide),
        pltpu.VMEM((width, 2 * WIDE), low),
        pltpu.VMEM((WIDE, width), low),
        pltpu.VMEM((2, PIECE, width), low),
        pltpu.VMEM((2, PIECE, width), low),
        pltpu.VMEM((4, PIECE, width), low),
        pltpu.VMEM((4, PIECE, width), low),
    ]
    outs = [
        ((tokens, width), low),
        ((tokens, width), wide),
        ((1, width), wide),
        ((1, width), wide),
        ((width, 2 * WIDE), low),
        ((4, PIECE, width), low),
    ]
    return call(
        kernel, "feed_forward", number, outs, [feed, feeds_a, full_both, down16, hidden, cotangent, gains], scratch,
        32 * SUBS - 8 + 4, in_specs=[ANY] * 4 + [VMEM] * 3, out_specs=[VMEM] * 4 + [ANY] * 2, local=4,
    )


class Either:
    def __init__(self, core, sems, make):
        self.core, start, most = core, sems.used, 0
        self.variants = []
        for order in (0, 1):
            sems.used = start
            self.variants.append(make(order))
            most = max(most, sems.used)
        sems.used = most

    def __getattr__(self, name):
        def run():
            for order in (0, 1):
                pl.when(self.core == order)(getattr(self.variants[order], name))

        return run


def split_lanes(ref, h):
    halves = lane_halves(ref.shape[-1])
    return None if halves[h] is None else ref.at[:, pl.ds(*halves[h])]


def whole_ref(ref):
    return ref


def ring_row(own, out, cut, sems, kind=RingGather):
    x, y, z, c = place()

    def make(order):
        slot = (lambda k: cut(out.at[x, k])) if order == 0 else (lambda k: cut(out.at[k, z]))
        peer = (lambda k: device(x, y, k, c)) if order == 0 else (lambda k: device(k, y, z, c))
        return kind(own, slot, lambda k, h: split_lanes(slot(k), h), (z, x)[order], peer, sems)

    return Either(c, sems, make)


def ring_rest(out, cut, sems, lean=False, kind=RingGather):
    x, y, z, c = place()

    def make(order):
        if order == 0:
            slot, half, me = lambda k: cut(out.at[k]), lambda k, h: cut(out.at[k, pl.ds(2 * h, 2)]), x
        else:
            slot, half, me = lambda k: cut(out.at[:, k]), lambda k, h: cut(out.at[pl.ds(2 * h, 2), k]), z
            if lean:
                half = lambda k, h: slot(k) if h else None
        peer = (lambda k: device(k, y, z, c)) if order == 0 else (lambda k: device(x, y, k, c))
        return kind(slot(me), slot, half, me, peer, sems)

    return Either(c, sems, make)


class Crossing:
    def __init__(self, out, cut, other_cut, sems):
        x, y, z, c = place()
        self.pushes = []
        for d in range(4):

            def make(order, d=d):
                quarters = out.at[(x + d) % 4], out.at[:, (z + d) % 4]
                piece, lands = cut(quarters[order]), other_cut(quarters[1 - order])
                return Push(piece, piece, sems, device(x, y, z, 1 - c), lands)

            self.pushes.append(Either(c, sems, make))

    def start(self, d):
        self.pushes[d].start()

    def close(self):
        for push in self.pushes:
            push.arrived()
            push.sent()


def turn(values, cosine, sine):
    middle = values.shape[-1] // 2
    leading, trailing = values[:, :middle], values[:, middle:]
    return jnp.concatenate([leading * cosine - trailing * sine, trailing * cosine + leading * sine], axis=1)


def unit_rows(values):
    scale = lax.rsqrt(jnp.mean(values * values, axis=-1, keepdims=True) + EPSILON)
    return values * scale, scale


def allowed_keys(offset, beginning, rows, span):
    query = offset + lax.broadcasted_iota(jnp.int32, (rows, span), 0)
    key = offset + rows - span + lax.broadcasted_iota(jnp.int32, (rows, span), 1)
    return (key <= query) & (key > query - WINDOW) & (key >= beginning)


def gain_picks(each, width):
    lane = lax.broadcasted_iota(jnp.int32, (16, width), 1)
    owner = (lane * 7282) >> 16 if each == 9 else lane >> 1
    pick = lax.broadcasted_iota(jnp.int32, (16, width), 0) == lane - owner * each
    lane = lax.broadcasted_iota(jnp.int32, (128, width), 1)
    owner = (lane * 7282) >> 16 if each == 9 else lane >> 1
    owns = lax.broadcasted_iota(jnp.int32, (128, width), 0) == owner
    return pick.astype(jnp.float32).astype(jnp.bfloat16), owns.astype(jnp.float32)


def gain_row(table, first, pick, owns):
    spread = dot(table[:, first : first + 16], pick, 1, 0)
    return jnp.sum(spread * owns, axis=0, keepdims=True)


def lanes_of(start, size):
    return lambda ref: ref.at[(slice(None),) * (len(ref.shape) - 1) + (pl.ds(start, size),)]


def attend(number, stream, doc_starts, own_query, own_key, own_value, own_output, own_gate, own_up, own_down, norms):
    tokens = stream.shape[0]
    span = tokens + WINDOW

    low, wide = jnp.bfloat16, jnp.float32
    keep = dict(
        normed=((tokens, D), low),
        query=((HEADS * tokens, HEAD_DIM), wide),
        key=((tokens, HEAD_DIM), wide),
        turned=((HEADS * tokens, HEAD_DIM), low),
        kv=((span, 2 * HEAD_DIM), low),
        probs=((HEADS * tokens, span), wide),
        mixed=((tokens, HEADS * HEAD_DIM), low),
        branch=((tokens, D), wide),
        hidden=((tokens, D), wide),
        feed=((tokens, D), low),
        gains=((8, D), wide),
        cosine=((tokens, HEAD_DIM // 2), wide),
        sine=((tokens, HEAD_DIM // 2), wide),
        qkv_weight=((D, 1536), low),
        output_weight=((HEADS * HEAD_DIM, D), low),
    )

    def kernel(
        stream_in, starts_in, query_in, key_in, value_in, output_in, gate_in, up_in, down_in, *refs
    ):
        norms_in, refs = refs[: len(norms)], list(refs[len(norms) :])

        def take(count):
            taken, refs[:] = refs[:count], refs[count:]
            return taken

        saved = SimpleNamespace(**dict(zip(keep, take(len(keep)))))
        both_out, down_out, feeds_out = take(3)
        v = SimpleNamespace(**dict(zip(keep, take(len(keep)))))
        (
            query_give, kv_give, query_box, kv_box, both_box, both_give, flat, merge, query_own, kv_own, both_own, query_all, kv_all, output_all, kv,
            owns9, owns2,
            send, recv, here,
        ) = refs
        saves = []

        def save(src, dst):
            saves.append(pltpu.make_async_copy(src, dst, here.at[5 + len(saves)]))
            saves[-1].start()

        x, y, z, c = place()
        q, s = lax.axis_index("seq"), lax.axis_index("shard")
        sems = Sems(send, recv)
        after, before = {"seq": (q + 1) % 16, "shard": s}, {"seq": (q + 15) % 16, "shard": s}
        for j in range(8):
            flat[pl.ds(j, 9, 8), :] = query_in[:, 128 * j : 128 * (j + 1)].astype(jnp.float32)
        query_give[...] = flat[:72, :].astype(jnp.bfloat16)
        for at, source in enumerate((key_in, value_in)):
            for j in range(2):
                flat[pl.ds(2 * at + j, 9, 4), :] = source[:, 128 * j : 128 * (j + 1)].astype(jnp.float32)
        flat[36:40, :] = jnp.zeros((4, 128), jnp.float32)
        for g, source in enumerate(norms_in):
            flat[36:37, 16 * g : 16 * g + source.shape[1]] = source[...].astype(jnp.float32)
        kv_give[...] = flat[:40, :].astype(jnp.bfloat16)
        greet(
            [device(x, y + dy, z, (c + dc) % 2) for dy, dc in SHARD_STEPS]
            + [device(x, y, z + d, c) for d in (1, 2, 3)]
            + [device(x + d, y, z, c) for d in (1, 2, 3)]
            + [after, before]
        )
        sent = []

        def spread(source, box, pieces=False):
            pushes = []
            for dy, dc in SHARD_STEPS:
                to, back = (y + dy) % 4 * 2 + (c + dc) % 2, (y + 4 - dy) % 4 * 2 + (c + 2 - dc) % 2
                src = source.at[to] if pieces else source
                push = Push(src, box.at[s], sems, device(x, y + dy, z, (c + dc) % 2), box.at[back])
                push.start()
                pushes.append(push)
            box[s] = source[s] if pieces else source[...]
            sent.extend(pushes)
            return pushes

        def collect(pushes, box, own):
            for push in pushes:
                push.arrived()
            tiles = own.shape[-1] // 128
            for d in range(8):
                flat[: box.shape[1], :] = box[d].astype(jnp.float32)
                for j in range(tiles):
                    merge[9 * d : 9 * d + 9, 128 * j : 128 * (j + 1)] = flat[pl.ds(j, 9, tiles), :]
                if box.shape[1] > 9 * tiles:
                    for start in (0, 256):
                        merge[72 + d : 73 + d, start : start + 128] = flat[9 * tiles : 9 * tiles + 1, :]
            own[...] = merge[: own.shape[0], : own.shape[-1]].astype(own.dtype)

        def halves(size):
            return [lanes_of(pl.multiple_of(core * size, 128), size) for core in (c, 1 - c)]

        my_query, their_query = halves(512)
        my_kv, their_kv = halves(256)
        mine = lambda ref: ref.at[(slice(None),) * (len(ref.shape) - 3) + (s,)]

        got_kv = spread(kv_give, kv_box)
        got_query = spread(query_give, query_box)
        down_ring = ring_row(down_in, down_out, whole_ref, sems)
        output_ring = ring_row(output_in, output_all, mine, sems, DirectGather)
        down_ring.first()
        output_ring.first()
        inputs = stream_in[...].astype(jnp.float32)
        unit = unit_rows(inputs)[0]
        starts = starts_in[...]
        positions = q * tokens + lax.broadcasted_iota(jnp.int32, (tokens, 1), 0)
        beginning = jnp.zeros((tokens, 1), jnp.int32)
        for j in range(8):
            start = starts[0:1, j : j + 1]
            beginning = jnp.maximum(beginning, jnp.where(start <= positions, start, 0))
        steps = lax.broadcasted_iota(jnp.int32, (1, HEAD_DIM // 2), 1).astype(jnp.float32)
        angles = (positions - beginning).astype(jnp.float32) * jnp.exp(steps * (-2.0 * math.log(10000.0) / HEAD_DIM))
        v.cosine[...] = jnp.cos(angles)
        v.sine[...] = jnp.sin(angles)
        pick9, owns9[...] = gain_picks(9, D)
        pick2, owns2[...] = gain_picks(2, HEAD_DIM)
        v.gains[...] = jnp.zeros_like(v.gains)
        merge[...] = jnp.zeros_like(merge)
        for d in range(8):
            for half, source in enumerate((gate_in, up_in)):
                for i in range(16):
                    to, start = WIDE * half + SLOT * i, 8 * PIECE * i + PIECE * d
                    merge[0:9, to : to + PIECE] = source[:, start : start + PIECE].astype(jnp.float32)
            for j in range(14):
                flat[pl.ds(j, 9, 14), :] = merge[0:9, 128 * j : 128 * (j + 1)]
            both_give[d] = flat[:126, :].astype(jnp.bfloat16)

        own = lambda src, dst, at: pltpu.make_async_copy(src, dst, here.at[at])
        collect(got_kv, kv_box, kv_own)
        kv_ring = ring_row(my_kv(kv_own), kv_all, my_kv, sems, DirectGather)
        kv_ring.first()
        other = device(x, y, z, 1 - c)
        column = lambda k: output_all.at[:, :, k * 2 + c]
        output_y = RingGather(
            column(y), column, lambda k, h: output_all.at[pl.ds(2 * h, 2), :, k * 2 + c],
            y, lambda k: device(x, k, z, c), sems,
        )
        output_cross = [
            Push(column((y + d) % 4), column((y + d) % 4), sems, other, output_all.at[:, :, (y + d) % 4 * 2 + 1 - c])
            for d in range(4)
        ]
        own(output_in, output_all.at[x, z, s], 2).start()
        collect(got_query, query_box, query_own)
        query_ring = ring_row(my_query(query_own), query_all, my_query, sems)
        query_ring.first()
        output_ring.relay()
        output_ring.last()
        own(output_in, output_all.at[x, z, s], 2).wait()
        output_rest = ring_rest(output_all, mine, sems, kind=DirectGather)
        output_rest.first()
        got_both = spread(both_give, both_box, True)
        copies = [
            own(my_kv(kv_own), my_kv(kv_all.at[x, z]), 0),
            own(down_in, down_out.at[x, z], 1),
            own(my_query(query_own), my_query(query_all.at[x, z]), 3),
        ]
        for copy in copies:
            copy.start()
        down_ring.relay()
        kv_ring.relay()
        query_ring.relay()
        for copy in copies:
            copy.wait()
        kv_ring.last()
        kv_rest = ring_rest(kv_all, my_kv, sems, kind=DirectGather)
        kv_cross = Crossing(kv_all, my_kv, their_kv, sems)
        kv_rest.first()
        kv_cross.start(0)
        query_ring.last()
        query_rest = ring_rest(query_all, my_query, sems)
        query_cross = Crossing(query_all, my_query, their_query, sems)
        query_rest.first()
        query_cross.start(0)
        output_rest.relay()
        output_rest.last()
        output_y.first()
        output_cross[0].start()
        down_ring.last()
        down_rest = ring_rest(down_out, whole_ref, sems, True)
        kv_rest.relay()
        kv_cross.start(3)
        kv_cross.start(1)
        collect(got_both, both_box, both_own)
        both_ring = ring_row(both_own, both_out, whole_ref, sems)
        both_ring.first()
        both_copy = own(both_own, both_out.at[x, z], 4)
        both_copy.start()
        kv_rest.last()
        kv_cross.start(2)
        query_rest.relay()
        query_cross.start(3)
        query_cross.start(1)
        down_rest.first()
        table = kv_all[:, :, 72:80, pl.ds(pl.multiple_of(c * 256, 128), 128)].reshape(128, 128)
        for g in range(4):
            v.gains[g : g + 1, :] = gain_row(table, 16 * g, pick9, owns9[...])
        for g in range(2):
            v.gains[4 + g : 5 + g, :HEAD_DIM] = gain_row(table, 64 + 16 * g, pick2, owns2[...])
        normed = (unit * v.gains[0:1, :]).astype(jnp.bfloat16)
        v.normed[...] = normed

        def assemble(blocks, lanes):
            @pl.loop(0, 8)
            def _(i):
                pair = [blocks[i // 2, i % 2 * 2 + k, :72].astype(jnp.float32) for k in range(2)]
                rows = pl.ds(pl.multiple_of(144 * i, 144), 144)
                v.qkv_weight[rows, lanes] = jnp.concatenate(pair, axis=0).astype(jnp.bfloat16)

        kv_cross.close()
        assemble(kv_all, slice(1024, 1536))

        near = Push(kv.at[2], kv.at[1], sems, after)
        far = Push(kv.at[1], kv.at[0], sems, after)
        key_value = dot(normed, v.qkv_weight[:, 1024:], 1, 0)
        key = key_value[:, :HEAD_DIM]
        v.key[...] = key
        key_turned = turn(unit_rows(key)[0] * v.gains[5:6, :HEAD_DIM], v.cosine[...], v.sine[...])
        kv[2, :, :HEAD_DIM] = key_turned.astype(jnp.bfloat16)
        kv[2, :, HEAD_DIM:] = key_value[:, HEAD_DIM:].astype(jnp.bfloat16)
        near.start()
        output_y.relay()
        output_cross[1].start()
        output_cross[3].start()
        query_rest.last()
        query_cross.start(2)
        both_ring.relay()
        for src, dst in ((v.gains, saved.gains), (v.cosine, saved.cosine), (v.sine, saved.sine)):
            save(src, dst)
        query_cross.close()
        assemble(query_all, slice(0, 1024))
        save(v.qkv_weight, saved.qkv_weight)
        both_ring.last()
        both_copy.wait()
        both_rest = ring_rest(both_out, whole_ref, sems, True)
        both_rest.first()
        down_rest.relay()
        for h in range(HEADS):
            lanes = slice(h * HEAD_DIM, (h + 1) * HEAD_DIM)
            span_h = slice(h * tokens, (h + 1) * tokens)
            query = dot(normed, v.qkv_weight[:, lanes], 1, 0)
            v.query[span_h, :] = query
            turned = turn(unit_rows(query)[0] * v.gains[4:5, :HEAD_DIM], v.cosine[...], v.sine[...])
            v.turned[span_h, :] = turned.astype(jnp.bfloat16)
        save(v.query, saved.query)
        save(v.turned, saved.turned)
        save(v.normed, saved.normed)
        save(v.key, saved.key)
        near.arrived()
        far.start()
        both_rest.relay()
        output_y.last()
        output_cross[2].start()
        down_rest.last()
        for push in output_cross:
            push.arrived()

        @pl.loop(0, 16)
        def _(i):
            for j in range(4):
                pair = [output_all[i // 4, i % 4, 2 * j + k].astype(jnp.float32) for k in range(2)]
                rows = pl.ds(pl.multiple_of(64 * i + 16 * j, 16), 16)
                v.output_weight[rows, :] = jnp.concatenate(pair, axis=0).astype(jnp.bfloat16)

        save(v.output_weight, saved.output_weight)
        far.arrived()
        v.kv[...] = kv[...].reshape(span, 2 * HEAD_DIM)
        save(v.kv, saved.kv)
        allowed = allowed_keys(q * tokens, beginning, tokens, span)
        keys, values = v.kv[:, :HEAD_DIM], v.kv[:, HEAD_DIM:]
        rows = tokens // SUBS

        def attend_part(part):
            here_rows = slice(part * rows, (part + 1) * rows)
            for h in range(HEADS):
                span_h = slice(h * tokens + part * rows, h * tokens + (part + 1) * rows)
                scores = dot(v.turned[span_h, :], keys, 1, 1) * HEAD_DIM ** (-0.5)
                scores = jnp.where(allowed[here_rows], scores, NEGATIVE)
                exponent = jnp.exp(scores - jnp.max(scores, axis=-1, keepdims=True))
                probs = exponent / jnp.sum(exponent, axis=-1, keepdims=True)
                v.probs[span_h, :] = probs
                mixed = dot(probs.astype(jnp.bfloat16), values, 1, 0)
                v.mixed[here_rows, h * HEAD_DIM : (h + 1) * HEAD_DIM] = mixed.astype(jnp.bfloat16)
            branch = dot(v.mixed[here_rows, :], v.output_weight[...], 1, 0)
            v.branch[here_rows, :] = branch
            hidden = inputs[here_rows] + unit_rows(branch)[0] * v.gains[1:2, :]
            v.hidden[here_rows, :] = hidden
            v.feed[here_rows, :] = (unit_rows(hidden)[0] * v.gains[2:3, :]).astype(jnp.bfloat16)

        attend_part(0)
        first_rows = v.feed.at[pl.ds(0, rows)]
        block = lambda k: feeds_out.at[k * 2 + c]
        feed_y = RingGather(
            first_rows, block, lambda k, h: feeds_out.at[k * 2 + c, pl.ds(h * (rows // 2), rows // 2)],
            y, lambda k: device(x, k, z, c), sems,
        )
        feed_cross = [
            Push(
                first_rows if d == 0 else block((y + d) % 4), block((y + d) % 4), sems, other,
                feeds_out.at[(y + d) % 4 * 2 + 1 - c],
            )
            for d in range(4)
        ]
        feed_y.first()
        feed_cross[0].start()
        save(first_rows, feeds_out.at[s])
        attend_part(1)
        for src, dst in (
            (v.probs, saved.probs), (v.branch, saved.branch), (v.hidden, saved.hidden), (v.mixed, saved.mixed),
            (v.feed, saved.feed),
        ):
            save(src, dst)
        feed_y.relay()
        feed_cross[1].start()
        feed_cross[3].start()
        both_rest.last()
        feed_y.last()
        feed_cross[2].start()
        for push in feed_cross:
            push.arrived()
        rings = [query_ring, kv_ring, down_ring, output_ring, both_ring]
        rings += [query_rest, kv_rest, down_rest, output_rest, both_rest, output_y, feed_y]
        for ring in rings:
            ring.close()
        for push in sent + output_cross + feed_cross + [near, far]:
            push.sent()
        for copy in saves:
            copy.wait()

    outs = list(keep.values()) + [
        ((4, 4, 72, 2 * WIDE), low),
        ((4, 4, PIECE, D), low),
        ((8, tokens // SUBS, D), low),
    ]
    scratch = [pltpu.VMEM(shape, kind) for shape, kind in keep.values()] + [
        pltpu.VMEM((72, 128), low),
        pltpu.VMEM((40, 128), low),
        pltpu.VMEM((8, 72, 128), low),
        pltpu.VMEM((8, 40, 128), low),
        pltpu.VMEM((8, 126, 128), low),
        pltpu.VMEM((8, 126, 128), low),
        pltpu.VMEM((128, 128), wide),
        pltpu.VMEM((80, 2 * WIDE), wide),
        pltpu.VMEM((72, 1024), low),
        pltpu.VMEM((80, 512), low),
        pltpu.VMEM((72, 2 * WIDE), low),
        pltpu.VMEM((4, 4, 72, 1024), low),
        pltpu.VMEM((4, 4, 80, 512), low),
        pltpu.VMEM((4, 4, 8, 8, D), low),
        pltpu.VMEM((3, tokens, 2 * HEAD_DIM), low),
        pltpu.VMEM((128, D), wide),
        pltpu.VMEM((128, HEAD_DIM), wide),
    ]
    out = call(
        kernel, "attend", number, outs,
        [stream, doc_starts, own_query, own_key, own_value, own_output, own_gate, own_up, own_down, *norms],
        scratch, 3 * 7 + 11 * 4 + 2 * 4 + 4 + 2 + 4 + 4, in_specs=[VMEM] * (9 + len(norms)), local=5 + 16,
    )
    return SimpleNamespace(**dict(zip(keep, out))), out[len(keep) :]


def sum_row(total, boxes, sems, lean=False, kind=RingSum):
    x, y, z, c = place()

    def make(order):
        if order == 0:
            chunk, half = lambda k: total.at[:, k], lambda k, h: total.at[pl.ds(2 * h, 2), k]
            if lean:
                half = lambda k, h: None if h else chunk(k)
            me, peer = z, lambda k: device(x, y, k, c)
        else:
            chunk, half = lambda k: total.at[k], lambda k, h: total.at[k, pl.ds(2 * h, 2)]
            me, peer = x, lambda k: device(k, y, z, c)
        own_boxes = list(boxes)
        if order == 1 and lean:
            own_boxes[0] = boxes[0].at[pl.ds(0, 2)]
        return kind(chunk, half, own_boxes, me, peer, sems, add_into)

    return Either(c, sems, make)


def sum_rest(total, boxes, sems, kind=RingSum):
    x, y, z, c = place()

    def make(order):
        if len(total.shape) == 3:
            chunk = lambda k: total.at[k]
        else:
            chunk = (lambda k: total.at[k, z]) if order == 0 else (lambda k: total.at[x, k])
        half = lambda k, h: split_lanes(chunk(k), h)
        peer = (lambda k: device(k, y, z, c)) if order == 0 else (lambda k: device(x, y, k, c))
        return kind(chunk, half, boxes, (x, z)[order], peer, sems, add_into)

    return Either(c, sems, make)


def norm_grad(values, gain, grad):
    unit, scale = unit_rows(values)
    scaled = gain * grad
    return (
        scale * (scaled - unit * jnp.mean(unit * scaled, axis=-1, keepdims=True)),
        jnp.sum(grad * unit, axis=0, keepdims=True),
    )


def scatter_boxes(rows, width, kind, row_only=False, lean=False):
    lanes = lane_halves(width)
    rest = [pltpu.VMEM((rows, size), kind) for _, size in lanes] + [pltpu.VMEM((rows, width), kind)] * 2
    if row_only:
        return [pltpu.VMEM((4, rows, width), kind)] + rest
    return (
        [pltpu.VMEM((4, 4, rows, width), kind)]
        + [pltpu.VMEM((4 if lean else 2, rows, width), kind), pltpu.VMEM((2, rows, width), kind)]
        + [pltpu.VMEM((4, rows, width), kind)] * 2
        + rest
    )


BOTH, DOWN, OUTPUT, QUERY, KV = range(5)
SHARED = (OUTPUT, QUERY, KV)
GIVE, TAKE = 9, 10


def attend_back(number, arrays):
    tokens = arrays["hidden"].shape[0]
    span = tokens + WINDOW
    names = list(arrays)
    low, wide = jnp.bfloat16, jnp.float32
    results = dict(
        stream_grad=((tokens, D), low),
        both_rows=((8, 126, 128), low),
        query_grad=((9, 1024), wide),
        key_grad=((9, 256), wide),
        value_grad=((9, 256), wide),
        output_grad=((8, D), wide),
        down_grad=((PIECE, D), wide),
        sums=((8, D), wide),
    )
    sizes = {BOTH: (72, 2 * WIDE), DOWN: (PIECE, D), OUTPUT: (64, 640), QUERY: (72, 512), KV: (72, 256)}
    stores = []
    for name, (rows, width) in sizes.items():
        if name == KV:
            stores.append([pltpu.VMEM((4, 4, rows, width), low)] + [pltpu.VMEM((4, rows, width), low)] * 3)
            stores[-1] += [pltpu.VMEM((rows, width), low)] * 5
        else:
            stores.append(scatter_boxes(rows, width, low, name == DOWN, name == BOTH))
        if name in SHARED:
            stores[-1] += [pltpu.VMEM((4, 4, rows, width), low)] * 2
    room = SimpleNamespace(
        hidden_grad=pltpu.VMEM((tokens, D), wide),
        branch_low=pltpu.VMEM((tokens, D), low),
        mixed_grad=pltpu.VMEM((HEADS * tokens, HEAD_DIM), low),
        score_low=pltpu.VMEM((HEADS * tokens, span), low),
        probs_low=pltpu.VMEM((HEADS * tokens, span), low),
        kv_grad=pltpu.VMEM((span, 2 * HEAD_DIM), wide),
        halo_out=pltpu.VMEM((2, tokens, 2 * HEAD_DIM), low),
        halo_in=pltpu.VMEM((2, tokens, 2 * HEAD_DIM), low),
        qkv_low=pltpu.VMEM((tokens, 1536), low),
        term=pltpu.VMEM((D, 1024), wide),
        merge=pltpu.VMEM((72, 2 * WIDE), wide),
        flat=pltpu.VMEM((128, 128), wide),
        both_give=pltpu.VMEM((8, 126, 128), low),
        query_give=pltpu.VMEM((8, 36, 128), low),
        query_take=pltpu.VMEM((8, 36, 128), low),
        kv_give=pltpu.VMEM((8, 18, 128), low),
        kv_take=pltpu.VMEM((8, 18, 128), low),
        output_give=pltpu.VMEM((8, 8, 640), low),
        output_take=pltpu.VMEM((8, 8, 640), low),
        own_sums=pltpu.VMEM((3, 8, D), wide),
        shard_sums=pltpu.VMEM((8, 8, D), wide),
        z_sums=pltpu.VMEM((4, 8, D), wide),
        x_sums=pltpu.VMEM((4, 8, D), wide),
    )
    room = vars(room)
    held_names = names[:-2]

    def kernel(*refs):
        refs = list(refs)

        def take(count):
            taken, refs[:] = refs[:count], refs[count:]
            return taken

        given = dict(zip(names, take(len(names))))
        o = SimpleNamespace(**dict(zip(results, take(len(results)))))
        a = SimpleNamespace(**dict(zip(held_names, take(len(held_names)))))
        b = SimpleNamespace(**dict(zip(room, take(len(room)))))
        held = {n: take(len(store)) for n, store in zip(sizes, stores)}
        send, recv, here = refs
        x, y, z, c = place()
        q, s = lax.axis_index("seq"), lax.axis_index("shard")
        sems = Sems(send, recv)
        other = device(x, y, z, 1 - c)
        after, before = {"seq": (q + 1) % 16, "shard": s}, {"seq": (q + 15) % 16, "shard": s}
        rings = {}
        for n in sizes:
            if n == DOWN:
                rings[n] = None, sum_rest(held[n][0], held[n][1:5], sems)
            elif n == KV:
                one = sum_row(held[n][0], held[n][1:4], sems, kind=DirectSum)
                rings[n] = one, sum_rest(held[n][0], held[n][4:7], sems, kind=DirectSum)
            else:
                one = sum_row(held[n][0], held[n][1:5], sems, n == BOTH)
                rings[n] = one, sum_rest(held[n][0], held[n][5:9], sems)
        cross = {n: Push(held[n][GIVE], held[n][TAKE], sems, other) for n in SHARED}
        loads = [
            pltpu.make_async_copy(given[names[-2]], held[BOTH][0], here.at[0]),
            pltpu.make_async_copy(given[names[-1]], held[DOWN][0], here.at[1]),
        ]
        for at, name in enumerate(held_names):
            loads.append(pltpu.make_async_copy(given[name], getattr(a, name), here.at[2 + at]))
        for load in loads:
            load.start()
        greet(
            [device(x, y + dy, z, (c + dc) % 2) for dy, dc in SHARD_STEPS]
            + [device(x, y, z + d, c) for d in (1, 2, 3)]
            + [device(x + d, y, z, c) for d in (1, 2, 3)]
            + [after, before]
        )
        loads[0].wait()
        rings[BOTH][0].first()
        loads[1].wait()
        rings[DOWN][1].first()
        for load in loads[2:]:
            load.wait()
        gains = a.gains
        cosine, sine = a.cosine, a.sine
        own = b.own_sums.at[0]
        own[...] = jnp.zeros(own.shape, wide)
        pending = []

        upstream = a.cotangent[...].astype(wide)
        extra, own[2:3, :] = norm_grad(a.hidden[...], gains[2:3, :], a.feed_grad[...])
        hidden_grad = upstream + extra
        b.hidden_grad[...] = hidden_grad
        branch_grad, own[1:2, :] = norm_grad(a.branch[...], gains[1:2, :], hidden_grad)
        b.branch_low[...] = branch_grad.astype(low)
        own[3:4, :] = a.post_grad[...]
        for at, squares in enumerate((
            jnp.sum(jnp.square(a.stream[...].astype(wide)), axis=0, keepdims=True),
            jnp.sum(jnp.square(a.hidden[...]), axis=0, keepdims=True),
            a.result_squares[...],
        )):
            folded = functools.reduce(jnp.add, [squares[:, 128 * j : 128 * (j + 1)] for j in range(D // 128)])
            own[4:5, 512 + 128 * at : 640 + 128 * at] = folded
        for h in range(HEADS):
            rows, lanes = slice(h * tokens, (h + 1) * tokens), slice(h * HEAD_DIM, (h + 1) * HEAD_DIM)
            b.mixed_grad[rows, :] = dot(b.branch_low[...], a.output_weight[lanes, :], 1, 1).astype(low)
        keys, values = a.kv[:, :HEAD_DIM], a.kv[:, HEAD_DIM:]
        for h in range(HEADS):
            rows = slice(h * tokens, (h + 1) * tokens)
            probs = a.probs[rows, :]
            prob_grad = dot(b.mixed_grad[rows, :], values, 1, 1)
            inner = jnp.sum(probs * prob_grad, axis=-1, keepdims=True)
            b.score_low[rows, :] = (probs * (prob_grad - inner) * HEAD_DIM ** (-0.5)).astype(low)
            b.probs_low[rows, :] = probs.astype(low)
        b.kv_grad[:, :HEAD_DIM] = dot(b.score_low[...], a.turned[...], 0, 0)
        b.kv_grad[:, HEAD_DIM:] = dot(b.probs_low[...], b.mixed_grad[...], 0, 0)

        halo_far = Push(b.halo_out.at[0], b.halo_in.at[0], sems, before)
        halo_near = Push(b.halo_out.at[1], b.halo_in.at[1], sems, before)
        b.halo_out[0] = b.kv_grad[:tokens, :].astype(low)
        halo_far.start()

        gain_grad = jnp.zeros((1, HEAD_DIM), wide)
        for h in range(HEADS):
            rows, lanes = slice(h * tokens, (h + 1) * tokens), slice(h * HEAD_DIM, (h + 1) * HEAD_DIM)
            turned_grad = dot(b.score_low[rows, :], keys, 1, 0)
            back = turn(turned_grad, cosine[...], -sine[...])
            grad, extra = norm_grad(a.query[rows, :], gains[4:5, :HEAD_DIM], back)
            gain_grad += extra
            b.qkv_low[:, lanes] = grad.astype(low)
        own[4:5, :HEAD_DIM] = gain_grad

        def term(start, width, give, take):
            out = b.term

            @pl.loop(0, D // 128)
            def _(i):
                lanes = pl.ds(pl.multiple_of(i * 128, 128), 128)
                out[lanes, : 2 * width] = dot(a.normed[:, lanes], b.qkv_low[:, start : start + 2 * width], 0, 0)

            @pl.loop(0, 16)
            def _(i):
                rows = pl.ds(pl.multiple_of(72 * i, 8), 72)
                for ref, core in ((take, c), (give, 1 - c)):
                    lanes = pl.ds(pl.multiple_of(core * width, 128), width)
                    ref[i // 4, i % 4] = out[rows, lanes].astype(low)

        term(0, 512, held[QUERY][GIVE], held[QUERY][0])
        cross[QUERY].start()

        @pl.loop(0, 8)
        def _(i):
            lanes = pl.ds(pl.multiple_of(i * 128, 128), 128)
            part = dot(a.mixed[:, lanes], b.branch_low[...], 0, 0).astype(low)
            for k in range(2):
                block = (2 * i + k) // 4, (2 * i + k) % 4
                for core in range(2):
                    lanes_out = slice(512 * core, 512 * core + 640)
                    value = part[64 * k : 64 * (k + 1), lanes_out]

                    @pl.when(c == core)
                    def _():
                        held[OUTPUT][0][block] = value

                    @pl.when(c != core)
                    def _():
                        held[OUTPUT][GIVE][block] = value

        cross[OUTPUT].start()
        rings[BOTH][0].second()
        rings[DOWN][1].second()
        halo_far.arrived()
        b.halo_out[1] = (b.kv_grad[tokens : 2 * tokens, :] + b.halo_in[0].astype(wide)).astype(low)
        halo_near.start()
        for n in (QUERY, OUTPUT):
            cross[n].arrived()
            add_into(held[n][0], held[n][TAKE])
            rings[n][0].first()
        halo_near.arrived()
        kv_grad = b.kv_grad[2 * tokens :, :] + b.halo_in[1].astype(wide)
        back = turn(kv_grad[:, :HEAD_DIM], cosine[...], -sine[...])
        grad, own[4:5, HEAD_DIM : 2 * HEAD_DIM] = norm_grad(a.key[...], gains[5:6, :HEAD_DIM], back)
        b.qkv_low[:, 1024:1280] = grad.astype(low)
        b.qkv_low[:, 1280:] = kv_grad[:, HEAD_DIM:].astype(low)
        term(1024, 256, held[KV][GIVE], held[KV][0])
        cross[KV].start()
        for n in (QUERY, OUTPUT):
            rings[n][0].second()
        cross[KV].arrived()
        add_into(held[KV][0], held[KV][TAKE])
        rings[KV][0].first()
        rings[BOTH][0].third()
        rings[BOTH][1].first()
        normed_grad = dot(b.qkv_low[...], a.qkv_weight[...], 1, 1)
        extra, own[0:1, :] = norm_grad(a.stream[...].astype(wide), gains[0:1, :], normed_grad)
        o.stream_grad[...] = (b.hidden_grad[...] + extra).astype(low)

        def all_sum(stage, box, me, steps, target):
            source = b.own_sums.at[stage]
            pushes = []
            for to, back in steps:
                push = Push(source, box.at[me], sems, target(to), box.at[back])
                push.start()
                pushes.append(push)
            pending.extend(pushes)
            box[me] = source[...]

            def finish():
                for push in pushes:
                    push.arrived()
                return functools.reduce(jnp.add, [box[k] for k in range(box.shape[0])])

            return finish

        steps = []
        for dy, dc in SHARD_STEPS:
            there = (y + dy) % 4, (c + dc) % 2
            steps.append((there, (y + 4 - dy) % 4 * 2 + (c + 2 - dc) % 2))
        finish = all_sum(0, b.shard_sums, s, steps, lambda t: device(x, t[0], z, t[1]))
        rings[KV][0].second()
        for n in (QUERY, OUTPUT):
            rings[n][0].third()
            rings[n][1].first()
        rings[BOTH][1].second()
        rings[DOWN][1].third()
        b.own_sums[1] = finish()
        turns = lambda at: [((at + d) % 4, (at + 4 - d) % 4) for d in (1, 2, 3)]
        finish = all_sum(1, b.z_sums, z, turns(z), lambda t: device(x, y, t, c))
        rings[KV][0].third()
        rings[KV][1].first()
        for n in (QUERY, OUTPUT):
            rings[n][1].second()

        def spread(source, box):
            pushes = []
            for dy, dc in SHARD_STEPS:
                to, back = (y + dy) % 4 * 2 + (c + dc) % 2, (y + 4 - dy) % 4 * 2 + (c + 2 - dc) % 2
                push = Push(source.at[to], box.at[s], sems, device(x, y + dy, z, (c + dc) % 2), box.at[back])
                push.start()
                pushes.append(push)
            box[s] = source[s]
            pending.extend(pushes)
            return pushes

        def flatten(block, give):
            width = block.shape[-1]
            tiles = width // 128
            merge, flat = b.merge, b.flat
            merge[:, :width] = block[...].astype(wide)
            for d in range(8):
                for j in range(tiles):
                    flat[pl.ds(j, 9, tiles), :] = merge[9 * d : 9 * d + 9, 128 * j : 128 * (j + 1)]
                give[d] = flat[: 9 * tiles, :].astype(low)

        def unflatten(value, tiles, write):
            b.flat[: 9 * tiles, :] = value
            for j in range(tiles):
                write(j, b.flat[pl.ds(j, 9, tiles), :])

        rings[KV][1].second()
        rings[BOTH][1].third()
        flatten(held[BOTH][0].at[x, z], b.both_give)
        got_both = spread(b.both_give, o.both_rows)
        for n in (QUERY, OUTPUT):
            rings[n][1].third()
        b.own_sums[2] = finish()
        finish = all_sum(2, b.x_sums, x, turns(x), lambda t: device(t, y, z, c))
        flatten(held[QUERY][0].at[x, z], b.query_give)
        got_query = spread(b.query_give, b.query_take)
        for d in range(8):
            b.output_give[d] = held[OUTPUT][0][x, z, 8 * d : 8 * d + 8, :]
        got_output = spread(b.output_give, b.output_take)
        rings[KV][1].third()
        flatten(held[KV][0].at[x, z], b.kv_give)
        got_kv = spread(b.kv_give, b.kv_take)
        o.down_grad[...] = held[DOWN][0][x + c * (z + 4 - x) - 4 * c].astype(wide)
        o.sums[...] = finish()

        def over_y(box, core):
            return functools.reduce(jnp.add, [box[2 * k + core].astype(wide) for k in range(4)])

        for push in got_query:
            push.arrived()
        for core in range(2):
            def write(j, value, core=core):
                o.query_grad[:, 512 * core + 128 * j : 512 * core + 128 * (j + 1)] = value

            unflatten(over_y(b.query_take, core), 4, write)
        for push in got_output:
            push.arrived()
        o.output_grad[:, :512] = over_y(b.output_take, 0)[:, :512]
        o.output_grad[:, 512:] = over_y(b.output_take, 1)
        for push in got_kv:
            push.arrived()
        for core, out in enumerate((o.key_grad, o.value_grad)):
            def write(j, value, out=out):
                out[:, 128 * j : 128 * (j + 1)] = value

            unflatten(over_y(b.kv_take, core), 2, write)
        for push in got_both:
            push.arrived()
        for pair in rings.values():
            for ring in pair:
                if ring is not None:
                    ring.close()
        for push in list(cross.values()) + pending + [halo_far, halo_near]:
            push.sent()

    ins = list(arrays.values())
    out = call(
        kernel, "attend_back", number, list(results.values()), ins, [pltpu.VMEM(arrays[n].shape, arrays[n].dtype) for n in held_names] + list(room.values()) + sum(stores, []), 4 * 8 + 4 + 3 + 2 + 13 + 28,
        out_specs=[VMEM] * len(results), local=len(ins),
    )
    return dict(zip(results, out))


def finish(both_rows, sums, *arrays):
    def kernel(rows, sums, *refs):
        sources, refs = refs[: len(arrays)], refs[len(arrays) :]
        gate, up, *small = refs[:9]
        copies, (merge, flat) = refs[9:-2], refs[-2:]
        own = lax.axis_index("seq") * 8 + lax.axis_index("shard")
        for g in range(4):
            small[g][...] = pltpu.roll(sums[...], D - 9 * own, 1)[g : g + 1, :9]
        for g in range(2):
            start = HEAD_DIM * g + 2 * own
            small[4 + g][...] = pltpu.roll(sums[...], D - start, 1)[4:5, :2]
        for at in range(3):
            total = jnp.sum(sums[4:5, 512 + 128 * at : 640 + 128 * at], axis=1, keepdims=True)
            small[6][:, at : at + 1] = jnp.sqrt(total / (32768 * D))
        for source, copy in zip(sources, copies):
            copy[...] = source[...]
        for d in range(8):
            flat[:126, :] = rows[d].astype(jnp.float32)
            for j in range(14):
                merge[0:9, 128 * j : 128 * (j + 1)] = flat[pl.ds(j, 9, 14), :]
            for half, out in enumerate((gate, up)):
                for i in range(16):
                    start, to = WIDE * half + SLOT * i, 8 * PIECE * i + PIECE * d
                    out[:, to : to + PIECE] = merge[0:9, start : start + PIECE]

    return pl.pallas_call(
        kernel,
        name="finish",
        out_shape=[jax.ShapeDtypeStruct((9, FF), jnp.float32)] * 2
        + [jax.ShapeDtypeStruct((1, n), jnp.float32) for n in (9, 9, 9, 9, 2, 2, 3)]
        + [jax.ShapeDtypeStruct(a.shape, a.dtype) for a in arrays],
        in_specs=[VMEM] * (2 + len(arrays)),
        out_specs=[VMEM] * (9 + len(arrays)),
        scratch_shapes=[pltpu.VMEM((16, 2 * WIDE), jnp.float32), pltpu.VMEM((128, 128), jnp.float32)],
        compiler_params=pltpu.CompilerParams(vmem_limit_bytes=60 * MIB),
    )(both_rows, sums, *arrays)


def local(
    stream, doc_starts, cotangent, attention_norm, query_weight, key_weight, value_weight, query_norm, key_norm,
    output_weight, attention_post_norm, mlp_norm, gate_weight, up_weight, down_weight, mlp_post_norm,
):
    norms = (attention_norm, attention_post_norm, mlp_norm, mlp_post_norm, query_norm, key_norm)
    ahead, (both16, down16, feeds_a) = attend(
        0, stream[0], doc_starts, query_weight, key_weight, value_weight, output_weight, gate_weight, up_weight,
        down_weight, [norm[None] for norm in norms],
    )

    block_output, feed_grad, gain_mlp_post_grad, result_squares, both_term, down_row = feed_forward(
        1, ahead.feed, feeds_a, both16.reshape(D, 2 * WIDE), down16, ahead.hidden, cotangent[0], ahead.gains
    )

    named = vars(ahead)
    del named["feed"]
    back = SimpleNamespace(**attend_back(
        2,
        dict(
            **named, feed_grad=feed_grad, cotangent=cotangent[0], stream=stream[0],
            post_grad=gain_mlp_post_grad, result_squares=result_squares,
            both_term=both_term.reshape(4, 4, 72, 2 * WIDE),
            down_row=down_row,
        ),
    ))

    gate_grad, up_grad, *rest = finish(
        back.both_rows, back.sums, block_output, back.stream_grad, back.query_grad, back.key_grad, back.value_grad,
        back.output_grad, back.down_grad,
    )
    small, (block_output, stream_grad, query_grad, key_grad, value_grad, output_grad, down_grad) = rest[:7], rest[7:]
    input_gain, post_gain, mlp_gain, mlp_post_gain, query_gain, key_gain, stream_rms = [value[0] for value in small]
    return (
        block_output[None],
        stream_grad[None],
        input_gain,
        query_grad,
        key_grad,
        value_grad,
        query_gain,
        key_gain,
        output_grad,
        post_gain,
        mlp_gain,
        gate_grad,
        up_grad,
        down_grad,
        mlp_post_gain,
        stream_rms,
    )


def solution(mesh):
    rows = P(("seq", "shard"))
    tokens = P("shard", "seq", None)
    table = P(("seq", "shard"), None)
    return jax.shard_map(
        local,
        mesh=mesh,
        in_specs=(
            tokens, P("shard", None), tokens, rows, table, table, table, rows, rows, table, rows, rows, table, table,
            table, rows,
        ),
        out_specs=(
            tokens, tokens, rows, table, table, table, rows, rows, table, rows, rows, table, table, table, rows, P(),
        ),
        check_vma=False,
    )
```

```python
import functools
import math
from types import SimpleNamespace

import jax
import jax.numpy as jnp
from jax import lax
from jax.experimental import pallas as pl
from jax.experimental.pallas import tpu as pltpu
from jax.sharding import PartitionSpec as P

D = 1152
HEADS = 4
HEAD_DIM = 256
WINDOW = 512
FF = 6912
PIECE = 54
SLOT = 56
WIDE = 16 * SLOT

EPSILON = 1e-06
NEGATIVE = -1e30
MESH = pl.DeviceIdType.MESH
MIB = 2**20


def place():
    q, s = lax.axis_index("seq"), lax.axis_index("shard")
    return q // 4, s // 2, q % 4, s % 2


def device(x, y, z, c):
    return {"seq": x % 4 * 4 + z % 4, "shard": y % 4 * 2 + c}


def greet(targets):
    barrier = pltpu.get_barrier_semaphore()
    for target in targets:
        pl.semaphore_signal(barrier, inc=1, device_id=target, device_id_type=MESH)
    pl.semaphore_wait(barrier, len(targets))


class Sems:
    def __init__(self, send, recv):
        self.send, self.recv, self.used = send, recv, 0

    def take(self):
        self.used += 1
        return self.send.at[self.used - 1], self.recv.at[self.used - 1]


class Push:
    def __init__(self, src, dst, sems, to, lands=None):
        send, recv = sems.take()
        self.out = pltpu.make_async_remote_copy(
            src_ref=src, dst_ref=dst, send_sem=send, recv_sem=recv, device_id=to, device_id_type=MESH
        )
        lands = dst if lands is None else lands
        self.back = pltpu.make_async_remote_copy(
            src_ref=lands, dst_ref=lands, send_sem=send, recv_sem=recv, device_id=to, device_id_type=MESH
        )

    def start(self):
        self.out.start()

    def arrived(self):
        self.back.wait_recv()

    def sent(self):
        self.out.wait_send()


class RingGather:
    def __init__(self, own, slot, half, me, peer, sems):
        up, down, far = (me + 1) % 4, (me + 3) % 4, (me + 2) % 4
        self.right = Push(own, slot(me), sems, peer(up), slot(down))
        self.left = Push(own, slot(me), sems, peer(down), slot(up))
        split = half(down, 0)
        self.right2 = None if split is None else Push(split, split, sems, peer(up), half(far, 0))
        split = half(up, 1)
        self.left2 = None if split is None else Push(split, split, sems, peer(down), half(far, 1))

    def first(self):
        self.right.start()
        self.left.start()

    def relay(self):
        self.right.arrived()
        if self.right2 is not None:
            self.right2.start()
        self.left.arrived()
        if self.left2 is not None:
            self.left2.start()

    def last(self):
        if self.right2 is not None:
            self.right2.arrived()
        if self.left2 is not None:
            self.left2.arrived()

    def close(self):
        for push in (self.right, self.left, self.right2, self.left2):
            if push is not None:
                push.sent()


class DirectGather:
    def __init__(self, own, slot, half, me, peer, sems):
        self.pushes = [
            Push(own, slot(me), sems, peer((me + d) % 4), slot((me + 4 - d) % 4)) for d in (1, 3, 2)
        ]

    def first(self):
        for push in self.pushes:
            push.start()

    def relay(self):
        for push in self.pushes[:2]:
            push.arrived()

    def last(self):
        self.pushes[2].arrived()

    def close(self):
        for push in self.pushes:
            push.sent()


class DirectSum:
    def __init__(self, chunk, half, inbox, me, peer, sems, add):
        self.total, self.inbox, self.add = chunk(me), inbox[:3], add
        self.pushes = [
            Push(chunk((me + d) % 4), box, sems, peer((me + d) % 4)) for d, box in zip((2, 1, 3), self.inbox)
        ]

    def first(self):
        for push in self.pushes:
            push.start()

    def second(self):
        pass

    def third(self):
        for push, box in zip(self.pushes, self.inbox):
            push.arrived()
            self.add(self.total, box)

    def close(self):
        for push in self.pushes:
            push.sent()


class RingSum:
    def __init__(self, chunk, half, inbox, me, peer, sems, add):
        up, down, far = (me + 1) % 4, (me + 3) % 4, (me + 2) % 4
        self.chunk, self.half, self.inbox, self.add = chunk, half, inbox, add
        self.me, self.up, self.down = me, up, down
        near_a, near_b, right, left = inbox
        self.far_a = Push(half(far, 0), near_a, sems, peer(up))
        split = half(far, 1)
        self.far_b = None if split is None else Push(split, near_b, sems, peer(down))
        self.right = Push(chunk(up), right, sems, peer(up))
        self.left = Push(chunk(down), left, sems, peer(down))

    def first(self):
        self.far_a.start()
        if self.far_b is not None:
            self.far_b.start()

    def second(self):
        self.far_a.arrived()
        self.add(self.half(self.up, 0), self.inbox[0])
        self.right.start()
        if self.far_b is not None:
            self.far_b.arrived()
            self.add(self.half(self.down, 1), self.inbox[1])
        self.left.start()

    def third(self):
        self.right.arrived()
        self.add(self.chunk(self.me), self.inbox[2])
        self.left.arrived()
        self.add(self.chunk(self.me), self.inbox[3])

    def close(self):
        for push in (self.far_a, self.far_b, self.right, self.left):
            if push is not None:
                push.sent()


def add_into(total, extra):
    if len(total.shape) == 2:
        summed = total[...].astype(jnp.float32) + extra[...].astype(jnp.float32)
        total[...] = summed.astype(total.dtype)
        return

    @pl.loop(0, total.shape[0])
    def _(step):
        add_into(total.at[step], extra.at[step])


ANY = pl.BlockSpec(memory_space=pl.ANY)
VMEM = pl.BlockSpec(memory_space=pltpu.VMEM)


def call(kernel, name, number, outs, ins, scratch, copies, in_specs=None, out_specs=None, local=0, aliases=None):
    outs = [jax.ShapeDtypeStruct(shape, dtype) for shape, dtype in outs]
    scratch = list(scratch) + [pltpu.SemaphoreType.DMA((copies,)), pltpu.SemaphoreType.DMA((copies,))]
    if local:
        scratch.append(pltpu.SemaphoreType.DMA((local,)))
    return pl.pallas_call(
        kernel,
        name=name,
        out_shape=outs,
        in_specs=in_specs or [ANY] * len(ins),
        out_specs=out_specs or [ANY] * len(outs),
        scratch_shapes=scratch,
        input_output_aliases=aliases or {},
        compiler_params=pltpu.CompilerParams(
            collective_id=number, has_side_effects=True, vmem_limit_bytes=60 * MIB
        ),
    )(*ins)


SHARD_STEPS = [(dy, dc) for dy in range(4) for dc in range(2) if dy or dc]


def lane_halves(width):
    low = width // 256 * 128 if width % 256 == 0 else (width // 128 + 1) // 2 * 128
    return ((0, low), (low, width - low)) if width > 128 else ((0, width), None)


def dot(a, b, contract_a, contract_b):
    return lax.dot_general(a, b, (((contract_a,), (contract_b,)), ((), ())), preferred_element_type=jnp.float32)


SUBS = 2
BACK = (0, 1, 3, 2)


def gelu_terms(gate):
    a, b = math.sqrt(2.0 / math.pi), 0.044715
    square = gate * gate
    bend = jnp.tanh(a * gate * (1.0 + b * square))
    half = 0.5 * (1.0 + bend)
    slope = half + 0.5 * gate * (1.0 - bend * bend) * a * (1.0 + 3.0 * b * square)
    return gate * half, slope


def feed_forward(number, feed, feeds_a, full_both, down16, hidden, cotangent, gains):
    tokens, width = feed.shape
    rows = tokens // SUBS
    half = rows // 2

    def kernel(
        feed_in, feeds_in, both_in, down_in, hidden_in, cotangent_in, gains_in,
        block_out, feed_out, gain_out, square_out, both_out, down_out,
        feeds, downs, both, active, part, inbox, near, right, left, w_both, w_down, raw, pad, both_term, down_term,
        far_a, far_b, right4, left4, send, recv, here,
    ):
        x, y, z, c = place()
        sems = Sems(send, recv)
        other = device(x, y, z, 1 - c)
        to = lambda d: device(x, y + d, z, c)
        span = lambda s: pl.ds(s * rows, rows)
        a, b = 0, 1
        loads = [
            pltpu.make_async_copy(feeds_in, feeds.at[a], here.at[0]),
            pltpu.make_async_copy(both_in, w_both, here.at[1]),
            pltpu.make_async_copy(down_in, raw, here.at[2]),
            pltpu.make_async_copy(feed_in.at[span(b)], feeds.at[b, y * 2 + c], here.at[3]),
        ]
        for load in loads:
            load.start()
        greet(
            [to(1), to(3), other, device(x, y, z + 1, c), device(x, y, z + 3, c)]
            + [device(x + 1, y, z, c), device(x + 3, y, z, c)]
        )

        def gather(source, blocks, s):
            slot = lambda k: blocks.at[s, k * 2 + c]
            ring = RingGather(
                source, slot, lambda k, h: blocks.at[s, k * 2 + c, pl.ds(h * half, half)],
                y, lambda k: device(x, k, z, c), sems,
            )
            cross = []
            for d in range(4):
                k = (y + d) % 4
                cross.append(
                    Push(source if d == 0 else slot(k), slot(k), sems, other, blocks.at[s, k * 2 + 1 - c])
                )

            def first():
                ring.first()
                cross[0].start()

            def relay():
                ring.relay()
                cross[1].start()
                cross[3].start()

            def last():
                ring.last()
                cross[2].start()

            def close():
                ring.close()
                for push in cross:
                    push.sent()

            return first, relay, last, [push.arrived for push in cross], close

        class Total:
            def __init__(self, s):
                self.s = s
                self.cross = {}
                for d in range(4):
                    k = (y + d) % 4
                    self.cross[d] = Push(part.at[s, k * 2 + 1 - c], inbox.at[s, d], sems, other)
                self.own = lambda d: part.at[s, (y + d) % 4 * 2 + c]
                self.far_a = Push(self.own(2).at[pl.ds(0, half)], near.at[s, 0], sems, to(1))
                self.far_b = Push(self.own(2).at[pl.ds(half, half)], near.at[s, 1], sems, to(3))
                self.right = Push(self.own(1), right.at[s], sems, to(1))
                self.left = Push(self.own(3), left.at[s], sems, to(3))

            def far(self):
                self.cross[2].arrived()
                add_into(self.own(2), inbox.at[self.s, 2])
                self.far_a.start()
                self.far_b.start()

            def sides(self):
                for d in (1, 3):
                    self.cross[d].arrived()
                    add_into(self.own(d), inbox.at[self.s, d])

            def go(self):
                self.far_a.arrived()
                add_into(self.own(1).at[pl.ds(0, half)], near.at[self.s, 0])
                self.right.start()
                self.far_b.arrived()
                add_into(self.own(3).at[pl.ds(half, half)], near.at[self.s, 1])
                self.left.start()

            def final(self):
                self.cross[0].arrived()
                self.right.arrived()
                self.left.arrived()
                s = self.s
                pieces = (self.own(0), inbox.at[s, 0], right.at[s], left.at[s])
                return functools.reduce(jnp.add, [p[...].astype(jnp.float32) for p in pieces])

            def close(self):
                for push in list(self.cross.values()) + [self.far_a, self.far_b, self.right, self.left]:
                    push.sent()

        def steps(body, before, totals):
            @pl.loop(0, 4 * SUBS)
            def _(t):
                for at, hook in before.items():
                    pl.when(t == at)(hook)
                s, i = t // 4, t % 4
                d = i + i // 2 - i // 3 * 2
                body(s, pl.ds((y + d) % 4 * 2, 2))
                for at in range(4 * SUBS):
                    push = totals[at // 4].cross[BACK[at % 4]]
                    pl.when(t == at)(push.start)

        def flat(value):
            return value.reshape(2 * rows, value.shape[-1])

        def pair(value):
            return value.reshape(2, rows, value.shape[-1])

        def forward(s, chip):
            sums = dot(flat(feeds[s, chip]), w_both[...], 1, 0)
            both[s, chip] = pair(sums.astype(jnp.bfloat16))
            bent, _ = gelu_terms(sums[:, :WIDE])
            low = (bent * sums[:, WIDE:]).astype(jnp.bfloat16)
            active[s, chip] = pair(low)
            part[s, chip] = pair(dot(low, w_down[...], 1, 0).astype(jnp.bfloat16))

        def backward(s, chip):
            grad = dot(flat(downs[s, chip]), w_down[...], 1, 1)
            sums = flat(both[s, chip]).astype(jnp.float32)
            bent, slope = gelu_terms(sums[:, :WIDE])
            gate_grad = (grad * sums[:, WIDE:] * slope).astype(jnp.bfloat16)
            up_grad = (grad * bent).astype(jnp.bfloat16)
            both[s, chip, :, :WIDE] = pair(gate_grad)
            both[s, chip, :, WIDE:] = pair(up_grad)
            part[s, chip] = pair(dot(flat(both[s, chip]), w_both[...], 1, 1).astype(jnp.bfloat16))

        gain_out[...] = jnp.zeros_like(gain_out)
        square_out[...] = jnp.zeros_like(square_out)

        def norm_back(total, s):
            down = total.final()
            gain_row = gains_in[3:4, :]
            upstream = cotangent_in[span(s), :].astype(jnp.float32)
            scale = lax.rsqrt(jnp.mean(down * down, axis=-1, keepdims=True) + EPSILON)
            unit = down * scale
            result = hidden_in[span(s), :] + unit * gain_row
            block_out[span(s), :] = result.astype(jnp.bfloat16)
            square_out[...] += jnp.sum(result * result, axis=0, keepdims=True)
            gain_out[...] += jnp.sum(upstream * unit, axis=0, keepdims=True)
            scaled = gain_row * upstream
            grad = scale * (scaled - unit * jnp.mean(unit * scaled, axis=-1, keepdims=True))
            downs[s, y * 2 + c] = grad.astype(jnp.bfloat16)

        first_b, relay_b, last_b, met_b, close_b = gather(feed_in.at[span(b)], feeds, b)
        sum_a, sum_b = Total(a), Total(b)
        first_b()
        pad[...] = jnp.zeros_like(pad)
        for load in loads:
            load.wait()

        @pl.loop(0, 8)
        def _(i):
            for k in range(2):
                pad[SLOT * k : SLOT * k + PIECE, :] = raw[i // 2, i % 2 * 2 + k].astype(jnp.float32)
            w_down[pl.ds(pl.multiple_of(2 * SLOT * i, 16), 2 * SLOT), :] = pad[...].astype(jnp.bfloat16)

        def at_4():
            sum_a.far()
            met_b[0]()

        def at_5():
            last_b()
            sum_a.sides()
            met_b[1]()

        def at_6():
            sum_a.go()
            met_b[3]()

        steps(forward, {3: relay_b, 4: at_4, 5: at_5, 6: at_6, 7: met_b[2]}, (sum_a, sum_b))
        sum_b.far()
        norm_back(sum_a, a)
        sum_a.close()
        first_a, relay_a, last_a, met_a, close_a = gather(downs.at[a, y * 2 + c], downs, a)
        first_a()
        sum_b.sides()
        sum_b.go()
        old_b, old_close_b = sum_b, close_b
        first_b, relay_b, last_b, met_b, close_b = gather(downs.at[b, y * 2 + c], downs, b)
        sum_a, sum_b = Total(a), Total(b)

        def down_terms(s):
            every = 8 * rows

            @pl.loop(0, WIDE // 128)
            def _(i):
                units = pl.ds(pl.multiple_of(i * 128, 128), 128)
                value = dot(active[s, :, :, units].reshape(every, 128), downs[s].reshape(every, width), 0, 0)
                if s == b:
                    value += down_term[units, :].astype(jnp.float32)
                down_term[units, :] = value.astype(jnp.bfloat16)

        def both_terms(s, low=0, high=width // 128):
            every = 8 * rows

            @pl.loop(low, high)
            def _(i):
                lanes = pl.ds(pl.multiple_of(i * 128, 128), 128)
                value = dot(feeds[s, :, :, lanes].reshape(every, 128), both[s].reshape(every, 2 * WIDE), 0, 0)
                if s == b:
                    value += both_term[lanes, :].astype(jnp.float32)
                both_term[lanes, :] = value.astype(jnp.bfloat16)

        def back_1():
            relay_a()
            met_a[1]()

        def back_2():
            last_a()
            met_a[3]()

        def back_4():
            norm_back(old_b, b)
            old_b.close()
            old_close_b()
            first_b()
            sum_a.far()
            met_b[0]()

        def back_5():
            down_terms(a)
            sum_a.sides()
            relay_b()
            both_terms(a)
            sum_a.go()
            last_b()
            met_b[1]()

        down_ring = sum_row(raw, (far_a, far_b, right4, left4), sems)

        def start_down():
            down_terms(b)

            @pl.loop(0, 8)
            def _(i):
                both_slots = down_term[pl.ds(pl.multiple_of(2 * SLOT * i, 16), 2 * SLOT), :].astype(jnp.float32)
                for k in range(2):
                    slot = both_slots[SLOT * k : SLOT * k + PIECE].astype(jnp.bfloat16)
                    raw[i // 2, i % 2 * 2 + k] = slot

            down_ring.first()

        steps(
            backward,
            {0: met_a[0], 1: back_1, 2: back_2, 3: met_a[2], 4: back_4, 5: back_5, 6: met_b[3], 7: met_b[2]},
            (sum_a, sum_b),
        )
        sum_b.far()
        sum_b.sides()
        start_down()
        sum_b.go()
        feed_out[span(a), :] = sum_a.final()
        both_terms(b, 0, 4)
        down_ring.second()
        both_terms(b, 4)
        save = pltpu.make_async_copy(both_term, both_out, here.at[1])
        save.start()
        feed_out[span(b), :] = sum_b.final()
        down_ring.third()
        rows_out = [pltpu.make_async_copy(row, down_out, here.at[0]) for row in (raw.at[:, z], raw.at[x])]
        for core in (0, 1):
            pl.when(c == core)(rows_out[core].start)
        down_ring.close()
        sum_a.close()
        sum_b.close()
        close_a()
        close_b()
        save.wait()
        for core in (0, 1):
            pl.when(c == core)(rows_out[core].wait)

    low, wide = jnp.bfloat16, jnp.float32
    blocks = (SUBS, 8, rows)
    scratch = [
        pltpu.VMEM(blocks + (width,), low),
        pltpu.VMEM(blocks + (width,), low),
        pltpu.VMEM(blocks + (2 * WIDE,), low),
        pltpu.VMEM(blocks + (WIDE,), low),
        pltpu.VMEM(blocks + (width,), low),
        pltpu.VMEM((SUBS, 4, rows, width), low),
        pltpu.VMEM((SUBS, 2, half, width), low),
        pltpu.VMEM((SUBS, rows, width), low),
        pltpu.VMEM((SUBS, rows, width), low),
        pltpu.VMEM((width, 2 * WIDE), low),
        pltpu.VMEM((WIDE, width), low),
        pltpu.VMEM((4, 4, PIECE, width), low),
        pltpu.VMEM((2 * SLOT, width), wide),
        pltpu.VMEM((width, 2 * WIDE), low),
        pltpu.VMEM((WIDE, width), low),
        pltpu.VMEM((2, PIECE, width), low),
        pltpu.VMEM((2, PIECE, width), low),
        pltpu.VMEM((4, PIECE, width), low),
        pltpu.VMEM((4, PIECE, width), low),
    ]
    outs = [
        ((tokens, width), low),
        ((tokens, width), wide),
        ((1, width), wide),
        ((1, width), wide),
        ((width, 2 * WIDE), low),
        ((4, PIECE, width), low),
    ]
    return call(
        kernel, "feed_forward", number, outs, [feed, feeds_a, full_both, down16, hidden, cotangent, gains], scratch,
        32 * SUBS - 8 + 4, in_specs=[ANY] * 4 + [VMEM] * 3, out_specs=[VMEM] * 4 + [ANY] * 2, local=4,
    )


class Either:
    def __init__(self, core, sems, make):
        self.core, start, most = core, sems.used, 0
        self.variants = []
        for order in (0, 1):
            sems.used = start
            self.variants.append(make(order))
            most = max(most, sems.used)
        sems.used = most

    def __getattr__(self, name):
        def run():
            for order in (0, 1):
                pl.when(self.core == order)(getattr(self.variants[order], name))

        return run


def split_lanes(ref, h):
    halves = lane_halves(ref.shape[-1])
    return None if halves[h] is None else ref.at[:, pl.ds(*halves[h])]


def whole_ref(ref):
    return ref


def ring_row(own, out, cut, sems, kind=RingGather):
    x, y, z, c = place()

    def make(order):
        slot = (lambda k: cut(out.at[x, k])) if order == 0 else (lambda k: cut(out.at[k, z]))
        peer = (lambda k: device(x, y, k, c)) if order == 0 else (lambda k: device(k, y, z, c))
        return kind(own, slot, lambda k, h: split_lanes(slot(k), h), (z, x)[order], peer, sems)

    return Either(c, sems, make)


def ring_rest(out, cut, sems, lean=False, kind=RingGather):
    x, y, z, c = place()

    def make(order):
        if order == 0:
            slot, half, me = lambda k: cut(out.at[k]), lambda k, h: cut(out.at[k, pl.ds(2 * h, 2)]), x
        else:
            slot, half, me = lambda k: cut(out.at[:, k]), lambda k, h: cut(out.at[pl.ds(2 * h, 2), k]), z
            if lean:
                half = lambda k, h: slot(k) if h else None
        peer = (lambda k: device(k, y, z, c)) if order == 0 else (lambda k: device(x, y, k, c))
        return kind(slot(me), slot, half, me, peer, sems)

    return Either(c, sems, make)


class Crossing:
    def __init__(self, out, cut, other_cut, sems):
        x, y, z, c = place()
        self.pushes = []
        for d in range(4):

            def make(order, d=d):
                quarters = out.at[(x + d) % 4], out.at[:, (z + d) % 4]
                piece, lands = cut(quarters[order]), other_cut(quarters[1 - order])
                return Push(piece, piece, sems, device(x, y, z, 1 - c), lands)

            self.pushes.append(Either(c, sems, make))

    def start(self, d):
        self.pushes[d].start()

    def close(self):
        for push in self.pushes:
            push.arrived()
            push.sent()


def turn(values, cosine, sine):
    middle = values.shape[-1] // 2
    leading, trailing = values[:, :middle], values[:, middle:]
    return jnp.concatenate([leading * cosine - trailing * sine, trailing * cosine + leading * sine], axis=1)


def unit_rows(values):
    scale = lax.rsqrt(jnp.mean(values * values, axis=-1, keepdims=True) + EPSILON)
    return values * scale, scale


def allowed_keys(offset, beginning, rows, span):
    query = offset + lax.broadcasted_iota(jnp.int32, (rows, span), 0)
    key = offset + rows - span + lax.broadcasted_iota(jnp.int32, (rows, span), 1)
    return (key <= query) & (key > query - WINDOW) & (key >= beginning)


def gain_picks(each, width):
    lane = lax.broadcasted_iota(jnp.int32, (16, width), 1)
    owner = (lane * 7282) >> 16 if each == 9 else lane >> 1
    pick = lax.broadcasted_iota(jnp.int32, (16, width), 0) == lane - owner * each
    lane = lax.broadcasted_iota(jnp.int32, (128, width), 1)
    owner = (lane * 7282) >> 16 if each == 9 else lane >> 1
    owns = lax.broadcasted_iota(jnp.int32, (128, width), 0) == owner
    return pick.astype(jnp.float32).astype(jnp.bfloat16), owns.astype(jnp.float32)


def gain_row(table, first, pick, owns):
    spread = dot(table[:, first : first + 16], pick, 1, 0)
    return jnp.sum(spread * owns, axis=0, keepdims=True)


def lanes_of(start, size):
    return lambda ref: ref.at[(slice(None),) * (len(ref.shape) - 1) + (pl.ds(start, size),)]


def attend(number, stream, doc_starts, own_query, own_key, own_value, own_output, own_gate, own_up, own_down, norms):
    tokens = stream.shape[0]
    span = tokens + WINDOW

    low, wide = jnp.bfloat16, jnp.float32
    keep = dict(
        normed=((tokens, D), low),
        query=((HEADS * tokens, HEAD_DIM), wide),
        key=((tokens, HEAD_DIM), wide),
        turned=((HEADS * tokens, HEAD_DIM), low),
        kv=((span, 2 * HEAD_DIM), low),
        probs=((HEADS * tokens, span), wide),
        mixed=((tokens, HEADS * HEAD_DIM), low),
        branch=((tokens, D), wide),
        hidden=((tokens, D), wide),
        feed=((tokens, D), low),
        gains=((8, D), wide),
        cosine=((tokens, HEAD_DIM // 2), wide),
        sine=((tokens, HEAD_DIM // 2), wide),
        qkv_weight=((D, 1536), low),
        output_weight=((HEADS * HEAD_DIM, D), low),
    )

    def kernel(
        stream_in, starts_in, query_in, key_in, value_in, output_in, gate_in, up_in, down_in, *refs
    ):
        norms_in, refs = refs[: len(norms)], list(refs[len(norms) :])

        def take(count):
            taken, refs[:] = refs[:count], refs[count:]
            return taken

        saved = SimpleNamespace(**dict(zip(keep, take(len(keep)))))
        both_out, down_out, feeds_out = take(3)
        v = SimpleNamespace(**dict(zip(keep, take(len(keep)))))
        (
            query_give, kv_give, query_box, kv_box, both_box, both_give, flat, merge, query_own, kv_own, both_own, query_all, kv_all, output_all, kv,
            owns9, owns2,
            send, recv, here,
        ) = refs
        saves = []

        def save(src, dst):
            saves.append(pltpu.make_async_copy(src, dst, here.at[5 + len(saves)]))
            saves[-1].start()

        x, y, z, c = place()
        q, s = lax.axis_index("seq"), lax.axis_index("shard")
        sems = Sems(send, recv)
        after, before = {"seq": (q + 1) % 16, "shard": s}, {"seq": (q + 15) % 16, "shard": s}
        for j in range(8):
            flat[pl.ds(j, 9, 8), :] = query_in[:, 128 * j : 128 * (j + 1)].astype(jnp.float32)
        query_give[...] = flat[:72, :].astype(jnp.bfloat16)
        for at, source in enumerate((key_in, value_in)):
            for j in range(2):
                flat[pl.ds(2 * at + j, 9, 4), :] = source[:, 128 * j : 128 * (j + 1)].astype(jnp.float32)
        flat[36:40, :] = jnp.zeros((4, 128), jnp.float32)
        for g, source in enumerate(norms_in):
            flat[36:37, 16 * g : 16 * g + source.shape[1]] = source[...].astype(jnp.float32)
        kv_give[...] = flat[:40, :].astype(jnp.bfloat16)
        greet(
            [device(x, y + dy, z, (c + dc) % 2) for dy, dc in SHARD_STEPS]
            + [device(x, y, z + d, c) for d in (1, 2, 3)]
            + [device(x + d, y, z, c) for d in (1, 2, 3)]
            + [after, before]
        )
        sent = []

        def spread(source, box, pieces=False):
            pushes = []
            for dy, dc in SHARD_STEPS:
                to, back = (y + dy) % 4 * 2 + (c + dc) % 2, (y + 4 - dy) % 4 * 2 + (c + 2 - dc) % 2
                src = source.at[to] if pieces else source
                push = Push(src, box.at[s], sems, device(x, y + dy, z, (c + dc) % 2), box.at[back])
                push.start()
                pushes.append(push)
            box[s] = source[s] if pieces else source[...]
            sent.extend(pushes)
            return pushes

        def collect(pushes, box, own):
            for push in pushes:
                push.arrived()
            tiles = own.shape[-1] // 128
            for d in range(8):
                flat[: box.shape[1], :] = box[d].astype(jnp.float32)
                for j in range(tiles):
                    merge[9 * d : 9 * d + 9, 128 * j : 128 * (j + 1)] = flat[pl.ds(j, 9, tiles), :]
                if box.shape[1] > 9 * tiles:
                    for start in (0, 256):
                        merge[72 + d : 73 + d, start : start + 128] = flat[9 * tiles : 9 * tiles + 1, :]
            own[...] = merge[: own.shape[0], : own.shape[-1]].astype(own.dtype)

        def halves(size):
            return [lanes_of(pl.multiple_of(core * size, 128), size) for core in (c, 1 - c)]

        my_query, their_query = halves(512)
        my_kv, their_kv = halves(256)
        mine = lambda ref: ref.at[(slice(None),) * (len(ref.shape) - 3) + (s,)]

        got_kv = spread(kv_give, kv_box)
        got_query = spread(query_give, query_box)
        down_ring = ring_row(down_in, down_out, whole_ref, sems)
        output_ring = ring_row(output_in, output_all, mine, sems, DirectGather)
        down_ring.first()
        output_ring.first()
        inputs = stream_in[...].astype(jnp.float32)
        unit = unit_rows(inputs)[0]
        starts = starts_in[...]
        positions = q * tokens + lax.broadcasted_iota(jnp.int32, (tokens, 1), 0)
        beginning = jnp.zeros((tokens, 1), jnp.int32)
        for j in range(8):
            start = starts[0:1, j : j + 1]
            beginning = jnp.maximum(beginning, jnp.where(start <= positions, start, 0))
        steps = lax.broadcasted_iota(jnp.int32, (1, HEAD_DIM // 2), 1).astype(jnp.float32)
        angles = (positions - beginning).astype(jnp.float32) * jnp.exp(steps * (-2.0 * math.log(10000.0) / HEAD_DIM))
        v.cosine[...] = jnp.cos(angles)
        v.sine[...] = jnp.sin(angles)
        pick9, owns9[...] = gain_picks(9, D)
        pick2, owns2[...] = gain_picks(2, HEAD_DIM)
        v.gains[...] = jnp.zeros_like(v.gains)
        merge[72:80, :] = jnp.zeros((8, merge.shape[1]), jnp.float32)

        own = lambda src, dst, at: pltpu.make_async_copy(src, dst, here.at[at])
        collect(got_kv, kv_box, kv_own)
        kv_ring = ring_row(my_kv(kv_own), kv_all, my_kv, sems, DirectGather)
        kv_ring.first()
        other = device(x, y, z, 1 - c)
        column = lambda k: output_all.at[:, :, k * 2 + c]
        output_y = RingGather(
            column(y), column, lambda k, h: output_all.at[pl.ds(2 * h, 2), :, k * 2 + c],
            y, lambda k: device(x, k, z, c), sems,
        )
        output_cross = [
            Push(column((y + d) % 4), column((y + d) % 4), sems, other, output_all.at[:, :, (y + d) % 4 * 2 + 1 - c])
            for d in range(4)
        ]
        own(output_in, output_all.at[x, z, s], 2).start()
        collect(got_query, query_box, query_own)
        query_ring = ring_row(my_query(query_own), query_all, my_query, sems)
        query_ring.first()
        output_ring.relay()
        output_ring.last()
        own(output_in, output_all.at[x, z, s], 2).wait()
        output_rest = ring_rest(output_all, mine, sems, kind=DirectGather)
        output_rest.first()
        merge[0:16, :] = jnp.zeros((16, merge.shape[1]), jnp.float32)
        for d in range(8):
            for half, source in enumerate((gate_in, up_in)):
                for i in range(16):
                    to, start = WIDE * half + SLOT * i, 8 * PIECE * i + PIECE * d
                    merge[0:9, to : to + PIECE] = source[:, start : start + PIECE].astype(jnp.float32)
            for j in range(14):
                flat[pl.ds(j, 9, 14), :] = merge[0:9, 128 * j : 128 * (j + 1)]
            both_give[d] = flat[:126, :].astype(jnp.bfloat16)
        got_both = spread(both_give, both_box, True)
        copies = [
            own(my_kv(kv_own), my_kv(kv_all.at[x, z]), 0),
            own(down_in, down_out.at[x, z], 1),
            own(my_query(query_own), my_query(query_all.at[x, z]), 3),
        ]
        for copy in copies:
            copy.start()
        down_ring.relay()
        kv_ring.relay()
        query_ring.relay()
        for copy in copies:
            copy.wait()
        kv_ring.last()
        kv_rest = ring_rest(kv_all, my_kv, sems, kind=DirectGather)
        kv_cross = Crossing(kv_all, my_kv, their_kv, sems)
        kv_rest.first()
        kv_cross.start(0)
        query_ring.last()
        query_rest = ring_rest(query_all, my_query, sems)
        query_cross = Crossing(query_all, my_query, their_query, sems)
        query_rest.first()
        query_cross.start(0)
        output_rest.relay()
        output_rest.last()
        output_y.first()
        output_cross[0].start()
        down_ring.last()
        down_rest = ring_rest(down_out, whole_ref, sems, True)
        kv_rest.relay()
        kv_cross.start(3)
        kv_cross.start(1)
        collect(got_both, both_box, both_own)
        both_ring = ring_row(both_own, both_out, whole_ref, sems)
        both_ring.first()
        both_copy = own(both_own, both_out.at[x, z], 4)
        both_copy.start()
        kv_rest.last()
        kv_cross.start(2)
        query_rest.relay()
        query_cross.start(3)
        query_cross.start(1)
        down_rest.first()
        table = kv_all[:, :, 72:80, pl.ds(pl.multiple_of(c * 256, 128), 128)].reshape(128, 128)
        for g in range(4):
            v.gains[g : g + 1, :] = gain_row(table, 16 * g, pick9, owns9[...])
        for g in range(2):
            v.gains[4 + g : 5 + g, :HEAD_DIM] = gain_row(table, 64 + 16 * g, pick2, owns2[...])
        normed = (unit * v.gains[0:1, :]).astype(jnp.bfloat16)
        v.normed[...] = normed

        def assemble(blocks, lanes):
            @pl.loop(0, 8)
            def _(i):
                pair = [blocks[i // 2, i % 2 * 2 + k, :72].astype(jnp.float32) for k in range(2)]
                rows = pl.ds(pl.multiple_of(144 * i, 144), 144)
                v.qkv_weight[rows, lanes] = jnp.concatenate(pair, axis=0).astype(jnp.bfloat16)

        kv_cross.close()
        assemble(kv_all, slice(1024, 1536))

        piece = lambda at, i: kv.at[at, :, pl.ds(HEAD_DIM * i, HEAD_DIM)]
        near = [Push(piece(2, i), piece(1, i), sems, after) for i in range(2)]
        far = [Push(piece(1, i), piece(0, i), sems, after) for i in range(2)]
        key = dot(normed, v.qkv_weight[:, 1024:1280], 1, 0)
        key_turned = turn(unit_rows(key)[0] * v.gains[5:6, :HEAD_DIM], v.cosine[...], v.sine[...])
        kv[2, :, :HEAD_DIM] = key_turned.astype(jnp.bfloat16)
        near[0].start()
        v.key[...] = key
        kv[2, :, HEAD_DIM:] = dot(normed, v.qkv_weight[:, 1280:], 1, 0).astype(jnp.bfloat16)
        near[1].start()
        output_y.relay()
        output_cross[1].start()
        output_cross[3].start()
        query_rest.last()
        query_cross.start(2)
        both_ring.relay()
        for src, dst in ((v.gains, saved.gains), (v.cosine, saved.cosine), (v.sine, saved.sine)):
            save(src, dst)
        query_cross.close()
        assemble(query_all, slice(0, 1024))
        save(v.qkv_weight, saved.qkv_weight)
        both_ring.last()
        both_copy.wait()
        both_rest = ring_rest(both_out, whole_ref, sems, True)
        both_rest.first()
        down_rest.relay()
        for h in range(HEADS):
            lanes = slice(h * HEAD_DIM, (h + 1) * HEAD_DIM)
            span_h = slice(h * tokens, (h + 1) * tokens)
            query = dot(normed, v.qkv_weight[:, lanes], 1, 0)
            v.query[span_h, :] = query
            turned = turn(unit_rows(query)[0] * v.gains[4:5, :HEAD_DIM], v.cosine[...], v.sine[...])
            v.turned[span_h, :] = turned.astype(jnp.bfloat16)
        save(v.query, saved.query)
        save(v.turned, saved.turned)
        save(v.normed, saved.normed)
        save(v.key, saved.key)
        for i in range(2):
            near[i].arrived()
            far[i].start()
        both_rest.relay()
        output_y.last()
        output_cross[2].start()
        down_rest.last()
        for push in output_cross:
            push.arrived()

        @pl.loop(0, 16)
        def _(i):
            for j in range(4):
                pair = [output_all[i // 4, i % 4, 2 * j + k].astype(jnp.float32) for k in range(2)]
                rows = pl.ds(pl.multiple_of(64 * i + 16 * j, 16), 16)
                v.output_weight[rows, :] = jnp.concatenate(pair, axis=0).astype(jnp.bfloat16)

        save(v.output_weight, saved.output_weight)
        for push in far:
            push.arrived()
        v.kv[...] = kv[...].reshape(span, 2 * HEAD_DIM)
        save(v.kv, saved.kv)
        allowed = allowed_keys(q * tokens, beginning, tokens, span)
        keys, values = v.kv[:, :HEAD_DIM], v.kv[:, HEAD_DIM:]
        rows = tokens // SUBS

        def attend_part(part):
            here_rows = slice(part * rows, (part + 1) * rows)
            for h in range(HEADS):
                span_h = slice(h * tokens + part * rows, h * tokens + (part + 1) * rows)
                scores = dot(v.turned[span_h, :], keys, 1, 1) * HEAD_DIM ** (-0.5)
                scores = jnp.where(allowed[here_rows], scores, NEGATIVE)
                exponent = jnp.exp(scores - jnp.max(scores, axis=-1, keepdims=True))
                probs = exponent / jnp.sum(exponent, axis=-1, keepdims=True)
                v.probs[span_h, :] = probs
                mixed = dot(probs.astype(jnp.bfloat16), values, 1, 0)
                v.mixed[here_rows, h * HEAD_DIM : (h + 1) * HEAD_DIM] = mixed.astype(jnp.bfloat16)
            branch = dot(v.mixed[here_rows, :], v.output_weight[...], 1, 0)
            v.branch[here_rows, :] = branch
            hidden = inputs[here_rows] + unit_rows(branch)[0] * v.gains[1:2, :]
            v.hidden[here_rows, :] = hidden
            v.feed[here_rows, :] = (unit_rows(hidden)[0] * v.gains[2:3, :]).astype(jnp.bfloat16)

        attend_part(0)
        first_rows = v.feed.at[pl.ds(0, rows)]
        block = lambda k: feeds_out.at[k * 2 + c]
        feed_y = RingGather(
            first_rows, block, lambda k, h: feeds_out.at[k * 2 + c, pl.ds(h * (rows // 2), rows // 2)],
            y, lambda k: device(x, k, z, c), sems,
        )
        feed_cross = [
            Push(
                first_rows if d == 0 else block((y + d) % 4), block((y + d) % 4), sems, other,
                feeds_out.at[(y + d) % 4 * 2 + 1 - c],
            )
            for d in range(4)
        ]
        feed_y.first()
        feed_cross[0].start()
        save(first_rows, feeds_out.at[s])
        attend_part(1)
        for src, dst in (
            (v.probs, saved.probs), (v.branch, saved.branch), (v.hidden, saved.hidden), (v.mixed, saved.mixed),
            (v.feed, saved.feed),
        ):
            save(src, dst)
        feed_y.relay()
        feed_cross[1].start()
        feed_cross[3].start()
        both_rest.last()
        feed_y.last()
        feed_cross[2].start()
        for push in feed_cross:
            push.arrived()
        rings = [query_ring, kv_ring, down_ring, output_ring, both_ring]
        rings += [query_rest, kv_rest, down_rest, output_rest, both_rest, output_y, feed_y]
        for ring in rings:
            ring.close()
        for push in sent + output_cross + feed_cross + near + far:
            push.sent()
        for copy in saves:
            copy.wait()

    outs = list(keep.values()) + [
        ((4, 4, 72, 2 * WIDE), low),
        ((4, 4, PIECE, D), low),
        ((8, tokens // SUBS, D), low),
    ]
    scratch = [pltpu.VMEM(shape, kind) for shape, kind in keep.values()] + [
        pltpu.VMEM((72, 128), low),
        pltpu.VMEM((40, 128), low),
        pltpu.VMEM((8, 72, 128), low),
        pltpu.VMEM((8, 40, 128), low),
        pltpu.VMEM((8, 126, 128), low),
        pltpu.VMEM((8, 126, 128), low),
        pltpu.VMEM((128, 128), wide),
        pltpu.VMEM((80, 2 * WIDE), wide),
        pltpu.VMEM((72, 1024), low),
        pltpu.VMEM((80, 512), low),
        pltpu.VMEM((72, 2 * WIDE), low),
        pltpu.VMEM((4, 4, 72, 1024), low),
        pltpu.VMEM((4, 4, 80, 512), low),
        pltpu.VMEM((4, 4, 8, 8, D), low),
        pltpu.VMEM((3, tokens, 2 * HEAD_DIM), low),
        pltpu.VMEM((128, D), wide),
        pltpu.VMEM((128, HEAD_DIM), wide),
    ]
    out = call(
        kernel, "attend", number, outs,
        [stream, doc_starts, own_query, own_key, own_value, own_output, own_gate, own_up, own_down, *norms],
        scratch, 3 * 7 + 11 * 4 + 2 * 4 + 4 + 4 + 4 + 4, in_specs=[VMEM] * (9 + len(norms)), local=5 + 16,
    )
    return SimpleNamespace(**dict(zip(keep, out))), out[len(keep) :]


def sum_row(total, boxes, sems, lean=False, kind=RingSum):
    x, y, z, c = place()

    def make(order):
        if order == 0:
            chunk, half = lambda k: total.at[:, k], lambda k, h: total.at[pl.ds(2 * h, 2), k]
            if lean:
                half = lambda k, h: None if h else chunk(k)
            me, peer = z, lambda k: device(x, y, k, c)
        else:
            chunk, half = lambda k: total.at[k], lambda k, h: total.at[k, pl.ds(2 * h, 2)]
            me, peer = x, lambda k: device(k, y, z, c)
        own_boxes = list(boxes)
        if order == 1 and lean:
            own_boxes[0] = boxes[0].at[pl.ds(0, 2)]
        return kind(chunk, half, own_boxes, me, peer, sems, add_into)

    return Either(c, sems, make)


def sum_rest(total, boxes, sems, kind=RingSum):
    x, y, z, c = place()

    def make(order):
        if len(total.shape) == 3:
            chunk = lambda k: total.at[k]
        else:
            chunk = (lambda k: total.at[k, z]) if order == 0 else (lambda k: total.at[x, k])
        half = lambda k, h: split_lanes(chunk(k), h)
        peer = (lambda k: device(k, y, z, c)) if order == 0 else (lambda k: device(x, y, k, c))
        return kind(chunk, half, boxes, (x, z)[order], peer, sems, add_into)

    return Either(c, sems, make)


def norm_grad(values, gain, grad):
    unit, scale = unit_rows(values)
    scaled = gain * grad
    return (
        scale * (scaled - unit * jnp.mean(unit * scaled, axis=-1, keepdims=True)),
        jnp.sum(grad * unit, axis=0, keepdims=True),
    )


def scatter_boxes(rows, width, kind, row_only=False, lean=False):
    lanes = lane_halves(width)
    rest = [pltpu.VMEM((rows, size), kind) for _, size in lanes] + [pltpu.VMEM((rows, width), kind)] * 2
    if row_only:
        return [pltpu.VMEM((4, rows, width), kind)] + rest
    return (
        [pltpu.VMEM((4, 4, rows, width), kind)]
        + [pltpu.VMEM((4 if lean else 2, rows, width), kind), pltpu.VMEM((2, rows, width), kind)]
        + [pltpu.VMEM((4, rows, width), kind)] * 2
        + rest
    )


BOTH, DOWN, OUTPUT, QUERY, KV = range(5)
SHARED = (OUTPUT, QUERY, KV)
GIVE, TAKE = 9, 10


def attend_back(number, arrays):
    tokens = arrays["hidden"].shape[0]
    span = tokens + WINDOW
    names = list(arrays)
    low, wide = jnp.bfloat16, jnp.float32
    results = dict(
        stream_grad=((tokens, D), low),
        both_rows=((8, 126, 128), low),
        query_grad=((9, 1024), wide),
        key_grad=((9, 256), wide),
        value_grad=((9, 256), wide),
        output_grad=((8, D), wide),
        down_grad=((PIECE, D), wide),
        sums=((8, D), wide),
    )
    sizes = {BOTH: (72, 2 * WIDE), DOWN: (PIECE, D), OUTPUT: (64, 640), QUERY: (72, 512), KV: (72, 256)}
    stores = []
    for name, (rows, width) in sizes.items():
        if name == KV:
            stores.append([pltpu.VMEM((4, 4, rows, width), low)] + [pltpu.VMEM((4, rows, width), low)] * 3)
            stores[-1] += [pltpu.VMEM((rows, width), low)] * 5
        else:
            stores.append(scatter_boxes(rows, width, low, name == DOWN, name == BOTH))
        if name in SHARED:
            stores[-1] += [pltpu.VMEM((4, 4, rows, width), low)] * 2
    room = SimpleNamespace(
        hidden_grad=pltpu.VMEM((tokens, D), wide),
        branch_low=pltpu.VMEM((tokens, D), low),
        mixed_grad=pltpu.VMEM((HEADS * tokens, HEAD_DIM), low),
        score_low=pltpu.VMEM((HEADS * tokens, span), low),
        probs_low=pltpu.VMEM((HEADS * tokens, span), low),
        kv_grad=pltpu.VMEM((span, 2 * HEAD_DIM), wide),
        halo_out=pltpu.VMEM((2, tokens, 2 * HEAD_DIM), low),
        halo_in=pltpu.VMEM((2, tokens, 2 * HEAD_DIM), low),
        qkv_low=pltpu.VMEM((tokens, 1536), low),
        term=pltpu.VMEM((D, 1024), wide),
        merge=pltpu.VMEM((72, 2 * WIDE), wide),
        flat=pltpu.VMEM((128, 128), wide),
        both_give=pltpu.VMEM((8, 126, 128), low),
        query_give=pltpu.VMEM((8, 36, 128), low),
        query_take=pltpu.VMEM((8, 36, 128), low),
        kv_give=pltpu.VMEM((8, 18, 128), low),
        kv_take=pltpu.VMEM((8, 18, 128), low),
        output_give=pltpu.VMEM((8, 8, 640), low),
        output_take=pltpu.VMEM((8, 8, 640), low),
        own_sums=pltpu.VMEM((3, 8, D), wide),
        shard_sums=pltpu.VMEM((8, 8, D), wide),
        z_sums=pltpu.VMEM((4, 8, D), wide),
        x_sums=pltpu.VMEM((4, 8, D), wide),
    )
    room = vars(room)
    held_names = names[:-2]

    def kernel(*refs):
        refs = list(refs)

        def take(count):
            taken, refs[:] = refs[:count], refs[count:]
            return taken

        given = dict(zip(names, take(len(names))))
        o = SimpleNamespace(**dict(zip(results, take(len(results)))))
        a = SimpleNamespace(**dict(zip(held_names, take(len(held_names)))))
        b = SimpleNamespace(**dict(zip(room, take(len(room)))))
        held = {n: take(len(store)) for n, store in zip(sizes, stores)}
        send, recv, here = refs
        x, y, z, c = place()
        q, s = lax.axis_index("seq"), lax.axis_index("shard")
        sems = Sems(send, recv)
        other = device(x, y, z, 1 - c)
        after, before = {"seq": (q + 1) % 16, "shard": s}, {"seq": (q + 15) % 16, "shard": s}
        rings = {}
        for n in sizes:
            if n == DOWN:
                rings[n] = None, sum_rest(held[n][0], held[n][1:5], sems)
            elif n == KV:
                one = sum_row(held[n][0], held[n][1:4], sems, kind=DirectSum)
                rings[n] = one, sum_rest(held[n][0], held[n][4:7], sems, kind=DirectSum)
            else:
                one = sum_row(held[n][0], held[n][1:5], sems, n == BOTH)
                rings[n] = one, sum_rest(held[n][0], held[n][5:9], sems)
        cross = {n: Push(held[n][GIVE], held[n][TAKE], sems, other) for n in SHARED}
        loads = [
            pltpu.make_async_copy(given[names[-2]], held[BOTH][0], here.at[0]),
            pltpu.make_async_copy(given[names[-1]], held[DOWN][0], here.at[1]),
        ]
        for at, name in enumerate(held_names):
            loads.append(pltpu.make_async_copy(given[name], getattr(a, name), here.at[2 + at]))
        for load in loads:
            load.start()
        greet(
            [device(x, y + dy, z, (c + dc) % 2) for dy, dc in SHARD_STEPS]
            + [device(x, y, z + d, c) for d in (1, 2, 3)]
            + [device(x + d, y, z, c) for d in (1, 2, 3)]
            + [after, before]
        )
        loads[0].wait()
        rings[BOTH][0].first()
        loads[1].wait()
        rings[DOWN][1].first()
        for load in loads[2:]:
            load.wait()
        gains = a.gains
        cosine, sine = a.cosine, a.sine
        own = b.own_sums.at[0]
        own[...] = jnp.zeros(own.shape, wide)
        pending = []

        upstream = a.cotangent[...].astype(wide)
        extra, own[2:3, :] = norm_grad(a.hidden[...], gains[2:3, :], a.feed_grad[...])
        hidden_grad = upstream + extra
        b.hidden_grad[...] = hidden_grad
        branch_grad, own[1:2, :] = norm_grad(a.branch[...], gains[1:2, :], hidden_grad)
        b.branch_low[...] = branch_grad.astype(low)
        own[3:4, :] = a.post_grad[...]
        for at, squares in enumerate((
            jnp.sum(jnp.square(a.stream[...].astype(wide)), axis=0, keepdims=True),
            jnp.sum(jnp.square(a.hidden[...]), axis=0, keepdims=True),
            a.result_squares[...],
        )):
            folded = functools.reduce(jnp.add, [squares[:, 128 * j : 128 * (j + 1)] for j in range(D // 128)])
            own[4:5, 512 + 128 * at : 640 + 128 * at] = folded
        for h in range(HEADS):
            rows, lanes = slice(h * tokens, (h + 1) * tokens), slice(h * HEAD_DIM, (h + 1) * HEAD_DIM)
            b.mixed_grad[rows, :] = dot(b.branch_low[...], a.output_weight[lanes, :], 1, 1).astype(low)
        keys, values = a.kv[:, :HEAD_DIM], a.kv[:, HEAD_DIM:]
        for h in range(HEADS):
            rows = slice(h * tokens, (h + 1) * tokens)
            probs = a.probs[rows, :]
            prob_grad = dot(b.mixed_grad[rows, :], values, 1, 1)
            inner = jnp.sum(probs * prob_grad, axis=-1, keepdims=True)
            b.score_low[rows, :] = (probs * (prob_grad - inner) * HEAD_DIM ** (-0.5)).astype(low)
            b.probs_low[rows, :] = probs.astype(low)

        lanes_of_kv = [slice(0, HEAD_DIM), slice(HEAD_DIM, 2 * HEAD_DIM)]
        piece = lambda ref, at, i: ref.at[at, :, pl.ds(HEAD_DIM * i, HEAD_DIM)]
        halo_far, halo_near = (
            [Push(piece(b.halo_out, at, i), piece(b.halo_in, at, i), sems, before) for i in range(2)] for at in range(2)
        )
        for i, (left, right) in enumerate(((b.score_low, a.turned), (b.probs_low, b.mixed_grad))):
            b.kv_grad[:, lanes_of_kv[i]] = dot(left[...], right[...], 0, 0)
            b.halo_out[0, :, lanes_of_kv[i]] = b.kv_grad[:tokens, lanes_of_kv[i]].astype(low)
            halo_far[i].start()

        gain_grad = jnp.zeros((1, HEAD_DIM), wide)
        for h in range(HEADS):
            rows, lanes = slice(h * tokens, (h + 1) * tokens), slice(h * HEAD_DIM, (h + 1) * HEAD_DIM)
            turned_grad = dot(b.score_low[rows, :], keys, 1, 0)
            back = turn(turned_grad, cosine[...], -sine[...])
            grad, extra = norm_grad(a.query[rows, :], gains[4:5, :HEAD_DIM], back)
            gain_grad += extra
            b.qkv_low[:, lanes] = grad.astype(low)
        own[4:5, :HEAD_DIM] = gain_grad

        def term(start, width, give, take):
            out = b.term

            @pl.loop(0, D // 128)
            def _(i):
                lanes = pl.ds(pl.multiple_of(i * 128, 128), 128)
                out[lanes, : 2 * width] = dot(a.normed[:, lanes], b.qkv_low[:, start : start + 2 * width], 0, 0)

            @pl.loop(0, 16)
            def _(i):
                rows = pl.ds(pl.multiple_of(72 * i, 8), 72)
                for ref, core in ((take, c), (give, 1 - c)):
                    lanes = pl.ds(pl.multiple_of(core * width, 128), width)
                    ref[i // 4, i % 4] = out[rows, lanes].astype(low)

        term(0, 512, held[QUERY][GIVE], held[QUERY][0])
        cross[QUERY].start()
        rings[BOTH][0].second()
        rings[DOWN][1].second()

        @pl.loop(0, 8)
        def _(i):
            lanes = pl.ds(pl.multiple_of(i * 128, 128), 128)
            part = dot(a.mixed[:, lanes], b.branch_low[...], 0, 0).astype(low)
            for k in range(2):
                block = (2 * i + k) // 4, (2 * i + k) % 4
                for core in range(2):
                    lanes_out = slice(512 * core, 512 * core + 640)
                    value = part[64 * k : 64 * (k + 1), lanes_out]

                    @pl.when(c == core)
                    def _():
                        held[OUTPUT][0][block] = value

                    @pl.when(c != core)
                    def _():
                        held[OUTPUT][GIVE][block] = value

        cross[OUTPUT].start()
        for i, lanes in enumerate(lanes_of_kv):
            halo_far[i].arrived()
            summed = b.kv_grad[tokens : 2 * tokens, lanes] + b.halo_in[0, :, lanes].astype(wide)
            b.halo_out[1, :, lanes] = summed.astype(low)
            halo_near[i].start()
        for n in (QUERY, OUTPUT):
            cross[n].arrived()
            add_into(held[n][0], held[n][TAKE])
            rings[n][0].first()
        halo_near[0].arrived()
        key_back = b.kv_grad[2 * tokens :, :HEAD_DIM] + b.halo_in[1, :, :HEAD_DIM].astype(wide)
        back = turn(key_back, cosine[...], -sine[...])
        grad, own[4:5, HEAD_DIM : 2 * HEAD_DIM] = norm_grad(a.key[...], gains[5:6, :HEAD_DIM], back)
        b.qkv_low[:, 1024:1280] = grad.astype(low)
        halo_near[1].arrived()
        value_back = b.kv_grad[2 * tokens :, HEAD_DIM:] + b.halo_in[1, :, HEAD_DIM:].astype(wide)
        b.qkv_low[:, 1280:] = value_back.astype(low)
        term(1024, 256, held[KV][GIVE], held[KV][0])
        cross[KV].start()
        for n in (QUERY, OUTPUT):
            rings[n][0].second()
        cross[KV].arrived()
        add_into(held[KV][0], held[KV][TAKE])
        rings[KV][0].first()
        normed_grad = dot(b.qkv_low[...], a.qkv_weight[...], 1, 1)
        extra, own[0:1, :] = norm_grad(a.stream[...].astype(wide), gains[0:1, :], normed_grad)
        o.stream_grad[...] = (b.hidden_grad[...] + extra).astype(low)

        def all_sum(stage, box, me, steps, target):
            source = b.own_sums.at[stage]
            pushes = []
            for to, back in steps:
                push = Push(source, box.at[me], sems, target(to), box.at[back])
                push.start()
                pushes.append(push)
            pending.extend(pushes)
            box[me] = source[...]

            def finish():
                for push in pushes:
                    push.arrived()
                return functools.reduce(jnp.add, [box[k] for k in range(box.shape[0])])

            return finish

        steps = []
        for dy, dc in SHARD_STEPS:
            there = (y + dy) % 4, (c + dc) % 2
            steps.append((there, (y + 4 - dy) % 4 * 2 + (c + 2 - dc) % 2))
        finish = all_sum(0, b.shard_sums, s, steps, lambda t: device(x, t[0], z, t[1]))
        rings[BOTH][0].third()
        rings[BOTH][1].first()
        rings[KV][0].second()
        for n in (QUERY, OUTPUT):
            rings[n][0].third()
            rings[n][1].first()
        rings[BOTH][1].second()
        rings[DOWN][1].third()
        b.own_sums[1] = finish()
        turns = lambda at: [((at + d) % 4, (at + 4 - d) % 4) for d in (1, 2, 3)]
        finish = all_sum(1, b.z_sums, z, turns(z), lambda t: device(x, y, t, c))
        rings[KV][0].third()
        rings[KV][1].first()
        for n in (QUERY, OUTPUT):
            rings[n][1].second()

        def spread(source, box):
            pushes = []
            for dy, dc in SHARD_STEPS:
                to, back = (y + dy) % 4 * 2 + (c + dc) % 2, (y + 4 - dy) % 4 * 2 + (c + 2 - dc) % 2
                push = Push(source.at[to], box.at[s], sems, device(x, y + dy, z, (c + dc) % 2), box.at[back])
                push.start()
                pushes.append(push)
            box[s] = source[s]
            pending.extend(pushes)
            return pushes

        def flatten(block, give):
            width = block.shape[-1]
            tiles = width // 128
            merge, flat = b.merge, b.flat
            merge[:, :width] = block[...].astype(wide)
            for d in range(8):
                for j in range(tiles):
                    flat[pl.ds(j, 9, tiles), :] = merge[9 * d : 9 * d + 9, 128 * j : 128 * (j + 1)]
                give[d] = flat[: 9 * tiles, :].astype(low)

        def unflatten(value, tiles, write):
            b.flat[: 9 * tiles, :] = value
            for j in range(tiles):
                write(j, b.flat[pl.ds(j, 9, tiles), :])

        rings[KV][1].second()
        rings[BOTH][1].third()
        flatten(held[BOTH][0].at[x, z], b.both_give)
        got_both = spread(b.both_give, o.both_rows)
        for n in (QUERY, OUTPUT):
            rings[n][1].third()
        b.own_sums[2] = finish()
        finish = all_sum(2, b.x_sums, x, turns(x), lambda t: device(t, y, z, c))
        flatten(held[QUERY][0].at[x, z], b.query_give)
        got_query = spread(b.query_give, b.query_take)
        for d in range(8):
            b.output_give[d] = held[OUTPUT][0][x, z, 8 * d : 8 * d + 8, :]
        got_output = spread(b.output_give, b.output_take)
        rings[KV][1].third()
        flatten(held[KV][0].at[x, z], b.kv_give)
        got_kv = spread(b.kv_give, b.kv_take)
        o.down_grad[...] = held[DOWN][0][x + c * (z + 4 - x) - 4 * c].astype(wide)
        o.sums[...] = finish()

        def over_y(box, core):
            return functools.reduce(jnp.add, [box[2 * k + core].astype(wide) for k in range(4)])

        for push in got_query:
            push.arrived()
        for core in range(2):
            def write(j, value, core=core):
                o.query_grad[:, 512 * core + 128 * j : 512 * core + 128 * (j + 1)] = value

            unflatten(over_y(b.query_take, core), 4, write)
        for push in got_output:
            push.arrived()
        o.output_grad[:, :512] = over_y(b.output_take, 0)[:, :512]
        o.output_grad[:, 512:] = over_y(b.output_take, 1)
        for push in got_kv:
            push.arrived()
        for core, out in enumerate((o.key_grad, o.value_grad)):
            def write(j, value, out=out):
                out[:, 128 * j : 128 * (j + 1)] = value

            unflatten(over_y(b.kv_take, core), 2, write)
        for push in got_both:
            push.arrived()
        for pair in rings.values():
            for ring in pair:
                if ring is not None:
                    ring.close()
        for push in list(cross.values()) + pending + halo_far + halo_near:
            push.sent()

    ins = list(arrays.values())
    out = call(
        kernel, "attend_back", number, list(results.values()), ins, [pltpu.VMEM(arrays[n].shape, arrays[n].dtype) for n in held_names] + list(room.values()) + sum(stores, []), 4 * 8 + 4 + 3 + 4 + 13 + 28,
        out_specs=[VMEM] * len(results), local=len(ins),
    )
    return dict(zip(results, out))


def finish(both_rows, sums, *arrays):
    def kernel(rows, sums, *refs):
        sources, refs = refs[: len(arrays)], refs[len(arrays) :]
        gate, up, *small = refs[:9]
        copies, (merge, flat) = refs[9:-2], refs[-2:]
        own = lax.axis_index("seq") * 8 + lax.axis_index("shard")
        for g in range(4):
            small[g][...] = pltpu.roll(sums[...], D - 9 * own, 1)[g : g + 1, :9]
        for g in range(2):
            start = HEAD_DIM * g + 2 * own
            small[4 + g][...] = pltpu.roll(sums[...], D - start, 1)[4:5, :2]
        for at in range(3):
            total = jnp.sum(sums[4:5, 512 + 128 * at : 640 + 128 * at], axis=1, keepdims=True)
            small[6][:, at : at + 1] = jnp.sqrt(total / (32768 * D))
        for source, copy in zip(sources, copies):
            copy[...] = source[...]
        for d in range(8):
            flat[:126, :] = rows[d].astype(jnp.float32)
            for j in range(14):
                merge[0:9, 128 * j : 128 * (j + 1)] = flat[pl.ds(j, 9, 14), :]
            for half, out in enumerate((gate, up)):
                for i in range(16):
                    start, to = WIDE * half + SLOT * i, 8 * PIECE * i + PIECE * d
                    out[:, to : to + PIECE] = merge[0:9, start : start + PIECE]

    return pl.pallas_call(
        kernel,
        name="finish",
        out_shape=[jax.ShapeDtypeStruct((9, FF), jnp.float32)] * 2
        + [jax.ShapeDtypeStruct((1, n), jnp.float32) for n in (9, 9, 9, 9, 2, 2, 3)]
        + [jax.ShapeDtypeStruct(a.shape, a.dtype) for a in arrays],
        in_specs=[VMEM] * (2 + len(arrays)),
        out_specs=[VMEM] * (9 + len(arrays)),
        scratch_shapes=[pltpu.VMEM((16, 2 * WIDE), jnp.float32), pltpu.VMEM((128, 128), jnp.float32)],
        compiler_params=pltpu.CompilerParams(vmem_limit_bytes=60 * MIB),
    )(both_rows, sums, *arrays)


def local(
    stream, doc_starts, cotangent, attention_norm, query_weight, key_weight, value_weight, query_norm, key_norm,
    output_weight, attention_post_norm, mlp_norm, gate_weight, up_weight, down_weight, mlp_post_norm,
):
    norms = (attention_norm, attention_post_norm, mlp_norm, mlp_post_norm, query_norm, key_norm)
    ahead, (both16, down16, feeds_a) = attend(
        0, stream[0], doc_starts, query_weight, key_weight, value_weight, output_weight, gate_weight, up_weight,
        down_weight, [norm[None] for norm in norms],
    )

    block_output, feed_grad, gain_mlp_post_grad, result_squares, both_term, down_row = feed_forward(
        1, ahead.feed, feeds_a, both16.reshape(D, 2 * WIDE), down16, ahead.hidden, cotangent[0], ahead.gains
    )

    named = vars(ahead)
    del named["feed"]
    back = SimpleNamespace(**attend_back(
        2,
        dict(
            **named, feed_grad=feed_grad, cotangent=cotangent[0], stream=stream[0],
            post_grad=gain_mlp_post_grad, result_squares=result_squares,
            both_term=both_term.reshape(4, 4, 72, 2 * WIDE),
            down_row=down_row,
        ),
    ))

    gate_grad, up_grad, *rest = finish(
        back.both_rows, back.sums, block_output, back.stream_grad, back.query_grad, back.key_grad, back.value_grad,
        back.output_grad, back.down_grad,
    )
    small, (block_output, stream_grad, query_grad, key_grad, value_grad, output_grad, down_grad) = rest[:7], rest[7:]
    input_gain, post_gain, mlp_gain, mlp_post_gain, query_gain, key_gain, stream_rms = [value[0] for value in small]
    return (
        block_output[None],
        stream_grad[None],
        input_gain,
        query_grad,
        key_grad,
        value_grad,
        query_gain,
        key_gain,
        output_grad,
        post_gain,
        mlp_gain,
        gate_grad,
        up_grad,
        down_grad,
        mlp_post_gain,
        stream_rms,
    )


def solution(mesh):
    rows = P(("seq", "shard"))
    tokens = P("shard", "seq", None)
    table = P(("seq", "shard"), None)
    return jax.shard_map(
        local,
        mesh=mesh,
        in_specs=(
            tokens, P("shard", None), tokens, rows, table, table, table, rows, rows, table, rows, rows, table, table,
            table, rows,
        ),
        out_specs=(
            tokens, tokens, rows, table, table, table, rows, rows, table, rows, rows, table, table, table, rows, P(),
        ),
        check_vma=False,
    )
```
